32 devices in a mesh: gx: 8 (over y, x, core), gy: 4 (over z).
Axes of the slice: x: 2, y: 2, z: 4, core: 2. Of those that a mesh axis runs over, the one named last changes fastest.
Arguments:
- source: bfloat16 [64, 16, 32, 128], P(None, 'gx', 'gy'), may hold values from -6 to 6
- preact: bfloat16 [64, 16, 32, 128], P(None, 'gx', 'gy'), may hold values from -6 to 6
- cotangent: bfloat16 [64, 16, 32, 128], P(None, 'gx', 'gy'), may hold values from -6 to 6
- kernel: bfloat16 [27, 64, 64], replicated, may hold values from -0.15625 to 0.15625
Outputs:
- grad_source: bfloat16 [64, 16, 32, 128], P(None, 'gx', 'gy')
- grad_kernel: float32 [110592], P(('gx', 'gy'))
The draws below stay inside these ranges and needn't reach their ends.
All inputs are finite; a program needn't handle non-finite values.
Results may differ from the reference program's by a relative error of at most 0.007.
Values may be sent and summed in bfloat16 or wider, within the bound.
No kernel may reach another device: no remote copies, remote signals or barrier semaphores. Data moves between devices by JAX's collectives and lax.ppermute only.
A program may use at most 64 MiB of HBM per device.

```python
import jax
import jax.numpy as jnp
from jax import lax

C = 64
NZ = 128
NX = 16
NY = 32


def block_scale(stream_key, extent, split, least, largest):
    def one(axis_at, parts):
        steps = jax.random.uniform(jax.random.fold_in(jax.random.fold_in(stream_key, 6), axis_at), (parts,), jnp.float32, least / len(split), largest / len(split))
        return jnp.repeat(jnp.exp(steps), extent[axis_at] // parts).reshape((-1,) + (1,) * (len(extent) - axis_at - 1))

    loudness = one(*split[0])
    for cut in split[1:]:
        loudness = loudness * one(*cut)
    return loudness


def centred(own_key, dims, deviation, reach, shards=(), kind=jnp.bfloat16):
    result = deviation * jax.random.normal(own_key, dims, jnp.float32)
    if shards:
        result = result * block_scale(own_key, dims, shards, -0.22, 0.18)
    return jnp.clip(result, -reach, reach).astype(kind)


def setup_inputs(seed: int = 0) -> dict:
    key_list = jax.random.split(jax.random.key(seed), 5)
    source = centred(key_list[0], (C, NX, NY, NZ), 1.0, 6.0, ((1, 8), (2, 4)))
    preact = centred(key_list[1], (C, NX, NY, NZ), 1.0, 6.0, ((1, 8), (2, 4)))
    cotangent = centred(key_list[2], (C, NX, NY, NZ), 1.0, 6.0, ((1, 8), (2, 4)))
    kernel = centred(key_list[3], (27, C, C), (27 * C) ** -0.5, 0.15625)
    return dict(source=source, preact=preact, cotangent=cotangent, kernel=kernel)


def reference(source, preact, cotangent, kernel):
    channels = source.shape[0]
    slope_grad = jnp.where(preact > 0, cotangent, jnp.zeros_like(cotangent))
    source_f = source.astype(jnp.float32)
    slope_f = slope_grad.astype(jnp.float32)
    kernel_f = kernel.astype(jnp.float32)
    slope_flat = slope_f.reshape(channels, -1)
    grad_source = jnp.zeros(slope_flat.shape, jnp.float32)
    pieces = []
    for a in range(3):
        for b in range(3):
            for c in range(3):
                tap = 9 * a + 3 * b + c
                moved_src = jnp.roll(source_f, (1 - a, 1 - b, 1 - c), axis=(1, 2, 3)).reshape(channels, -1)
                pieces.append(lax.dot_general(slope_flat, moved_src, (((1,), (1,)), ((), ())), precision=lax.Precision.HIGHEST, preferred_element_type=jnp.float32))
                moved_slope = jnp.roll(slope_f, (a - 1, b - 1, c - 1), axis=(1, 2, 3)).reshape(channels, -1)
                grad_source = grad_source + jnp.dot(kernel_f[tap].T, moved_slope, precision=lax.Precision.HIGHEST, preferred_element_type=jnp.float32)
    total_cells = source.shape[1] * source.shape[2] * source.shape[3]
    grad_kernel = jnp.stack(pieces, axis=0).reshape(-1) / jnp.sqrt(jnp.float32(total_cells))
    return (grad_source.reshape(source.shape).astype(jnp.bfloat16), grad_kernel)
```

```python
import math

import jax
import jax.numpy as jnp
from jax import lax
from jax.sharding import PartitionSpec as P


def with_halo(cells, sides, width):
    for axis, dim in sides:
        count = lax.axis_size(axis)
        head = lax.slice_in_dim(cells, 0, width, axis=dim)
        tail = lax.slice_in_dim(cells, cells.shape[dim] - width, cells.shape[dim], axis=dim)
        cells = jnp.concatenate(
            [
                lax.ppermute(tail, axis, [(i, (i + 1) % count) for i in range(count)]),
                cells,
                lax.ppermute(head, axis, [((i + 1) % count, i) for i in range(count)]),
            ],
            axis=dim,
        )
    return cells


def on_device(source, preact, cotangent, kernel):
    channels, width_x, width_y, depth_cells = source.shape
    cell_count = width_x * width_y * depth_cells
    devices = lax.axis_size("gx") * lax.axis_size("gy")
    slope = jnp.where(preact > 0, cotangent, jnp.zeros_like(cotangent))
    wide = with_halo(slope, (("gx", 1), ("gy", 2)), 1)
    columns = jnp.stack(
        [
            wide[:, 2 - a : 2 - a + width_x, 2 - b : 2 - b + width_y, :]
            for a in range(3)
            for b in range(3)
        ],
        axis=0,
    ).reshape(9 * channels, cell_count)
    moved = jnp.stack([jnp.roll(source, 1 - c, axis=3) for c in range(3)], axis=0)
    moved = moved.reshape(3 * channels, cell_count)
    partial = lax.dot_general(
        columns, moved, (((1,), (1,)), ((), ())), preferred_element_type=jnp.float32
    )
    partial = partial.reshape(9, channels, 3, channels).transpose(0, 2, 1, 3)
    partial = partial.astype(jnp.bfloat16).reshape(devices, -1)
    shares = lax.all_to_all(partial, ("gx", "gy"), 0, 0, tiled=True)
    norm_scale = 1.0 / math.sqrt(cell_count * devices)
    grad_kernel = jnp.sum(shares.astype(jnp.float32), axis=0) * norm_scale

    weights = kernel.reshape(9, 3, channels, channels).transpose(1, 3, 0, 2)
    weights = weights.reshape(3 * channels, 9 * channels)
    spread = jnp.dot(weights, columns, preferred_element_type=jnp.float32)
    spread = spread.reshape((3,) + source.shape)
    grad_source = sum(jnp.roll(spread[c], c - 1, axis=3) for c in range(3))
    return (grad_source.astype(jnp.bfloat16), grad_kernel)


def solution(mesh):
    placed = (P(None, "gx", "gy", None), P(None, "gx", "gy", None), P(None, "gx", "gy", None), P())
    return jax.shard_map(
        on_device,
        mesh=mesh,
        in_specs=placed,
        out_specs=(P(None, "gx", "gy", None), P(("gx", "gy"))),
        check_vma=False,
    )
```

```python
import math

import jax
import jax.numpy as jnp
from jax import lax
from jax.experimental import pallas as pl
from jax.experimental.pallas import tpu as pltpu
from jax.sharding import PartitionSpec as P

NT = (((1,), (1,)), ((), ()))


def to_next(block, axis):
    count = lax.axis_size(axis)
    return lax.ppermute(block, axis, [(i, (i + 1) % count) for i in range(count)])


def to_previous(block, axis):
    count = lax.axis_size(axis)
    return lax.ppermute(block, axis, [((i + 1) % count, i) for i in range(count)])


def roll_lanes(block, step):
    return pltpu.roll(block.astype(jnp.float32), step % block.shape[-1], axis=1).astype(block.dtype)


def weight_kernel(slope, before, after, source, low, high, out, left, right, gram, ordered):
    width_x, width_y, channels, depth = slope.shape
    for y in range(width_y):
        lanes = slice(y * depth, (y + 1) * depth)
        left[0:channels, lanes] = before[0, y]
        for x in range(width_x):
            left[(x + 1) * channels : (x + 2) * channels, lanes] = slope[x, y]
        left[(width_x + 1) * channels :, lanes] = after[0, y]
    for x in range(width_x):
        for row in range(-1, width_y + 1):
            if row < 0:
                cells = low[x]
            elif row == width_y:
                cells = high[x]
            else:
                cells = source[x, row]
            for c in range(3):
                moved = cells if c == 1 else roll_lanes(cells, 1 - c)
                for b in range(3):
                    y = row + 1 - b
                    if 0 <= y < width_y:
                        first = (3 * b + c) * channels
                        right[x, first : first + channels, y * depth : (y + 1) * depth] = moved
    for x in range(width_x):
        part = lax.dot_general(
            left[x * channels : (x + 3) * channels, :], right[x], NT, preferred_element_type=jnp.float32
        )
        total = part if x == 0 else total + part
    for pair in range(5):
        lanes = total[:, 2 * pair * channels : min(2 * pair + 2, 9) * channels]
        gram[pair, :, : lanes.shape[1]] = lanes
    half = channels // 2
    first_half = lax.broadcasted_iota(jnp.int32, (half, 2 * channels), 1) < channels
    for a in range(3):
        top = (2 - a) * channels
        for pair in range(5):
            even = gram[pair, pl.ds(top, half, stride=2), :]
            odd = gram[pair, pl.ds(top + 1, half, stride=2), :]
            tap = 9 * a + 2 * pair
            ordered[tap * half : (tap + 1) * half, :] = jnp.where(first_half, even, pltpu.roll(odd, channels, axis=1))
            if pair < 4:
                tap += 1
                ordered[tap * half : (tap + 1) * half, :] = jnp.where(
                    first_half, pltpu.roll(even, channels, axis=1), odd
                )
    if len(out.shape) == 3:
        rows = out.shape[1]
        for part in range(out.shape[0]):
            out[part] = ordered[part * rows : (part + 1) * rows, :].astype(out.dtype)
    else:
        out[...] = ordered[...].astype(out.dtype)


def source_kernel(slope, before, after, low, high, weights, out, columns, spread):
    width_x, width_y, channels, depth = slope.shape
    for wide_x in range(width_x + 2):
        for row in range(-1, width_y + 1):
            if row < 0:
                cells = low[wide_x]
            elif row == width_y:
                cells = high[wide_x]
            elif wide_x == 0:
                cells = before[0, row]
            elif wide_x == width_x + 1:
                cells = after[0, row]
            else:
                cells = slope[wide_x - 1, row]
            for b in range(3):
                y = row + b - 1
                if 0 <= y < width_y:
                    first = (3 * wide_x + b) * channels
                    columns[first : first + channels, y * depth : (y + 1) * depth] = cells
    for x in range(width_x):
        spread[...] = jnp.dot(
            weights[...], columns[3 * x * channels : 3 * (x + 3) * channels, :], preferred_element_type=jnp.float32
        )
        for y in range(width_y):
            lanes = slice(y * depth, (y + 1) * depth)
            total = spread[channels : 2 * channels, lanes]
            total += pltpu.roll(spread[0:channels, lanes], depth - 1, axis=1)
            total += pltpu.roll(spread[2 * channels :, lanes], 1, axis=1)
            out[x, y] = total.astype(out.dtype)


def on_device(source, preact, cotangent, kernel):
    channels, width_x, width_y, depth = source.shape
    devices = lax.axis_size("gx") * lax.axis_size("gy")
    cell_count = width_x * width_y * depth
    lines = 27 * channels * channels // 128
    share = (devices, lines // devices, 128) if lines % devices == 0 else (lines, 128)

    src = source.transpose(1, 2, 0, 3)
    src_low = to_next(src[:, width_y - 1], "gy")
    src_high = to_previous(src[:, 0], "gy")
    slope = jnp.where(preact > 0, cotangent, jnp.zeros_like(cotangent)).transpose(1, 2, 0, 3)
    before = to_next(slope[width_x - 1 :], "gx")
    after = to_previous(slope[:1], "gx")

    vmem = pl.BlockSpec(memory_space=pltpu.VMEM)
    partial = pl.pallas_call(
        weight_kernel,
        out_shape=jax.ShapeDtypeStruct(share, jnp.bfloat16),
        in_specs=[vmem] * 6,
        out_specs=vmem,
        scratch_shapes=[
            pltpu.VMEM(((width_x + 2) * channels, width_y * depth), jnp.bfloat16),
            pltpu.VMEM((width_x, 9 * channels, width_y * depth), jnp.bfloat16),
            pltpu.VMEM((5, 3 * channels, 2 * channels), jnp.float32),
            pltpu.VMEM((lines, 128), jnp.float32),
        ],
        compiler_params=pltpu.CompilerParams(vmem_limit_bytes=32 * 1024 * 1024),
        cost_estimate=pl.CostEstimate(
            flops=54 * channels * channels * cell_count, bytes_accessed=2 * 1024 * 1024, transcendentals=0
        ),
        name="weight_grad",
    )(slope, before, after, src, src_low, src_high)
    shares = lax.all_to_all(partial.reshape(devices, -1, *share[2:]), ("gx", "gy"), 0, 0, tiled=True)
    norm_scale = 1.0 / math.sqrt(cell_count * devices)
    grad_kernel = (jnp.sum(shares.astype(jnp.float32), axis=0) * norm_scale).reshape(-1)

    head = jnp.concatenate([before[:, 0], slope[:, 0], after[:, 0]], axis=0)
    tail = jnp.concatenate([before[:, -1], slope[:, -1], after[:, -1]], axis=0)
    low = to_next(tail, "gy")
    high = to_previous(head, "gy")
    weights = kernel.reshape(3, 3, 3, channels, channels)[::-1]
    weights = weights.transpose(2, 4, 0, 1, 3).reshape(3 * channels, 9 * channels)
    grad_source = pl.pallas_call(
        source_kernel,
        out_shape=jax.ShapeDtypeStruct(slope.shape, jnp.bfloat16),
        in_specs=[vmem] * 6,
        out_specs=vmem,
        scratch_shapes=[
            pltpu.VMEM((3 * (width_x + 2) * channels, width_y * depth), jnp.bfloat16),
            pltpu.VMEM((3 * channels, width_y * depth), jnp.float32),
        ],
        compiler_params=pltpu.CompilerParams(vmem_limit_bytes=32 * 1024 * 1024),
        cost_estimate=pl.CostEstimate(
            flops=54 * channels * channels * cell_count, bytes_accessed=2 * 1024 * 1024, transcendentals=0
        ),
        name="source_grad",
    )(slope, before, after, low, high, weights)
    return (grad_source.transpose(2, 0, 1, 3), grad_kernel)


def solution(mesh):
    placed = (P(None, "gx", "gy", None), P(None, "gx", "gy", None), P(None, "gx", "gy", None), P())
    return jax.shard_map(
        on_device,
        mesh=mesh,
        in_specs=placed,
        out_specs=(P(None, "gx", "gy", None), P(("gx", "gy"))),
        check_vma=False,
    )
```

```python
import math

import jax
import jax.numpy as jnp
from jax import lax
from jax.experimental import pallas as pl
from jax.experimental.pallas import tpu as pltpu
from jax.sharding import PartitionSpec as P

NT = (((1,), (1,)), ((), ()))
TN = (((0,), (0,)), ((), ()))
PARAMS = pltpu.CompilerParams(vmem_limit_bytes=32 * 1024 * 1024)


def neighbours(first, last, axis):
    count = lax.axis_size(axis)
    even = lax.axis_index(axis) & 1 == 0
    near = [(i, i ^ 1) for i in range(count)]
    far = [(i, (i - 1) % count if i % 2 == 0 else (i + 1) % count) for i in range(count)]
    got_near = lax.ppermute(jnp.where(even, last, first), axis, near)
    got_far = lax.ppermute(jnp.where(even, first, last), axis, far)
    return got_near, got_far, even


def fill_columns(wide, near, far, even, columns):
    width_x, rows, channels, depth = wide.shape
    for wide_x in range(width_x + 2):
        for row in range(rows):
            if wide_x == 0:
                cells = jnp.where(even, far[row], near[row])
            elif wide_x == width_x + 1:
                cells = jnp.where(even, near[row], far[row])
            else:
                cells = wide[wide_x - 1, row]
            for b in range(3):
                y = row + b - 2
                if 0 <= y < rows - 2:
                    first = (3 * wide_x + b) * channels
                    columns[first : first + channels, y * depth : (y + 1) * depth] = cells


def weight_kernel(parity, wide, near, far, source, out, columns, moved, gram, ordered):
    width_x, width_y, channels, depth = source.shape
    fill_columns(wide, near, far, parity[0] == 0, columns)
    for x in range(width_x):
        for y in range(width_y):
            lanes = slice(y * depth, (y + 1) * depth)
            cells = source[x, y]
            narrow = cells.astype(jnp.float32)
            moved[x, 0:channels, lanes] = pltpu.roll(narrow, 1, axis=1).astype(cells.dtype)
            moved[x, channels : 2 * channels, lanes] = cells
            moved[x, 2 * channels :, lanes] = pltpu.roll(narrow, depth - 1, axis=1).astype(cells.dtype)
    total = None
    for x in range(width_x):
        part = lax.dot_general(
            columns[3 * x * channels : 3 * (x + 3) * channels, :], moved[x], NT, preferred_element_type=jnp.float32
        )
        total = part if total is None else total + part
    gram[0] = total[:, : 2 * channels]
    gram[1, :, :channels] = total[:, 2 * channels :]
    half = channels // 2
    first_half = lax.broadcasted_iota(jnp.int32, (half, 2 * channels), 1) < channels
    for a in range(3):
        for b in range(3):
            top = (3 * (2 - a) + b) * channels
            line = (9 * a + 3 * b) * half
            even = gram[0, pl.ds(top, half, stride=2), :]
            odd = gram[0, pl.ds(top + 1, half, stride=2), :]
            ordered[line : line + half, :] = jnp.where(first_half, even, pltpu.roll(odd, channels, axis=1))
            ordered[line + half : line + 2 * half, :] = jnp.where(first_half, pltpu.roll(even, channels, axis=1), odd)
            even = gram[1, pl.ds(top, half, stride=2), :]
            odd = gram[1, pl.ds(top + 1, half, stride=2), :]
            ordered[line + 2 * half : line + 3 * half, :] = jnp.where(
                first_half, even, pltpu.roll(odd, channels, axis=1)
            )
    if len(out.shape) == 3:
        rows = out.shape[1]
        for part in range(out.shape[0]):
            out[part] = ordered[part * rows : (part + 1) * rows, :].astype(out.dtype)
    else:
        out[...] = ordered[...].astype(out.dtype)


def source_kernel(parity, wide, near, far, kernel, out, columns, weights, spread):
    width_x, width_y, channels, depth = out.shape
    fill_columns(wide, near, far, parity[0] == 0, columns)
    for a in range(3):
        for b in range(3):
            for c in range(3):
                first = (3 * (2 - a) + b) * channels
                weights[c, first : first + channels, :] = kernel[9 * a + 3 * b + c]
    for x in range(width_x):
        cells = columns[3 * x * channels : 3 * (x + 3) * channels, :]
        for c in range(3):
            spread[c] = lax.dot_general(weights[c], cells, TN, preferred_element_type=jnp.float32)
        for y in range(width_y):
            lanes = slice(y * depth, (y + 1) * depth)
            total = spread[1, :, lanes]
            total += pltpu.roll(spread[0, :, lanes], depth - 1, axis=1)
            total += pltpu.roll(spread[2, :, lanes], 1, axis=1)
            out[x, y] = total.astype(out.dtype)


def on_device(source, preact, cotangent, kernel):
    channels, width_x, width_y, depth = source.shape
    devices = lax.axis_size("gx") * lax.axis_size("gy")
    cell_count = width_x * width_y * depth
    lines = 27 * channels * channels // 128
    share = (devices, lines // devices, 128) if lines % devices == 0 else (lines, 128)

    slope = jnp.where(preact > 0, cotangent, jnp.zeros_like(cotangent)).transpose(1, 2, 0, 3)
    near, far, even = neighbours(slope[:, :1], slope[:, -1:], "gy")
    wide = jnp.concatenate([jnp.where(even, far, near), slope, jnp.where(even, near, far)], axis=1)
    near, far, even = neighbours(wide[0], wide[-1], "gx")
    parity = (lax.axis_index("gx") & 1).reshape(1)

    cost = pl.CostEstimate(
        flops=54 * channels * channels * cell_count, bytes_accessed=2 * 1024 * 1024, transcendentals=0
    )
    vmem = pl.BlockSpec(memory_space=pltpu.VMEM)
    smem = pl.BlockSpec(memory_space=pltpu.SMEM)
    columns = pltpu.VMEM((3 * (width_x + 2) * channels, width_y * depth), jnp.bfloat16)
    partial = pl.pallas_call(
        weight_kernel,
        out_shape=jax.ShapeDtypeStruct(share, jnp.bfloat16),
        in_specs=[smem] + [vmem] * 4,
        out_specs=vmem,
        scratch_shapes=[
            columns,
            pltpu.VMEM((width_x, 3 * channels, width_y * depth), jnp.bfloat16),
            pltpu.VMEM((2, 9 * channels, 2 * channels), jnp.float32),
            pltpu.VMEM((lines, 128), jnp.float32),
        ],
        compiler_params=PARAMS,
        cost_estimate=cost,
        name="weight_grad",
    )(parity, wide, near, far, source.transpose(1, 2, 0, 3))
    shares = lax.all_to_all(partial.reshape(devices, -1, *share[2:]), ("gx", "gy"), 0, 0, tiled=True)
    norm_scale = 1.0 / math.sqrt(cell_count * devices)
    grad_kernel = (jnp.sum(shares.astype(jnp.float32), axis=0) * norm_scale).reshape(-1)

    grad_source = pl.pallas_call(
        source_kernel,
        out_shape=jax.ShapeDtypeStruct(slope.shape, jnp.bfloat16),
        in_specs=[smem] + [vmem] * 4,
        out_specs=vmem,
        scratch_shapes=[
            columns,
            pltpu.VMEM((3, 9 * channels, channels), jnp.bfloat16),
            pltpu.VMEM((3, channels, width_y * depth), jnp.float32),
        ],
        compiler_params=PARAMS,
        cost_estimate=cost,
        name="source_grad",
    )(parity, wide, near, far, kernel)
    return (grad_source.transpose(2, 0, 1, 3), grad_kernel)


def solution(mesh):
    placed = (P(None, "gx", "gy", None), P(None, "gx", "gy", None), P(None, "gx", "gy", None), P())
    return jax.shard_map(
        on_device,
        mesh=mesh,
        in_specs=placed,
        out_specs=(P(None, "gx", "gy", None), P(("gx", "gy"))),
        check_vma=False,
    )
```

```python
import math

import jax
import jax.numpy as jnp
from jax import lax
from jax.experimental import pallas as pl
from jax.experimental.pallas import tpu as pltpu
from jax.sharding import PartitionSpec as P

NT = (((1,), (1,)), ((), ()))
TN = (((0,), (0,)), ((), ()))
PARAMS = pltpu.CompilerParams(vmem_limit_bytes=32 * 1024 * 1024)


def to_next(block, axis):
    count = lax.axis_size(axis)
    return lax.ppermute(block, axis, [(i, (i + 1) % count) for i in range(count)])


def to_previous(block, axis):
    count = lax.axis_size(axis)
    return lax.ppermute(block, axis, [((i + 1) % count, i) for i in range(count)])


def swapped(first, last, axis):
    count = lax.axis_size(axis)
    even = lax.axis_index(axis) & 1 == 0
    near = [(i, i ^ 1) for i in range(count)]
    far = [(i, (i - 1) % count if i % 2 == 0 else (i + 1) % count) for i in range(count)]
    got_far = lax.ppermute(jnp.where(even, first, last), axis, far)
    got_near = lax.ppermute(jnp.where(even, last, first), axis, near)
    return got_near, got_far


def roll_lanes(block, step):
    return pltpu.roll(block.astype(jnp.float32), step % block.shape[-1], axis=1).astype(block.dtype)


def weight_kernel(parity, slope, before, after, source, near, far, out, left, right, gram, ordered):
    width_x, width_y, channels, depth = slope.shape
    even = parity[0] == 0
    for y in range(width_y):
        lanes = slice(y * depth, (y + 1) * depth)
        left[0:channels, lanes] = before[0, y]
        for x in range(width_x):
            left[(x + 1) * channels : (x + 2) * channels, lanes] = slope[x, y]
        left[(width_x + 1) * channels :, lanes] = after[0, y]
    for x in range(width_x):
        for row in range(-1, width_y + 1):
            if row < 0:
                cells = jnp.where(even, far[x], near[x])
            elif row == width_y:
                cells = jnp.where(even, near[x], far[x])
            else:
                cells = source[x, row]
            for c in range(3):
                moved = cells if c == 1 else roll_lanes(cells, 1 - c)
                for b in range(3):
                    y = row + 1 - b
                    if 0 <= y < width_y:
                        first = (3 * b + c) * channels
                        right[x, first : first + channels, y * depth : (y + 1) * depth] = moved
    total = None
    for x in range(width_x):
        part = lax.dot_general(
            left[x * channels : (x + 3) * channels, :], right[x], NT, preferred_element_type=jnp.float32
        )
        total = part if total is None else total + part
    for pair in range(5):
        lanes = total[:, 2 * pair * channels : min(2 * pair + 2, 9) * channels]
        gram[pair, :, : lanes.shape[1]] = lanes
    half = channels // 2
    first_half = lax.broadcasted_iota(jnp.int32, (half, 2 * channels), 1) < channels
    for a in range(3):
        top = (2 - a) * channels
        for pair in range(5):
            low = gram[pair, pl.ds(top, half, stride=2), :]
            high = gram[pair, pl.ds(top + 1, half, stride=2), :]
            tap = 9 * a + 2 * pair
            ordered[tap * half : (tap + 1) * half, :] = jnp.where(first_half, low, pltpu.roll(high, channels, axis=1))
            if pair < 4:
                tap += 1
                ordered[tap * half : (tap + 1) * half, :] = jnp.where(
                    first_half, pltpu.roll(low, channels, axis=1), high
                )
    if len(out.shape) == 4:
        rows = out.shape[2]
        for part in range(out.shape[0] * out.shape[1]):
            out[part // out.shape[1], part % out.shape[1]] = ordered[part * rows : (part + 1) * rows, :].astype(
                out.dtype
            )
    else:
        out[...] = ordered[...].astype(out.dtype)


def source_kernel(parity, slope, before, after, near, far, kernel, out, columns, weights, spread):
    width_x, width_y, channels, depth = slope.shape
    even = parity[0] == 0
    for wide_x in range(width_x + 2):
        for row in range(-1, width_y + 1):
            if row < 0:
                cells = jnp.where(even, far[wide_x], near[wide_x])
            elif row == width_y:
                cells = jnp.where(even, near[wide_x], far[wide_x])
            elif wide_x == 0:
                cells = before[0, row]
            elif wide_x == width_x + 1:
                cells = after[0, row]
            else:
                cells = slope[wide_x - 1, row]
            for b in range(3):
                y = row + b - 1
                if 0 <= y < width_y:
                    first = (3 * wide_x + b) * channels
                    columns[first : first + channels, y * depth : (y + 1) * depth] = cells
    for a in range(3):
        for b in range(3):
            for c in range(3):
                first = (3 * (2 - a) + b) * channels
                weights[c, first : first + channels, :] = kernel[9 * a + 3 * b + c]
    for x in range(width_x):
        cells = columns[3 * x * channels : 3 * (x + 3) * channels, :]
        for c in range(3):
            spread[c] = lax.dot_general(weights[c], cells, TN, preferred_element_type=jnp.float32)
        for y in range(width_y):
            lanes = slice(y * depth, (y + 1) * depth)
            total = spread[1, :, lanes]
            total += pltpu.roll(spread[0, :, lanes], depth - 1, axis=1)
            total += pltpu.roll(spread[2, :, lanes], 1, axis=1)
            out[x, y] = total.astype(out.dtype)


def on_device(source, preact, cotangent, kernel):
    channels, width_x, width_y, depth = source.shape
    count_x, count_y = lax.axis_size("gx"), lax.axis_size("gy")
    devices = count_x * count_y
    cell_count = width_x * width_y * depth
    lines = 27 * channels * channels // 128
    share = (count_x, count_y, lines // devices, 128) if lines % devices == 0 else (lines, 128)
    parity = (lax.axis_index("gy") & 1).reshape(1)

    slope = jnp.where(preact > 0, cotangent, jnp.zeros_like(cotangent)).transpose(1, 2, 0, 3)
    before = to_next(slope[width_x - 1 :], "gx")
    after = to_previous(slope[:1], "gx")
    src = source.transpose(1, 2, 0, 3)
    src_near, src_far = swapped(src[:, 0], src[:, -1], "gy")

    cost = pl.CostEstimate(
        flops=54 * channels * channels * cell_count, bytes_accessed=2 * 1024 * 1024, transcendentals=0
    )
    vmem = pl.BlockSpec(memory_space=pltpu.VMEM)
    smem = pl.BlockSpec(memory_space=pltpu.SMEM)
    partial = pl.pallas_call(
        weight_kernel,
        out_shape=jax.ShapeDtypeStruct(share, jnp.bfloat16),
        in_specs=[smem] + [vmem] * 6,
        out_specs=vmem,
        scratch_shapes=[
            pltpu.VMEM(((width_x + 2) * channels, width_y * depth), jnp.bfloat16),
            pltpu.VMEM((width_x, 9 * channels, width_y * depth), jnp.bfloat16),
            pltpu.VMEM((5, 3 * channels, 2 * channels), jnp.float32),
            pltpu.VMEM((lines, 128), jnp.float32),
        ],
        compiler_params=PARAMS,
        cost_estimate=cost,
        name="weight_grad",
    )(parity, slope, before, after, src, src_near, src_far)
    shares = lax.all_to_all(partial.reshape(count_x, count_y, -1, *share[3:]), "gx", 0, 0, tiled=True)
    shares = jnp.sum(shares.astype(jnp.float32), axis=0).astype(jnp.bfloat16)
    shares = lax.all_to_all(shares, "gy", 0, 0, tiled=True)
    norm_scale = 1.0 / math.sqrt(cell_count * devices)
    grad_kernel = (jnp.sum(shares.astype(jnp.float32), axis=0) * norm_scale).reshape(-1)

    head = jnp.concatenate([before[:, 0], slope[:, 0], after[:, 0]], axis=0)
    tail = jnp.concatenate([before[:, -1], slope[:, -1], after[:, -1]], axis=0)
    head, tail, _ = lax.optimization_barrier((head, tail, partial))
    near, far = swapped(head, tail, "gy")
    grad_source = pl.pallas_call(
        source_kernel,
        out_shape=jax.ShapeDtypeStruct(slope.shape, jnp.bfloat16),
        in_specs=[smem] + [vmem] * 6,
        out_specs=vmem,
        scratch_shapes=[
            pltpu.VMEM((3 * (width_x + 2) * channels, width_y * depth), jnp.bfloat16),
            pltpu.VMEM((3, 9 * channels, channels), jnp.bfloat16),
            pltpu.VMEM((3, channels, width_y * depth), jnp.float32),
        ],
        compiler_params=PARAMS,
        cost_estimate=cost,
        name="source_grad",
    )(parity, slope, before, after, near, far, kernel)
    return (grad_source.transpose(2, 0, 1, 3), grad_kernel)


def solution(mesh):
    placed = (P(None, "gx", "gy", None), P(None, "gx", "gy", None), P(None, "gx", "gy", None), P())
    return jax.shard_map(
        on_device,
        mesh=mesh,
        in_specs=placed,
        out_specs=(P(None, "gx", "gy", None), P(("gx", "gy"))),
        check_vma=False,
    )
```

```python
import math

import jax
import jax.numpy as jnp
from jax import lax
from jax.experimental import pallas as pl
from jax.experimental.pallas import tpu as pltpu
from jax.sharding import PartitionSpec as P

NT = (((1,), (1,)), ((), ()))
TN = (((0,), (0,)), ((), ()))
PARAMS = pltpu.CompilerParams(vmem_limit_bytes=32 * 1024 * 1024)


def to_next(block, axis):
    count = lax.axis_size(axis)
    return lax.ppermute(block, axis, [(i, (i + 1) % count) for i in range(count)])


def to_previous(block, axis):
    count = lax.axis_size(axis)
    return lax.ppermute(block, axis, [((i + 1) % count, i) for i in range(count)])


def swapped(first, last, axis):
    count = lax.axis_size(axis)
    even = lax.axis_index(axis) & 1 == 0
    near = [(i, i ^ 1) for i in range(count)]
    far = [(i, (i - 1) % count if i % 2 == 0 else (i + 1) % count) for i in range(count)]
    got_far = lax.ppermute(jnp.where(even, first, last), axis, far)
    got_near = lax.ppermute(jnp.where(even, last, first), axis, near)
    return got_near, got_far


def roll_lanes(block, step):
    return pltpu.roll(block.astype(jnp.float32), step % block.shape[-1], axis=1).astype(block.dtype)


def weight_kernel(parity, slope, before, after, source, near, far, out, left, right, gram, ordered):
    width_x, width_y, channels, depth = slope.shape
    even = parity[0] == 0
    for y in range(width_y):
        lanes = slice(y * depth, (y + 1) * depth)
        left[0:channels, lanes] = before[0, y]
        for x in range(width_x):
            left[(x + 1) * channels : (x + 2) * channels, lanes] = slope[x, y]
        left[(width_x + 1) * channels :, lanes] = after[0, y]
    for x in range(width_x):
        for row in range(-1, width_y + 1):
            if row < 0:
                cells = jnp.where(even, far[x], near[x])
            elif row == width_y:
                cells = jnp.where(even, near[x], far[x])
            else:
                cells = source[x, row]
            for c in range(3):
                moved = cells if c == 1 else roll_lanes(cells, 1 - c)
                for b in range(3):
                    y = row + 1 - b
                    if 0 <= y < width_y:
                        first = (3 * b + c) * channels
                        right[x, first : first + channels, y * depth : (y + 1) * depth] = moved
    total = None
    for x in range(width_x):
        part = lax.dot_general(
            left[x * channels : (x + 3) * channels, :], right[x], NT, preferred_element_type=jnp.float32
        )
        total = part if total is None else total + part
    for pair in range(5):
        lanes = total[:, 2 * pair * channels : min(2 * pair + 2, 9) * channels]
        gram[pair, :, : lanes.shape[1]] = lanes
    half = channels // 2
    first_half = lax.broadcasted_iota(jnp.int32, (half, 2 * channels), 1) < channels
    for a in range(3):
        top = (2 - a) * channels
        for pair in range(5):
            low = gram[pair, pl.ds(top, half, stride=2), :]
            high = gram[pair, pl.ds(top + 1, half, stride=2), :]
            tap = 9 * a + 2 * pair
            ordered[tap * half : (tap + 1) * half, :] = jnp.where(first_half, low, pltpu.roll(high, channels, axis=1))
            if pair < 4:
                tap += 1
                ordered[tap * half : (tap + 1) * half, :] = jnp.where(
                    first_half, pltpu.roll(low, channels, axis=1), high
                )
    if len(out.shape) == 3:
        rows = out.shape[1]
        for part in range(out.shape[0]):
            out[part] = ordered[part * rows : (part + 1) * rows, :].astype(out.dtype)
    else:
        out[...] = ordered[...].astype(out.dtype)


def source_kernel(parity, slope, before, after, near, far, kernel, out, columns, weights, spread):
    width_x, width_y, channels, depth = slope.shape
    even = parity[0] == 0
    for wide_x in range(width_x + 2):
        for row in range(-1, width_y + 1):
            if row < 0:
                cells = jnp.where(even, far[wide_x], near[wide_x])
            elif row == width_y:
                cells = jnp.where(even, near[wide_x], far[wide_x])
            elif wide_x == 0:
                cells = before[0, row]
            elif wide_x == width_x + 1:
                cells = after[0, row]
            else:
                cells = slope[wide_x - 1, row]
            for b in range(3):
                y = row + b - 1
                if 0 <= y < width_y:
                    first = (3 * wide_x + b) * channels
                    columns[first : first + channels, y * depth : (y + 1) * depth] = cells
    for a in range(3):
        for b in range(3):
            for c in range(3):
                first = (3 * (2 - a) + b) * channels
                weights[c, first : first + channels, :] = kernel[9 * a + 3 * b + c]
    for x in range(width_x):
        cells = columns[3 * x * channels : 3 * (x + 3) * channels, :]
        for c in range(3):
            spread[c] = lax.dot_general(weights[c], cells, TN, preferred_element_type=jnp.float32)
        for y in range(width_y):
            lanes = slice(y * depth, (y + 1) * depth)
            total = spread[1, :, lanes]
            total += pltpu.roll(spread[0, :, lanes], depth - 1, axis=1)
            total += pltpu.roll(spread[2, :, lanes], 1, axis=1)
            out[x, y] = total.astype(out.dtype)


def on_device(source, preact, cotangent, kernel):
    channels, width_x, width_y, depth = source.shape
    devices = lax.axis_size("gx") * lax.axis_size("gy")
    cell_count = width_x * width_y * depth
    lines = 27 * channels * channels // 128
    share = (devices, lines // devices, 128) if lines % devices == 0 else (lines, 128)
    parity = (lax.axis_index("gy") & 1).reshape(1)

    slope = jnp.where(preact > 0, cotangent, jnp.zeros_like(cotangent)).transpose(1, 2, 0, 3)
    src = source.transpose(1, 2, 0, 3)
    slope, src = lax.optimization_barrier((slope, src))
    before = to_next(slope[width_x - 1 :], "gx")
    after = to_previous(slope[:1], "gx")
    src_near, src_far = swapped(src[:, 0], src[:, -1], "gy")

    cost = pl.CostEstimate(
        flops=54 * channels * channels * cell_count, bytes_accessed=2 * 1024 * 1024, transcendentals=0
    )
    vmem = pl.BlockSpec(memory_space=pltpu.VMEM)
    smem = pl.BlockSpec(memory_space=pltpu.SMEM)
    partial = pl.pallas_call(
        weight_kernel,
        out_shape=jax.ShapeDtypeStruct(share, jnp.bfloat16),
        in_specs=[smem] + [vmem] * 6,
        out_specs=vmem,
        scratch_shapes=[
            pltpu.VMEM(((width_x + 2) * channels, width_y * depth), jnp.bfloat16),
            pltpu.VMEM((width_x, 9 * channels, width_y * depth), jnp.bfloat16),
            pltpu.VMEM((5, 3 * channels, 2 * channels), jnp.float32),
            pltpu.VMEM((lines, 128), jnp.float32),
        ],
        compiler_params=PARAMS,
        cost_estimate=cost,
        name="weight_grad",
    )(parity, slope, before, after, src, src_near, src_far)
    head = jnp.concatenate([before[:, 0], slope[:, 0], after[:, 0]], axis=0)
    tail = jnp.concatenate([before[:, -1], slope[:, -1], after[:, -1]], axis=0)
    near, far = swapped(head, tail, "gy")
    partial, near, far = lax.optimization_barrier((partial, near, far))
    shares = lax.all_to_all(partial.reshape(devices, -1, *share[2:]), ("gx", "gy"), 0, 0, tiled=True)
    norm_scale = 1.0 / math.sqrt(cell_count * devices)
    grad_kernel = (jnp.sum(shares.astype(jnp.float32), axis=0) * norm_scale).reshape(-1)

    grad_source = pl.pallas_call(
        source_kernel,
        out_shape=jax.ShapeDtypeStruct(slope.shape, jnp.bfloat16),
        in_specs=[smem] + [vmem] * 6,
        out_specs=vmem,
        scratch_shapes=[
            pltpu.VMEM((3 * (width_x + 2) * channels, width_y * depth), jnp.bfloat16),
            pltpu.VMEM((3, 9 * channels, channels), jnp.bfloat16),
            pltpu.VMEM((3, channels, width_y * depth), jnp.float32),
        ],
        compiler_params=PARAMS,
        cost_estimate=cost,
        name="source_grad",
    )(parity, slope, before, after, near, far, kernel)
    return (grad_source.transpose(2, 0, 1, 3), grad_kernel)


def solution(mesh):
    placed = (P(None, "gx", "gy", None), P(None, "gx", "gy", None), P(None, "gx", "gy", None), P())
    return jax.shard_map(
        on_device,
        mesh=mesh,
        in_specs=placed,
        out_specs=(P(None, "gx", "gy", None), P(("gx", "gy"))),
        check_vma=False,
    )
```

```python
import math

import jax
import jax.numpy as jnp
from jax import lax
from jax.experimental import pallas as pl
from jax.experimental.pallas import tpu as pltpu
from jax.sharding import PartitionSpec as P

NT = (((1,), (1,)), ((), ()))
TN = (((0,), (0,)), ((), ()))
PARAMS = pltpu.CompilerParams(vmem_limit_bytes=32 * 1024 * 1024)


def to_next(block, axis):
    count = lax.axis_size(axis)
    return lax.ppermute(block, axis, [(i, (i + 1) % count) for i in range(count)])


def to_previous(block, axis):
    count = lax.axis_size(axis)
    return lax.ppermute(block, axis, [((i + 1) % count, i) for i in range(count)])


def swapped(first, last, axis):
    count = lax.axis_size(axis)
    even = lax.axis_index(axis) & 1 == 0
    near = [(i, i ^ 1) for i in range(count)]
    far = [(i, (i - 1) % count if i % 2 == 0 else (i + 1) % count) for i in range(count)]
    got_far = lax.ppermute(jnp.where(even, first, last), axis, far)
    got_near = lax.ppermute(jnp.where(even, last, first), axis, near)
    return got_near, got_far


def roll_lanes(block, step):
    return pltpu.roll(block.astype(jnp.float32), step % block.shape[-1], axis=1).astype(block.dtype)


def weight_kernel(parity, slope, before, after, source, near, far, out, left, right, gram, ordered):
    width_x, width_y, channels, depth = slope.shape
    even = parity[0] == 0
    for y in range(width_y):
        lanes = slice(y * depth, (y + 1) * depth)
        left[0:channels, lanes] = before[0, y]
        for x in range(width_x):
            left[(x + 1) * channels : (x + 2) * channels, lanes] = slope[x, y]
        left[(width_x + 1) * channels :, lanes] = after[0, y]
    for x in range(width_x):
        for row in range(-1, width_y + 1):
            if row < 0:
                cells = jnp.where(even, far[x], near[x])
            elif row == width_y:
                cells = jnp.where(even, near[x], far[x])
            else:
                cells = source[x, row]
            for c in range(3):
                moved = cells if c == 1 else roll_lanes(cells, 1 - c)
                for b in range(3):
                    y = row + 1 - b
                    if 0 <= y < width_y:
                        first = (3 * b + c) * channels
                        right[x, first : first + channels, y * depth : (y + 1) * depth] = moved
    total = None
    for x in range(width_x):
        part = lax.dot_general(
            left[x * channels : (x + 3) * channels, :], right[x], NT, preferred_element_type=jnp.float32
        )
        total = part if total is None else total + part
    for pair in range(5):
        lanes = total[:, 2 * pair * channels : min(2 * pair + 2, 9) * channels]
        gram[pair, :, : lanes.shape[1]] = lanes
    half = channels // 2
    first_half = lax.broadcasted_iota(jnp.int32, (half, 2 * channels), 1) < channels
    for a in range(3):
        top = (2 - a) * channels
        for pair in range(5):
            low = gram[pair, pl.ds(top, half, stride=2), :]
            high = gram[pair, pl.ds(top + 1, half, stride=2), :]
            tap = 9 * a + 2 * pair
            ordered[tap * half : (tap + 1) * half, :] = jnp.where(first_half, low, pltpu.roll(high, channels, axis=1))
            if pair < 4:
                tap += 1
                ordered[tap * half : (tap + 1) * half, :] = jnp.where(
                    first_half, pltpu.roll(low, channels, axis=1), high
                )
    if len(out.shape) == 3:
        rows = out.shape[1]
        for part in range(out.shape[0]):
            out[part] = ordered[part * rows : (part + 1) * rows, :].astype(out.dtype)
    else:
        out[...] = ordered[...].astype(out.dtype)


def source_kernel(parity, slope, before, after, near, far, kernel, out, columns, weights, spread):
    width_x, width_y, channels, depth = slope.shape
    even = parity[0] == 0
    for wide_x in range(width_x + 2):
        for row in range(-1, width_y + 1):
            if row < 0:
                cells = jnp.where(even, far[wide_x], near[wide_x])
            elif row == width_y:
                cells = jnp.where(even, near[wide_x], far[wide_x])
            elif wide_x == 0:
                cells = before[0, row]
            elif wide_x == width_x + 1:
                cells = after[0, row]
            else:
                cells = slope[wide_x - 1, row]
            for b in range(3):
                y = row + b - 1
                if 0 <= y < width_y:
                    first = (3 * wide_x + b) * channels
                    columns[first : first + channels, y * depth : (y + 1) * depth] = cells
    for a in range(3):
        for b in range(3):
            for c in range(3):
                first = (3 * (2 - a) + b) * channels
                weights[c, first : first + channels, :] = kernel[9 * a + 3 * b + c]
    for x in range(width_x):
        cells = columns[3 * x * channels : 3 * (x + 3) * channels, :]
        for c in range(3):
            spread[c] = lax.dot_general(weights[c], cells, TN, preferred_element_type=jnp.float32)
        for y in range(width_y):
            lanes = slice(y * depth, (y + 1) * depth)
            total = spread[1, :, lanes]
            total += pltpu.roll(spread[0, :, lanes], depth - 1, axis=1)
            total += pltpu.roll(spread[2, :, lanes], 1, axis=1)
            out[x, y] = total.astype(out.dtype)


def on_device(source, preact, cotangent, kernel):
    channels, width_x, width_y, depth = source.shape
    devices = lax.axis_size("gx") * lax.axis_size("gy")
    cell_count = width_x * width_y * depth
    lines = 27 * channels * channels // 128
    share = (devices, lines // devices, 128) if lines % devices == 0 else (lines, 128)
    parity = (lax.axis_index("gy") & 1).reshape(1)

    slope = jnp.where(preact > 0, cotangent, jnp.zeros_like(cotangent)).transpose(1, 2, 0, 3)
    src = source.transpose(1, 2, 0, 3)
    slope, src = lax.optimization_barrier((slope, src))
    before = to_next(slope[width_x - 1 :], "gx")
    after = to_previous(slope[:1], "gx")
    src_near, src_far = swapped(src[:, 0], src[:, -1], "gy")

    short, long = (
        pl.CostEstimate(flops=scale * channels * channels * cell_count, bytes_accessed=0, transcendentals=0)
        for scale in (1, 5400)
    )
    vmem = pl.BlockSpec(memory_space=pltpu.VMEM)
    smem = pl.BlockSpec(memory_space=pltpu.SMEM)
    partial = pl.pallas_call(
        weight_kernel,
        out_shape=jax.ShapeDtypeStruct(share, jnp.bfloat16),
        in_specs=[smem] + [vmem] * 6,
        out_specs=vmem,
        scratch_shapes=[
            pltpu.VMEM(((width_x + 2) * channels, width_y * depth), jnp.bfloat16),
            pltpu.VMEM((width_x, 9 * channels, width_y * depth), jnp.bfloat16),
            pltpu.VMEM((5, 3 * channels, 2 * channels), jnp.float32),
            pltpu.VMEM((lines, 128), jnp.float32),
        ],
        compiler_params=PARAMS,
        cost_estimate=short,
        name="weight_grad",
    )(parity, slope, before, after, src, src_near, src_far)
    head = jnp.concatenate([before[:, 0], slope[:, 0], after[:, 0]], axis=0)
    tail = jnp.concatenate([before[:, -1], slope[:, -1], after[:, -1]], axis=0)
    near, far = swapped(head, tail, "gy")
    shares = lax.all_to_all(partial.reshape(devices, -1, *share[2:]), ("gx", "gy"), 0, 0, tiled=True)
    norm_scale = 1.0 / math.sqrt(cell_count * devices)
    grad_kernel = (jnp.sum(shares.astype(jnp.float32), axis=0) * norm_scale).reshape(-1)

    grad_source = pl.pallas_call(
        source_kernel,
        out_shape=jax.ShapeDtypeStruct(slope.shape, jnp.bfloat16),
        in_specs=[smem] + [vmem] * 6,
        out_specs=vmem,
        scratch_shapes=[
            pltpu.VMEM((3 * (width_x + 2) * channels, width_y * depth), jnp.bfloat16),
            pltpu.VMEM((3, 9 * channels, channels), jnp.bfloat16),
            pltpu.VMEM((3, channels, width_y * depth), jnp.float32),
        ],
        compiler_params=PARAMS,
        cost_estimate=long,
        name="source_grad",
    )(parity, slope, before, after, near, far, kernel)
    return (grad_source.transpose(2, 0, 1, 3), grad_kernel)


def solution(mesh):
    placed = (P(None, "gx", "gy", None), P(None, "gx", "gy", None), P(None, "gx", "gy", None), P())
    return jax.shard_map(
        on_device,
        mesh=mesh,
        in_specs=placed,
        out_specs=(P(None, "gx", "gy", None), P(("gx", "gy"))),
        check_vma=False,
    )
```

```python
import math

import jax
import jax.numpy as jnp
from jax import lax
from jax.experimental import pallas as pl
from jax.experimental.pallas import tpu as pltpu
from jax.sharding import PartitionSpec as P

NT = (((1,), (1,)), ((), ()))
TN = (((0,), (0,)), ((), ()))
PARAMS = pltpu.CompilerParams(vmem_limit_bytes=32 * 1024 * 1024)


def to_next(block, axis):
    count = lax.axis_size(axis)
    return lax.ppermute(block, axis, [(i, (i + 1) % count) for i in range(count)])


def to_previous(block, axis):
    count = lax.axis_size(axis)
    return lax.ppermute(block, axis, [((i + 1) % count, i) for i in range(count)])


def swapped(first, last, axis):
    count = lax.axis_size(axis)
    even = lax.axis_index(axis) & 1 == 0
    near = [(i, i ^ 1) for i in range(count)]
    far = [(i, (i - 1) % count if i % 2 == 0 else (i + 1) % count) for i in range(count)]
    got_far = lax.ppermute(jnp.where(even, first, last), axis, far)
    got_near = lax.ppermute(jnp.where(even, last, first), axis, near)
    return got_near, got_far


def fill_columns(parity, slope, before, after, rows, corners, columns):
    width_x, width_y, channels, depth = slope.shape
    even = parity[0] == 0
    for wide_x in range(width_x + 2):
        inside = 0 < wide_x <= width_x
        near, far = rows if inside else corners
        place = wide_x - 1 if inside else min(wide_x, 1)
        for row in range(-1, width_y + 1):
            if row < 0:
                cells = jnp.where(even, far[place], near[place])
            elif row == width_y:
                cells = jnp.where(even, near[place], far[place])
            elif inside:
                cells = slope[wide_x - 1, row]
            else:
                cells = (after if wide_x else before)[0, row]
            for b in range(3):
                y = row + b - 1
                if 0 <= y < width_y:
                    first = (3 * wide_x + b) * channels
                    columns[first : first + channels, y * depth : (y + 1) * depth] = cells


def weight_kernel(
    parity, slope, before, after, row_near, row_far, corner_near, corner_far, source, out, columns, moved, gram, ordered
):
    width_x, width_y, channels, depth = source.shape
    fill_columns(parity, slope, before, after, (row_near, row_far), (corner_near, corner_far), columns)
    for x in range(width_x):
        for y in range(width_y):
            lanes = slice(y * depth, (y + 1) * depth)
            cells = source[x, y]
            wide = cells.astype(jnp.float32)
            moved[x, 0:channels, lanes] = pltpu.roll(wide, 1, axis=1).astype(cells.dtype)
            moved[x, channels : 2 * channels, lanes] = cells
            moved[x, 2 * channels :, lanes] = pltpu.roll(wide, depth - 1, axis=1).astype(cells.dtype)
    total = None
    for x in range(width_x):
        part = lax.dot_general(
            columns[3 * x * channels : 3 * (x + 3) * channels, :], moved[x], NT, preferred_element_type=jnp.float32
        )
        total = part if total is None else total + part
    gram[0] = total[:, : 2 * channels]
    gram[1, :, :channels] = total[:, 2 * channels :]
    half = channels // 2
    first_half = lax.broadcasted_iota(jnp.int32, (half, 2 * channels), 1) < channels
    for a in range(3):
        for b in range(3):
            top = (3 * (2 - a) + b) * channels
            line = (9 * a + 3 * b) * half
            low = gram[0, pl.ds(top, half, stride=2), :]
            high = gram[0, pl.ds(top + 1, half, stride=2), :]
            ordered[line : line + half, :] = jnp.where(first_half, low, pltpu.roll(high, channels, axis=1))
            ordered[line + half : line + 2 * half, :] = jnp.where(first_half, pltpu.roll(low, channels, axis=1), high)
            low = gram[1, pl.ds(top, half, stride=2), :]
            high = gram[1, pl.ds(top + 1, half, stride=2), :]
            ordered[line + 2 * half : line + 3 * half, :] = jnp.where(
                first_half, low, pltpu.roll(high, channels, axis=1)
            )
    if len(out.shape) == 5:
        _, pairs, count_y, rows, _ = out.shape
        for part in range(2 * pairs * count_y):
            place = (part // count_y % 2, part // count_y // 2, part % count_y)
            out[place] = ordered[part * rows : (part + 1) * rows, :].astype(out.dtype)
    else:
        out[...] = ordered[...].astype(out.dtype)


def source_kernel(
    parity, slope, before, after, row_near, row_far, corner_near, corner_far, kernel, out, columns, weights, spread
):
    width_x, width_y, channels, depth = slope.shape
    fill_columns(parity, slope, before, after, (row_near, row_far), (corner_near, corner_far), columns)
    for a in range(3):
        for b in range(3):
            for c in range(3):
                first = (3 * (2 - a) + b) * channels
                weights[c, first : first + channels, :] = kernel[9 * a + 3 * b + c]
    for x in range(width_x):
        cells = columns[3 * x * channels : 3 * (x + 3) * channels, :]
        for c in range(3):
            spread[c] = lax.dot_general(weights[c], cells, TN, preferred_element_type=jnp.float32)
        for y in range(width_y):
            lanes = slice(y * depth, (y + 1) * depth)
            total = spread[1, :, lanes]
            total += pltpu.roll(spread[0, :, lanes], depth - 1, axis=1)
            total += pltpu.roll(spread[2, :, lanes], 1, axis=1)
            out[x, y] = total.astype(out.dtype)


def on_device(source, preact, cotangent, kernel):
    channels, width_x, width_y, depth = source.shape
    devices = lax.axis_size("gx") * lax.axis_size("gy")
    cell_count = width_x * width_y * depth
    lines = 27 * channels * channels // 128
    pairs, count_y = lax.axis_size("gx") // 2, lax.axis_size("gy")
    share = (2, pairs, count_y, lines // devices, 128) if lines % devices == 0 else (lines, 128)
    parity = (lax.axis_index("gy") & 1).reshape(1)

    slope = jnp.where(preact > 0, cotangent, jnp.zeros_like(cotangent)).transpose(1, 2, 0, 3)
    before = to_next(slope[width_x - 1 :], "gx")
    after = to_previous(slope[:1], "gx")
    row_near, row_far = swapped(slope[:, 0], slope[:, -1], "gy")
    head = jnp.concatenate([before[:, 0], after[:, 0]], axis=0)
    tail = jnp.concatenate([before[:, -1], after[:, -1]], axis=0)
    corner_near, corner_far = swapped(head, tail, "gy")
    halo = (parity, slope, before, after, row_near, row_far, corner_near, corner_far)

    cost = pl.CostEstimate(
        flops=54 * channels * channels * cell_count, bytes_accessed=2 * 1024 * 1024, transcendentals=0
    )
    vmem = pl.BlockSpec(memory_space=pltpu.VMEM)
    smem = pl.BlockSpec(memory_space=pltpu.SMEM)
    columns = pltpu.VMEM((3 * (width_x + 2) * channels, width_y * depth), jnp.bfloat16)
    partial = pl.pallas_call(
        weight_kernel,
        out_shape=jax.ShapeDtypeStruct(share, jnp.bfloat16),
        in_specs=[smem] + [vmem] * 8,
        out_specs=vmem,
        scratch_shapes=[
            columns,
            pltpu.VMEM((width_x, 3 * channels, width_y * depth), jnp.bfloat16),
            pltpu.VMEM((2, 9 * channels, 2 * channels), jnp.float32),
            pltpu.VMEM((lines, 128), jnp.float32),
        ],
        compiler_params=PARAMS,
        cost_estimate=cost,
        name="weight_grad",
    )(*halo, source.transpose(1, 2, 0, 3))
    if len(share) == 2:
        partial = partial.reshape(pairs, 2, count_y, -1).transpose(1, 0, 2, 3)
    core = lax.axis_index("gx") & 1
    swap = [(i, i ^ 1) for i in range(2 * pairs)]
    other = lax.ppermute(lax.dynamic_index_in_dim(partial, 1 - core, 0, False), "gx", swap)
    own = lax.dynamic_index_in_dim(partial, core, 0, False)
    both = (own.astype(jnp.float32) + other.astype(jnp.float32)).astype(jnp.bfloat16)
    groups = [[(2 * i + c) * count_y + j for i in range(pairs) for j in range(count_y)] for c in range(2)]
    both = both.reshape(pairs * count_y, *both.shape[2:])
    shares = lax.all_to_all(both, ("gx", "gy"), 0, 0, axis_index_groups=groups, tiled=True)
    norm_scale = 1.0 / math.sqrt(cell_count * devices)
    grad_kernel = (jnp.sum(shares.astype(jnp.float32), axis=0) * norm_scale).reshape(-1)

    grad_source = pl.pallas_call(
        source_kernel,
        out_shape=jax.ShapeDtypeStruct(slope.shape, jnp.bfloat16),
        in_specs=[smem] + [vmem] * 8,
        out_specs=vmem,
        scratch_shapes=[
            columns,
            pltpu.VMEM((3, 9 * channels, channels), jnp.bfloat16),
            pltpu.VMEM((3, channels, width_y * depth), jnp.float32),
        ],
        compiler_params=PARAMS,
        cost_estimate=cost,
        name="source_grad",
    )(*halo, kernel)
    return (grad_source.transpose(2, 0, 1, 3), grad_kernel)


def solution(mesh):
    placed = (P(None, "gx", "gy", None), P(None, "gx", "gy", None), P(None, "gx", "gy", None), P())
    return jax.shard_map(
        on_device,
        mesh=mesh,
        in_specs=placed,
        out_specs=(P(None, "gx", "gy", None), P(("gx", "gy"))),
        check_vma=False,
    )
```

```python
import math

import jax
import jax.numpy as jnp
from jax import lax
from jax.experimental import pallas as pl
from jax.experimental.pallas import tpu as pltpu
from jax.sharding import PartitionSpec as P

NT = (((1,), (1,)), ((), ()))
TN = (((0,), (0,)), ((), ()))
PARAMS = pltpu.CompilerParams(vmem_limit_bytes=32 * 1024 * 1024)


def to_next(block, axis):
    count = lax.axis_size(axis)
    return lax.ppermute(block, axis, [(i, (i + 1) % count) for i in range(count)])


def to_previous(block, axis):
    count = lax.axis_size(axis)
    return lax.ppermute(block, axis, [((i + 1) % count, i) for i in range(count)])


def swapped(first, last, axis):
    count = lax.axis_size(axis)
    even = lax.axis_index(axis) & 1 == 0
    near = [(i, i ^ 1) for i in range(count)]
    far = [(i, (i - 1) % count if i % 2 == 0 else (i + 1) % count) for i in range(count)]
    got_far = lax.ppermute(jnp.where(even, first, last), axis, far)
    got_near = lax.ppermute(jnp.where(even, last, first), axis, near)
    return got_near, got_far


def roll_lanes(block, step):
    return pltpu.roll(block.astype(jnp.float32), step % block.shape[-1], axis=1).astype(block.dtype)


def weight_kernel(parity, slope, before, after, source, near, far, out, left, right, gram, ordered):
    width_x, width_y, channels, depth = slope.shape
    even = parity[0] == 0
    for y in range(width_y):
        lanes = slice(y * depth, (y + 1) * depth)
        left[0:channels, lanes] = before[0, y]
        for x in range(width_x):
            left[(x + 1) * channels : (x + 2) * channels, lanes] = slope[x, y]
        left[(width_x + 1) * channels :, lanes] = after[0, y]
    for x in range(width_x):
        for row in range(-1, width_y + 1):
            if row < 0:
                cells = jnp.where(even, far[x], near[x])
            elif row == width_y:
                cells = jnp.where(even, near[x], far[x])
            else:
                cells = source[x, row]
            for c in range(3):
                moved = cells if c == 1 else roll_lanes(cells, 1 - c)
                for b in range(3):
                    y = row + 1 - b
                    if 0 <= y < width_y:
                        first = (3 * b + c) * channels
                        right[x, first : first + channels, y * depth : (y + 1) * depth] = moved
    total = None
    for x in range(width_x):
        part = lax.dot_general(
            left[x * channels : (x + 3) * channels, :], right[x], NT, preferred_element_type=jnp.float32
        )
        total = part if total is None else total + part
    for pair in range(5):
        lanes = total[:, 2 * pair * channels : min(2 * pair + 2, 9) * channels]
        gram[pair, :, : lanes.shape[1]] = lanes
    half = channels // 2
    first_half = lax.broadcasted_iota(jnp.int32, (half, 2 * channels), 1) < channels
    for a in range(3):
        top = (2 - a) * channels
        for pair in range(5):
            low = gram[pair, pl.ds(top, half, stride=2), :]
            high = gram[pair, pl.ds(top + 1, half, stride=2), :]
            tap = 9 * a + 2 * pair
            ordered[tap * half : (tap + 1) * half, :] = jnp.where(first_half, low, pltpu.roll(high, channels, axis=1))
            if pair < 4:
                tap += 1
                ordered[tap * half : (tap + 1) * half, :] = jnp.where(
                    first_half, pltpu.roll(low, channels, axis=1), high
                )
    if len(out.shape) == 3:
        rows = out.shape[1]
        for part in range(out.shape[0]):
            out[part] = ordered[part * rows : (part + 1) * rows, :].astype(out.dtype)
    else:
        out[...] = ordered[...].astype(out.dtype)


def source_kernel(parity, slope, before, after, near, far, kernel, out, columns, weights, spread):
    width_x, width_y, channels, depth = slope.shape
    even = parity[0] == 0
    for wide_x in range(width_x + 2):
        for row in range(-1, width_y + 1):
            if row < 0:
                cells = jnp.where(even, far[wide_x], near[wide_x])
            elif row == width_y:
                cells = jnp.where(even, near[wide_x], far[wide_x])
            elif wide_x == 0:
                cells = before[0, row]
            elif wide_x == width_x + 1:
                cells = after[0, row]
            else:
                cells = slope[wide_x - 1, row]
            for b in range(3):
                y = row + b - 1
                if 0 <= y < width_y:
                    first = (3 * wide_x + b) * channels
                    columns[first : first + channels, y * depth : (y + 1) * depth] = cells
    for a in range(3):
        for b in range(3):
            for c in range(3):
                first = (3 * (2 - a) + b) * channels
                weights[c, first : first + channels, :] = kernel[9 * a + 3 * b + c]
    for x in range(width_x):
        cells = columns[3 * x * channels : 3 * (x + 3) * channels, :]
        for c in range(3):
            spread[c] = lax.dot_general(weights[c], cells, TN, preferred_element_type=jnp.float32)
        for y in range(width_y):
            lanes = slice(y * depth, (y + 1) * depth)
            total = spread[1, :, lanes]
            total += pltpu.roll(spread[0, :, lanes], depth - 1, axis=1)
            total += pltpu.roll(spread[2, :, lanes], 1, axis=1)
            out[x, y] = total.astype(out.dtype)


def on_device(source, preact, cotangent, kernel):
    channels, width_x, width_y, depth = source.shape
    devices = lax.axis_size("gx") * lax.axis_size("gy")
    cell_count = width_x * width_y * depth
    lines = 27 * channels * channels // 128
    share = (devices, lines // devices, 128) if lines % devices == 0 else (lines, 128)
    parity = (lax.axis_index("gy") & 1).reshape(1)

    slope = jnp.where(preact > 0, cotangent, jnp.zeros_like(cotangent)).transpose(1, 2, 0, 3)
    src = source.transpose(1, 2, 0, 3)
    slope, src = lax.optimization_barrier((slope, src))
    before = to_next(slope[width_x - 1 :], "gx")
    after = to_previous(slope[:1], "gx")
    src_near, src_far = swapped(src[:, 0], src[:, -1], "gy")

    short, long = (
        pl.CostEstimate(flops=scale * channels * channels * cell_count, bytes_accessed=2 * 1024 * 1024, transcendentals=0)
        for scale in (54, 5400)
    )
    vmem = pl.BlockSpec(memory_space=pltpu.VMEM)
    smem = pl.BlockSpec(memory_space=pltpu.SMEM)
    partial = pl.pallas_call(
        weight_kernel,
        out_shape=jax.ShapeDtypeStruct(share, jnp.bfloat16),
        in_specs=[smem] + [vmem] * 6,
        out_specs=vmem,
        scratch_shapes=[
            pltpu.VMEM(((width_x + 2) * channels, width_y * depth), jnp.bfloat16),
            pltpu.VMEM((width_x, 9 * channels, width_y * depth), jnp.bfloat16),
            pltpu.VMEM((5, 3 * channels, 2 * channels), jnp.float32),
            pltpu.VMEM((lines, 128), jnp.float32),
        ],
        compiler_params=PARAMS,
        cost_estimate=short,
        name="weight_grad",
    )(parity, slope, before, after, src, src_near, src_far)
    head = jnp.concatenate([before[:, 0], slope[:, 0], after[:, 0]], axis=0)
    tail = jnp.concatenate([before[:, -1], slope[:, -1], after[:, -1]], axis=0)
    near, far = swapped(head, tail, "gy")
    shares = lax.all_to_all(partial.reshape(devices, -1, *share[2:]), ("gx", "gy"), 0, 0, tiled=True)
    norm_scale = 1.0 / math.sqrt(cell_count * devices)
    grad_kernel = (jnp.sum(shares.astype(jnp.float32), axis=0) * norm_scale).reshape(-1)

    grad_source = pl.pallas_call(
        source_kernel,
        out_shape=jax.ShapeDtypeStruct(slope.shape, jnp.bfloat16),
        in_specs=[smem] + [vmem] * 6,
        out_specs=vmem,
        scratch_shapes=[
            pltpu.VMEM((3 * (width_x + 2) * channels, width_y * depth), jnp.bfloat16),
            pltpu.VMEM((3, 9 * channels, channels), jnp.bfloat16),
            pltpu.VMEM((3, channels, width_y * depth), jnp.float32),
        ],
        compiler_params=PARAMS,
        cost_estimate=long,
        name="source_grad",
    )(parity, slope, before, after, near, far, kernel)
    return (grad_source.transpose(2, 0, 1, 3), grad_kernel)


def solution(mesh):
    placed = (P(None, "gx", "gy", None), P(None, "gx", "gy", None), P(None, "gx", "gy", None), P())
    return jax.shard_map(
        on_device,
        mesh=mesh,
        in_specs=placed,
        out_specs=(P(None, "gx", "gy", None), P(("gx", "gy"))),
        check_vma=False,
    )
```

```python
import math

import jax
import jax.numpy as jnp
from jax import lax
from jax.experimental import pallas as pl
from jax.experimental.pallas import tpu as pltpu
from jax.sharding import PartitionSpec as P

NT = (((1,), (1,)), ((), ()))
TN = (((0,), (0,)), ((), ()))
PARAMS = pltpu.CompilerParams(vmem_limit_bytes=32 * 1024 * 1024)


def to_next(block, axis):
    count = lax.axis_size(axis)
    return lax.ppermute(block, axis, [(i, (i + 1) % count) for i in range(count)])


def to_previous(block, axis):
    count = lax.axis_size(axis)
    return lax.ppermute(block, axis, [((i + 1) % count, i) for i in range(count)])


def swapped(first, last, axis):
    count = lax.axis_size(axis)
    even = lax.axis_index(axis) & 1 == 0
    near = [(i, i ^ 1) for i in range(count)]
    far = [(i, (i - 1) % count if i % 2 == 0 else (i + 1) % count) for i in range(count)]
    got_far = lax.ppermute(jnp.where(even, first, last), axis, far)
    got_near = lax.ppermute(jnp.where(even, last, first), axis, near)
    return got_near, got_far


def roll_lanes(block, step):
    return pltpu.roll(block.astype(jnp.float32), step % block.shape[-1], axis=1).astype(block.dtype)


def weight_kernel(parity, slope, before, after, far, near, source, out, left, right, gram, ordered):
    width_x, width_y, channels, depth = slope.shape
    even = parity[0] == 0
    for y in range(width_y):
        lanes = slice(y * depth, (y + 1) * depth)
        left[0:channels, lanes] = before[0, y]
        for x in range(width_x):
            left[(x + 1) * channels : (x + 2) * channels, lanes] = slope[x, y]
        left[(width_x + 1) * channels :, lanes] = after[0, y]
    for x in range(width_x):
        for row in range(-1, width_y + 1):
            if row < 0:
                cells = jnp.where(even, far[x], near[x])
            elif row == width_y:
                cells = jnp.where(even, near[x], far[x])
            else:
                cells = source[x, row]
            for c in range(3):
                moved = cells if c == 1 else roll_lanes(cells, 1 - c)
                for b in range(3):
                    y = row + 1 - b
                    if 0 <= y < width_y:
                        first = (3 * b + c) * channels
                        right[x, first : first + channels, y * depth : (y + 1) * depth] = moved
    total = None
    for x in range(width_x):
        part = lax.dot_general(
            left[x * channels : (x + 3) * channels, :], right[x], NT, preferred_element_type=jnp.float32
        )
        total = part if total is None else total + part
    for pair in range(5):
        lanes = total[:, 2 * pair * channels : min(2 * pair + 2, 9) * channels]
        gram[pair, :, : lanes.shape[1]] = lanes
    half = channels // 2
    first_half = lax.broadcasted_iota(jnp.int32, (half, 2 * channels), 1) < channels
    for a in range(3):
        top = (2 - a) * channels
        for pair in range(5):
            low = gram[pair, pl.ds(top, half, stride=2), :]
            high = gram[pair, pl.ds(top + 1, half, stride=2), :]
            tap = 9 * a + 2 * pair
            ordered[tap * half : (tap + 1) * half, :] = jnp.where(first_half, low, pltpu.roll(high, channels, axis=1))
            if pair < 4:
                tap += 1
                ordered[tap * half : (tap + 1) * half, :] = jnp.where(
                    first_half, pltpu.roll(low, channels, axis=1), high
                )
    if len(out.shape) == 3:
        rows = out.shape[1]
        for part in range(out.shape[0]):
            out[part] = ordered[part * rows : (part + 1) * rows, :].astype(out.dtype)
    else:
        out[...] = ordered[...].astype(out.dtype)


def source_kernel(parity, slope, before, after, _, __, far, near, kernel, out, columns, weights, spread):
    width_x, width_y, channels, depth = slope.shape
    even = parity[0] == 0
    for wide_x in range(width_x + 2):
        for row in range(-1, width_y + 1):
            if row < 0:
                cells = jnp.where(even, far[wide_x], near[wide_x])
            elif row == width_y:
                cells = jnp.where(even, near[wide_x], far[wide_x])
            elif wide_x == 0:
                cells = before[0, row]
            elif wide_x == width_x + 1:
                cells = after[0, row]
            else:
                cells = slope[wide_x - 1, row]
            for b in range(3):
                y = row + b - 1
                if 0 <= y < width_y:
                    first = (3 * wide_x + b) * channels
                    columns[first : first + channels, y * depth : (y + 1) * depth] = cells
    for a in range(3):
        for b in range(3):
            for c in range(3):
                first = (3 * (2 - a) + b) * channels
                weights[c, first : first + channels, :] = kernel[9 * a + 3 * b + c]
    for x in range(width_x):
        cells = columns[3 * x * channels : 3 * (x + 3) * channels, :]
        for c in range(3):
            spread[c] = lax.dot_general(weights[c], cells, TN, preferred_element_type=jnp.float32)
        for y in range(width_y):
            lanes = slice(y * depth, (y + 1) * depth)
            total = spread[1, :, lanes]
            total += pltpu.roll(spread[0, :, lanes], depth - 1, axis=1)
            total += pltpu.roll(spread[2, :, lanes], 1, axis=1)
            out[x, y] = total.astype(out.dtype)


def on_device(source, preact, cotangent, kernel):
    channels, width_x, width_y, depth = source.shape
    devices = lax.axis_size("gx") * lax.axis_size("gy")
    cell_count = width_x * width_y * depth
    lines = 27 * channels * channels // 128
    share = (devices, lines // devices, 128) if lines % devices == 0 else (lines, 128)
    parity = (lax.axis_index("gy") & 1).reshape(1)

    slope = jnp.where(preact > 0, cotangent, jnp.zeros_like(cotangent)).transpose(1, 2, 0, 3)
    src = source.transpose(1, 2, 0, 3)
    slope, src = lax.optimization_barrier((slope, src))
    before = to_next(slope[width_x - 1 :], "gx")
    after = to_previous(slope[:1], "gx")
    src_near, src_far = swapped(src[:, 0], src[:, -1], "gy")

    short, long = (
        pl.CostEstimate(flops=scale * channels * channels * cell_count, bytes_accessed=2 * 1024 * 1024, transcendentals=0)
        for scale in (54, 5400)
    )
    vmem = pl.BlockSpec(memory_space=pltpu.VMEM)
    smem = pl.BlockSpec(memory_space=pltpu.SMEM)
    partial = pl.pallas_call(
        weight_kernel,
        out_shape=jax.ShapeDtypeStruct(share, jnp.bfloat16),
        in_specs=[smem] + [vmem] * 6,
        out_specs=vmem,
        scratch_shapes=[
            pltpu.VMEM(((width_x + 2) * channels, width_y * depth), jnp.bfloat16),
            pltpu.VMEM((width_x, 9 * channels, width_y * depth), jnp.bfloat16),
            pltpu.VMEM((5, 3 * channels, 2 * channels), jnp.float32),
            pltpu.VMEM((lines, 128), jnp.float32),
        ],
        compiler_params=PARAMS,
        cost_estimate=short,
        name="weight_grad",
    )(parity, slope, before, after, src_far, src_near, src)
    head = jnp.concatenate([before[:, 0], slope[:, 0], after[:, 0]], axis=0)
    tail = jnp.concatenate([before[:, -1], slope[:, -1], after[:, -1]], axis=0)
    near, far = swapped(head, tail, "gy")
    shares = lax.all_to_all(partial.reshape(devices, -1, *share[2:]), ("gx", "gy"), 0, 0, tiled=True)
    norm_scale = 1.0 / math.sqrt(cell_count * devices)
    grad_kernel = (jnp.sum(shares.astype(jnp.float32), axis=0) * norm_scale).reshape(-1)

    grad_source = pl.pallas_call(
        source_kernel,
        out_shape=jax.ShapeDtypeStruct(slope.shape, jnp.bfloat16),
        in_specs=[smem] + [vmem] * 3 + [pl.BlockSpec(memory_space=pl.ANY)] * 2 + [vmem] * 3,
        out_specs=vmem,
        scratch_shapes=[
            pltpu.VMEM((3 * (width_x + 2) * channels, width_y * depth), jnp.bfloat16),
            pltpu.VMEM((3, 9 * channels, channels), jnp.bfloat16),
            pltpu.VMEM((3, channels, width_y * depth), jnp.float32),
        ],
        compiler_params=PARAMS,
        cost_estimate=long,
        name="source_grad",
    )(parity, slope, before, after, src_far, src_near, far, near, kernel)
    return (grad_source.transpose(2, 0, 1, 3), grad_kernel)


def solution(mesh):
    placed = (P(None, "gx", "gy", None), P(None, "gx", "gy", None), P(None, "gx", "gy", None), P())
    return jax.shard_map(
        on_device,
        mesh=mesh,
        in_specs=placed,
        out_specs=(P(None, "gx", "gy", None), P(("gx", "gy"))),
        check_vma=False,
    )
```

```python
import math

import jax
import jax.numpy as jnp
from jax import lax
from jax.experimental import pallas as pl
from jax.experimental.pallas import tpu as pltpu
from jax.sharding import PartitionSpec as P

NT = (((1,), (1,)), ((), ()))
TN = (((0,), (0,)), ((), ()))
PARAMS = pltpu.CompilerParams(vmem_limit_bytes=32 * 1024 * 1024)


def to_next(block, axis):
    count = lax.axis_size(axis)
    return lax.ppermute(block, axis, [(i, (i + 1) % count) for i in range(count)])


def to_previous(block, axis):
    count = lax.axis_size(axis)
    return lax.ppermute(block, axis, [((i + 1) % count, i) for i in range(count)])


def swapped(first, last, axis):
    count = lax.axis_size(axis)
    even = lax.axis_index(axis) & 1 == 0
    near = [(i, i ^ 1) for i in range(count)]
    far = [(i, (i - 1) % count if i % 2 == 0 else (i + 1) % count) for i in range(count)]
    got_far = lax.ppermute(jnp.where(even, first, last), axis, far)
    got_near = lax.ppermute(jnp.where(even, last, first), axis, near)
    return got_near, got_far


def roll_lanes(block, step):
    return pltpu.roll(block.astype(jnp.float32), step % block.shape[-1], axis=1).astype(block.dtype)


def weight_kernel(parity, slope, before, after, far, near, source, out, left, right, gram, ordered):
    width_x, width_y, channels, depth = slope.shape
    even = parity[0] == 0
    for y in range(width_y):
        lanes = slice(y * depth, (y + 1) * depth)
        left[0:channels, lanes] = before[0, y]
        for x in range(width_x):
            left[(x + 1) * channels : (x + 2) * channels, lanes] = slope[x, y]
        left[(width_x + 1) * channels :, lanes] = after[0, y]
    for x in range(width_x):
        for row in range(-1, width_y + 1):
            if row < 0:
                cells = jnp.where(even, far[x], near[x])
            elif row == width_y:
                cells = jnp.where(even, near[x], far[x])
            else:
                cells = source[x, row]
            for c in range(3):
                moved = cells if c == 1 else roll_lanes(cells, 1 - c)
                for b in range(3):
                    y = row + 1 - b
                    if 0 <= y < width_y:
                        first = (3 * b + c) * channels
                        right[x, first : first + channels, y * depth : (y + 1) * depth] = moved
    total = None
    for x in range(width_x):
        part = lax.dot_general(
            left[x * channels : (x + 3) * channels, :], right[x], NT, preferred_element_type=jnp.float32
        )
        total = part if total is None else total + part
    for pair in range(5):
        lanes = total[:, 2 * pair * channels : min(2 * pair + 2, 9) * channels]
        gram[pair, :, : lanes.shape[1]] = lanes
    half = channels // 2
    first_half = lax.broadcasted_iota(jnp.int32, (half, 2 * channels), 1) < channels
    for a in range(3):
        top = (2 - a) * channels
        for pair in range(5):
            low = gram[pair, pl.ds(top, half, stride=2), :]
            high = gram[pair, pl.ds(top + 1, half, stride=2), :]
            tap = 9 * a + 2 * pair
            ordered[tap * half : (tap + 1) * half, :] = jnp.where(first_half, low, pltpu.roll(high, channels, axis=1))
            if pair < 4:
                tap += 1
                ordered[tap * half : (tap + 1) * half, :] = jnp.where(
                    first_half, pltpu.roll(low, channels, axis=1), high
                )
    if len(out.shape) == 3:
        rows = out.shape[1]
        for part in range(out.shape[0]):
            out[part] = ordered[part * rows : (part + 1) * rows, :].astype(out.dtype)
    else:
        out[...] = ordered[...].astype(out.dtype)


def source_kernel(parity, slope, before, after, _, __, far, near, kernel, out, columns, weights, spread):
    width_x, width_y, channels, depth = slope.shape
    even = parity[0] == 0
    for wide_x in range(width_x + 2):
        for row in range(-1, width_y + 1):
            if row < 0:
                cells = jnp.where(even, far[wide_x], near[wide_x])
            elif row == width_y:
                cells = jnp.where(even, near[wide_x], far[wide_x])
            elif wide_x == 0:
                cells = before[0, row]
            elif wide_x == width_x + 1:
                cells = after[0, row]
            else:
                cells = slope[wide_x - 1, row]
            for b in range(3):
                y = row + b - 1
                if 0 <= y < width_y:
                    first = (3 * wide_x + b) * channels
                    columns[first : first + channels, y * depth : (y + 1) * depth] = cells
    for a in range(3):
        for b in range(3):
            for c in range(3):
                first = (3 * (2 - a) + b) * channels
                weights[c, first : first + channels, :] = kernel[9 * a + 3 * b + c]
    for x in range(width_x):
        cells = columns[3 * x * channels : 3 * (x + 3) * channels, :]
        for c in range(3):
            spread[c] = lax.dot_general(weights[c], cells, TN, preferred_element_type=jnp.float32)
        for y in range(width_y):
            lanes = slice(y * depth, (y + 1) * depth)
            total = spread[1, :, lanes]
            total += pltpu.roll(spread[0, :, lanes], depth - 1, axis=1)
            total += pltpu.roll(spread[2, :, lanes], 1, axis=1)
            out[x, y] = total.astype(out.dtype)


def on_device(source, preact, cotangent, kernel):
    channels, width_x, width_y, depth = source.shape
    devices = lax.axis_size("gx") * lax.axis_size("gy")
    cell_count = width_x * width_y * depth
    lines = 27 * channels * channels // 128
    share = (devices, lines // devices, 128) if lines % devices == 0 else (lines, 128)
    parity = (lax.axis_index("gy") & 1).reshape(1)

    slope = jnp.where(preact > 0, cotangent, jnp.zeros_like(cotangent)).transpose(1, 2, 0, 3)
    src = source.transpose(1, 2, 0, 3)
    slope, src = lax.optimization_barrier((slope, src))
    before = to_next(slope[width_x - 1 :], "gx")
    after = to_previous(slope[:1], "gx")
    src_near, src_far = swapped(src[:, 0], src[:, -1], "gy")

    short, long = (
        pl.CostEstimate(flops=scale * channels * cell_count, bytes_accessed=scale * 15000, transcendentals=0)
        for scale in (54, 5400)
    )
    vmem = pl.BlockSpec(memory_space=pltpu.VMEM)
    smem = pl.BlockSpec(memory_space=pltpu.SMEM)
    partial = pl.pallas_call(
        weight_kernel,
        out_shape=jax.ShapeDtypeStruct(share, jnp.bfloat16),
        in_specs=[smem] + [vmem] * 6,
        out_specs=vmem,
        scratch_shapes=[
            pltpu.VMEM(((width_x + 2) * channels, width_y * depth), jnp.bfloat16),
            pltpu.VMEM((width_x, 9 * channels, width_y * depth), jnp.bfloat16),
            pltpu.VMEM((5, 3 * channels, 2 * channels), jnp.float32),
            pltpu.VMEM((lines, 128), jnp.float32),
        ],
        compiler_params=PARAMS,
        cost_estimate=short,
        name="weight_grad",
    )(parity, slope, before, after, src_far, src_near, src)
    head = jnp.concatenate([before[:, 0], slope[:, 0], after[:, 0]], axis=0)
    tail = jnp.concatenate([before[:, -1], slope[:, -1], after[:, -1]], axis=0)
    near, far = swapped(head, tail, "gy")
    shares = lax.all_to_all(partial.reshape(devices, -1, *share[2:]), ("gx", "gy"), 0, 0, tiled=True)
    norm_scale = 1.0 / math.sqrt(cell_count * devices)
    grad_kernel = (jnp.sum(shares.astype(jnp.float32), axis=0) * norm_scale).reshape(-1)

    grad_source = pl.pallas_call(
        source_kernel,
        out_shape=jax.ShapeDtypeStruct(slope.shape, jnp.bfloat16),
        in_specs=[smem] + [vmem] * 3 + [pl.BlockSpec(memory_space=pl.ANY)] * 2 + [vmem] * 3,
        out_specs=vmem,
        scratch_shapes=[
            pltpu.VMEM((3 * (width_x + 2) * channels, width_y * depth), jnp.bfloat16),
            pltpu.VMEM((3, 9 * channels, channels), jnp.bfloat16),
            pltpu.VMEM((3, channels, width_y * depth), jnp.float32),
        ],
        compiler_params=PARAMS,
        cost_estimate=long,
        name="source_grad",
    )(parity, slope, before, after, src_far, src_near, far, near, kernel)
    return (grad_source.transpose(2, 0, 1, 3), grad_kernel)


def solution(mesh):
    placed = (P(None, "gx", "gy", None), P(None, "gx", "gy", None), P(None, "gx", "gy", None), P())
    return jax.shard_map(
        on_device,
        mesh=mesh,
        in_specs=placed,
        out_specs=(P(None, "gx", "gy", None), P(("gx", "gy"))),
        check_vma=False,
    )
```

```python
import math

import jax
import jax.numpy as jnp
from jax import lax
from jax.experimental import pallas as pl
from jax.experimental.pallas import tpu as pltpu
from jax.sharding import PartitionSpec as P

NT = (((1,), (1,)), ((), ()))
TN = (((0,), (0,)), ((), ()))
PARAMS = pltpu.CompilerParams(vmem_limit_bytes=32 * 1024 * 1024)


def to_next(block, axis):
    count = lax.axis_size(axis)
    return lax.ppermute(block, axis, [(i, (i + 1) % count) for i in range(count)])


def to_previous(block, axis):
    count = lax.axis_size(axis)
    return lax.ppermute(block, axis, [((i + 1) % count, i) for i in range(count)])


def swapped(first, last, axis):
    count = lax.axis_size(axis)
    even = lax.axis_index(axis) & 1 == 0
    near = [(i, i ^ 1) for i in range(count)]
    far = [(i, (i - 1) % count if i % 2 == 0 else (i + 1) % count) for i in range(count)]
    got_far = lax.ppermute(jnp.where(even, first, last), axis, far)
    got_near = lax.ppermute(jnp.where(even, last, first), axis, near)
    return got_near, got_far


def roll_lanes(block, step):
    return pltpu.roll(block.astype(jnp.float32), step % block.shape[-1], axis=1).astype(block.dtype)


def weight_kernel(parity, slope, before, after, far, near, source, out, left, right, gram, ordered):
    width_x, width_y, channels, depth = slope.shape
    even = parity[0] == 0
    for y in range(width_y):
        lanes = slice(y * depth, (y + 1) * depth)
        left[0:channels, lanes] = before[0, y]
        for x in range(width_x):
            left[(x + 1) * channels : (x + 2) * channels, lanes] = slope[x, y]
        left[(width_x + 1) * channels :, lanes] = after[0, y]
    for x in range(width_x):
        for row in range(-1, width_y + 1):
            if row < 0:
                cells = jnp.where(even, far[x], near[x])
            elif row == width_y:
                cells = jnp.where(even, near[x], far[x])
            else:
                cells = source[x, row]
            for c in range(3):
                moved = cells if c == 1 else roll_lanes(cells, 1 - c)
                for b in range(3):
                    y = row + 1 - b
                    if 0 <= y < width_y:
                        first = (3 * b + c) * channels
                        right[x, first : first + channels, y * depth : (y + 1) * depth] = moved
    total = None
    for x in range(width_x):
        part = lax.dot_general(
            left[x * channels : (x + 3) * channels, :], right[x], NT, preferred_element_type=jnp.float32
        )
        total = part if total is None else total + part
    for pair in range(5):
        lanes = total[:, 2 * pair * channels : min(2 * pair + 2, 9) * channels]
        gram[pair, :, : lanes.shape[1]] = lanes
    half = channels // 2
    first_half = lax.broadcasted_iota(jnp.int32, (half, 2 * channels), 1) < channels
    for a in range(3):
        top = (2 - a) * channels
        for pair in range(5):
            low = gram[pair, pl.ds(top, half, stride=2), :]
            high = gram[pair, pl.ds(top + 1, half, stride=2), :]
            tap = 9 * a + 2 * pair
            ordered[tap * half : (tap + 1) * half, :] = jnp.where(first_half, low, pltpu.roll(high, channels, axis=1))
            if pair < 4:
                tap += 1
                ordered[tap * half : (tap + 1) * half, :] = jnp.where(
                    first_half, pltpu.roll(low, channels, axis=1), high
                )
    if len(out.shape) == 3:
        rows = out.shape[1]
        for part in range(out.shape[0]):
            out[part] = ordered[part * rows : (part + 1) * rows, :].astype(out.dtype)
    else:
        out[...] = ordered[...].astype(out.dtype)


def source_kernel(parity, slope, before, after, _, __, far, near, kernel, out, columns, weights, spread):
    width_x, width_y, channels, depth = slope.shape
    even = parity[0] == 0
    for wide_x in range(width_x + 2):
        for row in range(-1, width_y + 1):
            if row < 0:
                cells = jnp.where(even, far[wide_x], near[wide_x])
            elif row == width_y:
                cells = jnp.where(even, near[wide_x], far[wide_x])
            elif wide_x == 0:
                cells = before[0, row]
            elif wide_x == width_x + 1:
                cells = after[0, row]
            else:
                cells = slope[wide_x - 1, row]
            for b in range(3):
                y = row + b - 1
                if 0 <= y < width_y:
                    first = (3 * wide_x + b) * channels
                    columns[first : first + channels, y * depth : (y + 1) * depth] = cells
    for a in range(3):
        for b in range(3):
            for c in range(3):
                first = (3 * (2 - a) + b) * channels
                weights[c, first : first + channels, :] = kernel[9 * a + 3 * b + c]
    for x in range(width_x):
        cells = columns[3 * x * channels : 3 * (x + 3) * channels, :]
        for c in range(3):
            spread[c] = lax.dot_general(weights[c], cells, TN, preferred_element_type=jnp.float32)
        for y in range(width_y):
            lanes = slice(y * depth, (y + 1) * depth)
            total = spread[1, :, lanes]
            total += pltpu.roll(spread[0, :, lanes], depth - 1, axis=1)
            total += pltpu.roll(spread[2, :, lanes], 1, axis=1)
            out[x, y] = total.astype(out.dtype)


def on_device(source, preact, cotangent, kernel):
    channels, width_x, width_y, depth = source.shape
    devices = lax.axis_size("gx") * lax.axis_size("gy")
    cell_count = width_x * width_y * depth
    lines = 27 * channels * channels // 128
    share = (devices, lines // devices, 128) if lines % devices == 0 else (lines, 128)
    parity = (lax.axis_index("gy") & 1).reshape(1)

    slope = jnp.where(preact > 0, cotangent, jnp.zeros_like(cotangent)).transpose(1, 2, 0, 3)
    src = source.transpose(1, 2, 0, 3)
    slope, src = lax.optimization_barrier((slope, src))
    before = to_next(slope[width_x - 1 :], "gx")
    after = to_previous(slope[:1], "gx")
    src_near, src_far = swapped(src[:, 0], src[:, -1], "gy")

    short = pl.CostEstimate(flops=0, bytes_accessed=800_000, transcendentals=0)
    long = pl.CostEstimate(
        flops=5400 * channels * channels * cell_count, bytes_accessed=2 * 1024 * 1024, transcendentals=0
    )
    vmem = pl.BlockSpec(memory_space=pltpu.VMEM)
    smem = pl.BlockSpec(memory_space=pltpu.SMEM)
    partial = pl.pallas_call(
        weight_kernel,
        out_shape=jax.ShapeDtypeStruct(share, jnp.bfloat16),
        in_specs=[smem] + [vmem] * 6,
        out_specs=vmem,
        scratch_shapes=[
            pltpu.VMEM(((width_x + 2) * channels, width_y * depth), jnp.bfloat16),
            pltpu.VMEM((width_x, 9 * channels, width_y * depth), jnp.bfloat16),
            pltpu.VMEM((5, 3 * channels, 2 * channels), jnp.float32),
            pltpu.VMEM((lines, 128), jnp.float32),
        ],
        compiler_params=PARAMS,
        cost_estimate=short,
        name="weight_grad",
    )(parity, slope, before, after, src_far, src_near, src)
    head = jnp.concatenate([before[:, 0], slope[:, 0], after[:, 0]], axis=0)
    tail = jnp.concatenate([before[:, -1], slope[:, -1], after[:, -1]], axis=0)
    near, far = swapped(head, tail, "gy")
    shares = lax.all_to_all(partial.reshape(devices, -1, *share[2:]), ("gx", "gy"), 0, 0, tiled=True)
    norm_scale = 1.0 / math.sqrt(cell_count * devices)
    grad_kernel = (jnp.sum(shares.astype(jnp.float32), axis=0) * norm_scale).reshape(-1)

    grad_source = pl.pallas_call(
        source_kernel,
        out_shape=jax.ShapeDtypeStruct(slope.shape, jnp.bfloat16),
        in_specs=[smem] + [vmem] * 3 + [pl.BlockSpec(memory_space=pl.ANY)] * 2 + [vmem] * 3,
        out_specs=vmem,
        scratch_shapes=[
            pltpu.VMEM((3 * (width_x + 2) * channels, width_y * depth), jnp.bfloat16),
            pltpu.VMEM((3, 9 * channels, channels), jnp.bfloat16),
            pltpu.VMEM((3, channels, width_y * depth), jnp.float32),
        ],
        compiler_params=PARAMS,
        cost_estimate=long,
        name="source_grad",
    )(parity, slope, before, after, src_far, src_near, far, near, kernel)
    return (grad_source.transpose(2, 0, 1, 3), grad_kernel)


def solution(mesh):
    placed = (P(None, "gx", "gy", None), P(None, "gx", "gy", None), P(None, "gx", "gy", None), P())
    return jax.shard_map(
        on_device,
        mesh=mesh,
        in_specs=placed,
        out_specs=(P(None, "gx", "gy", None), P(("gx", "gy"))),
        check_vma=False,
    )
```

```python
import math

import jax
import jax.numpy as jnp
from jax import lax
from jax.experimental import pallas as pl
from jax.experimental.pallas import tpu as pltpu
from jax.sharding import PartitionSpec as P

NT = (((1,), (1,)), ((), ()))
TN = (((0,), (0,)), ((), ()))
PARAMS = pltpu.CompilerParams(vmem_limit_bytes=32 * 1024 * 1024)


def to_next(block, axis):
    count = lax.axis_size(axis)
    return lax.ppermute(block, axis, [(i, (i + 1) % count) for i in range(count)])


def to_previous(block, axis):
    count = lax.axis_size(axis)
    return lax.ppermute(block, axis, [((i + 1) % count, i) for i in range(count)])


def swapped(first, last, axis):
    count = lax.axis_size(axis)
    even = lax.axis_index(axis) & 1 == 0
    near = [(i, i ^ 1) for i in range(count)]
    far = [(i, (i - 1) % count if i % 2 == 0 else (i + 1) % count) for i in range(count)]
    got_far = lax.ppermute(jnp.where(even, first, last), axis, far)
    got_near = lax.ppermute(jnp.where(even, last, first), axis, near)
    return got_near, got_far


def roll_lanes(block, step):
    return pltpu.roll(block.astype(jnp.float32), step % block.shape[-1], axis=1).astype(block.dtype)


def weight_kernel(parity, slope, before, after, source, far, near, out, left, right, gram, ordered):
    width_x, width_y, channels, depth = slope.shape
    even = parity[0] == 0
    for y in range(width_y):
        lanes = slice(y * depth, (y + 1) * depth)
        left[0:channels, lanes] = before[0, y]
        for x in range(width_x):
            left[(x + 1) * channels : (x + 2) * channels, lanes] = slope[x, y]
        left[(width_x + 1) * channels :, lanes] = after[0, y]
    for x in range(width_x):
        for row in range(-1, width_y + 1):
            if row < 0:
                cells = jnp.where(even, far[x], near[x])
            elif row == width_y:
                cells = jnp.where(even, near[x], far[x])
            else:
                cells = source[x, row]
            for c in range(3):
                moved = cells if c == 1 else roll_lanes(cells, 1 - c)
                for b in range(3):
                    y = row + 1 - b
                    if 0 <= y < width_y:
                        first = (3 * b + c) * channels
                        right[x, first : first + channels, y * depth : (y + 1) * depth] = moved
    total = None
    for x in range(width_x):
        part = lax.dot_general(
            left[x * channels : (x + 3) * channels, :], right[x], NT, preferred_element_type=jnp.float32
        )
        total = part if total is None else total + part
    for pair in range(5):
        lanes = total[:, 2 * pair * channels : min(2 * pair + 2, 9) * channels]
        gram[pair, :, : lanes.shape[1]] = lanes
    half = channels // 2
    first_half = lax.broadcasted_iota(jnp.int32, (half, 2 * channels), 1) < channels
    for a in range(3):
        top = (2 - a) * channels
        for pair in range(5):
            low = gram[pair, pl.ds(top, half, stride=2), :]
            high = gram[pair, pl.ds(top + 1, half, stride=2), :]
            tap = 9 * a + 2 * pair
            ordered[tap * half : (tap + 1) * half, :] = jnp.where(first_half, low, pltpu.roll(high, channels, axis=1))
            if pair < 4:
                tap += 1
                ordered[tap * half : (tap + 1) * half, :] = jnp.where(
                    first_half, pltpu.roll(low, channels, axis=1), high
                )
    if len(out.shape) == 3:
        rows = out.shape[1]
        for part in range(out.shape[0]):
            out[part] = ordered[part * rows : (part + 1) * rows, :].astype(out.dtype)
    else:
        out[...] = ordered[...].astype(out.dtype)


def plane(slope, before, after, wide_x, row):
    if wide_x == 0:
        return before[0, row]
    if wide_x == slope.shape[0] + 1:
        return after[0, row]
    return slope[wide_x - 1, row]


def gather(parts):
    depth = parts[1].shape[1]
    return parts[1] + pltpu.roll(parts[0], depth - 1, axis=1) + pltpu.roll(parts[2], 1, axis=1)


def edge_kernel(slope, before, after, kernel, down, up, columns, weights):
    width_x, width_y, channels, depth = slope.shape
    for out, row, b in ((down, 0, 0), (up, width_y - 1, 2)):
        for wide_x in range(width_x + 2):
            columns[wide_x * channels : (wide_x + 1) * channels, :] = plane(slope, before, after, wide_x, row)
        for a in range(3):
            for c in range(3):
                weights[c, (2 - a) * channels : (3 - a) * channels, :] = kernel[9 * a + 3 * b + c]
        for x in range(width_x):
            cells = columns[x * channels : (x + 3) * channels, :]
            parts = [lax.dot_general(weights[c], cells, TN, preferred_element_type=jnp.float32) for c in range(3)]
            out[x] = gather(parts).astype(out.dtype)


def source_kernel(parity, slope, before, after, far, near, kernel, out, columns, weights, spread):
    width_x, width_y, channels, depth = slope.shape
    even = parity[0] == 0
    zeros = jnp.zeros((channels, depth), slope.dtype)
    for wide_x in range(width_x + 2):
        for row in range(-1, width_y + 1):
            cells = plane(slope, before, after, wide_x, row) if 0 <= row < width_y else zeros
            for b in range(3):
                y = row + b - 1
                if 0 <= y < width_y:
                    first = (3 * wide_x + b) * channels
                    columns[first : first + channels, y * depth : (y + 1) * depth] = cells
    for a in range(3):
        for b in range(3):
            for c in range(3):
                first = (3 * (2 - a) + b) * channels
                weights[c, first : first + channels, :] = kernel[9 * a + 3 * b + c]
    for x in range(width_x):
        cells = columns[3 * x * channels : 3 * (x + 3) * channels, :]
        for c in range(3):
            spread[c] = lax.dot_general(weights[c], cells, TN, preferred_element_type=jnp.float32)
        for y in range(width_y):
            lanes = slice(y * depth, (y + 1) * depth)
            total = gather([spread[c, :, lanes] for c in range(3)])
            if y == 0:
                total += jnp.where(even, far[x], near[x]).astype(jnp.float32)
            if y == width_y - 1:
                total += jnp.where(even, near[x], far[x]).astype(jnp.float32)
            out[x, y] = total.astype(out.dtype)


def on_device(source, preact, cotangent, kernel):
    channels, width_x, width_y, depth = source.shape
    devices = lax.axis_size("gx") * lax.axis_size("gy")
    cell_count = width_x * width_y * depth
    lines = 27 * channels * channels // 128
    share = (devices, lines // devices, 128) if lines % devices == 0 else (lines, 128)
    parity = (lax.axis_index("gy") & 1).reshape(1)

    slope = jnp.where(preact > 0, cotangent, jnp.zeros_like(cotangent)).transpose(1, 2, 0, 3)
    src = source.transpose(1, 2, 0, 3)
    slope, src = lax.optimization_barrier((slope, src))
    before = to_next(slope[width_x - 1 :], "gx")
    after = to_previous(slope[:1], "gx")
    src_near, src_far = swapped(src[:, 0], src[:, -1], "gy")

    cost = pl.CostEstimate(
        flops=54 * channels * channels * cell_count, bytes_accessed=2 * 1024 * 1024, transcendentals=0
    )
    vmem = pl.BlockSpec(memory_space=pltpu.VMEM)
    smem = pl.BlockSpec(memory_space=pltpu.SMEM)
    partial = pl.pallas_call(
        weight_kernel,
        out_shape=jax.ShapeDtypeStruct(share, jnp.bfloat16),
        in_specs=[smem] + [vmem] * 6,
        out_specs=vmem,
        scratch_shapes=[
            pltpu.VMEM(((width_x + 2) * channels, width_y * depth), jnp.bfloat16),
            pltpu.VMEM((width_x, 9 * channels, width_y * depth), jnp.bfloat16),
            pltpu.VMEM((5, 3 * channels, 2 * channels), jnp.float32),
            pltpu.VMEM((lines, 128), jnp.float32),
        ],
        compiler_params=PARAMS,
        cost_estimate=cost,
        name="weight_grad",
    )(parity, slope, before, after, src, src_far, src_near)
    edge = jax.ShapeDtypeStruct((width_x, channels, depth), jnp.bfloat16)
    down, up = pl.pallas_call(
        edge_kernel,
        out_shape=(edge, edge),
        in_specs=[vmem] * 4,
        out_specs=(vmem, vmem),
        scratch_shapes=[
            pltpu.VMEM(((width_x + 2) * channels, depth), jnp.bfloat16),
            pltpu.VMEM((3, 3 * channels, channels), jnp.bfloat16),
        ],
        compiler_params=PARAMS,
        cost_estimate=pl.CostEstimate(
            flops=36 * channels * channels * width_x * depth, bytes_accessed=256 * 1024, transcendentals=0
        ),
        name="source_edges",
    )(slope, before, after, kernel)
    near, far = swapped(down, up, "gy")
    partial, near, far = lax.optimization_barrier((partial, near, far))
    shares = lax.all_to_all(partial.reshape(devices, -1, *share[2:]), ("gx", "gy"), 0, 0, tiled=True)
    norm_scale = 1.0 / math.sqrt(cell_count * devices)
    grad_kernel = (jnp.sum(shares.astype(jnp.float32), axis=0) * norm_scale).reshape(-1)

    grad_source = pl.pallas_call(
        source_kernel,
        out_shape=jax.ShapeDtypeStruct(slope.shape, jnp.bfloat16),
        in_specs=[smem] + [vmem] * 6,
        out_specs=vmem,
        scratch_shapes=[
            pltpu.VMEM((3 * (width_x + 2) * channels, width_y * depth), jnp.bfloat16),
            pltpu.VMEM((3, 9 * channels, channels), jnp.bfloat16),
            pltpu.VMEM((3, channels, width_y * depth), jnp.float32),
        ],
        compiler_params=PARAMS,
        cost_estimate=cost,
        name="source_grad",
    )(parity, slope, before, after, far, near, kernel)
    return (grad_source.transpose(2, 0, 1, 3), grad_kernel)


def solution(mesh):
    placed = (P(None, "gx", "gy", None), P(None, "gx", "gy", None), P(None, "gx", "gy", None), P())
    return jax.shard_map(
        on_device,
        mesh=mesh,
        in_specs=placed,
        out_specs=(P(None, "gx", "gy", None), P(("gx", "gy"))),
        check_vma=False,
    )
```

```python
import math

import jax
import jax.numpy as jnp
from jax import lax
from jax.experimental import pallas as pl
from jax.experimental.pallas import tpu as pltpu
from jax.sharding import PartitionSpec as P

NT = (((1,), (1,)), ((), ()))
TN = (((0,), (0,)), ((), ()))
PARAMS = pltpu.CompilerParams(vmem_limit_bytes=32 * 1024 * 1024)


def to_next(block, axis):
    count = lax.axis_size(axis)
    return lax.ppermute(block, axis, [(i, (i + 1) % count) for i in range(count)])


def to_previous(block, axis):
    count = lax.axis_size(axis)
    return lax.ppermute(block, axis, [((i + 1) % count, i) for i in range(count)])


def swapped(first, last, axis):
    count = lax.axis_size(axis)
    even = lax.axis_index(axis) & 1 == 0
    near = [(i, i ^ 1) for i in range(count)]
    far = [(i, (i - 1) % count if i % 2 == 0 else (i + 1) % count) for i in range(count)]
    got_far = lax.ppermute(jnp.where(even, first, last), axis, far)
    got_near = lax.ppermute(jnp.where(even, last, first), axis, near)
    return got_near, got_far


def roll_lanes(block, step):
    return pltpu.roll(block.astype(jnp.float32), step % block.shape[-1], axis=1).astype(block.dtype)


def weight_kernel(parity, slope, after, before, source, near, far, out, left, right, gram, ordered):
    width_x, width_y, channels, depth = slope.shape
    even = parity[0] == 0
    for y in range(width_y):
        lanes = slice(y * depth, (y + 1) * depth)
        left[0:channels, lanes] = before[0, y]
        for x in range(width_x):
            left[(x + 1) * channels : (x + 2) * channels, lanes] = slope[x, y]
        left[(width_x + 1) * channels :, lanes] = after[0, y]
    for x in range(width_x):
        for row in range(-1, width_y + 1):
            if row < 0:
                cells = jnp.where(even, far[x], near[x])
            elif row == width_y:
                cells = jnp.where(even, near[x], far[x])
            else:
                cells = source[x, row]
            for c in range(3):
                moved = cells if c == 1 else roll_lanes(cells, 1 - c)
                for b in range(3):
                    y = row + 1 - b
                    if 0 <= y < width_y:
                        first = (3 * b + c) * channels
                        right[x, first : first + channels, y * depth : (y + 1) * depth] = moved
    total = None
    for x in range(width_x):
        part = lax.dot_general(
            left[x * channels : (x + 3) * channels, :], right[x], NT, preferred_element_type=jnp.float32
        )
        total = part if total is None else total + part
    for pair in range(5):
        lanes = total[:, 2 * pair * channels : min(2 * pair + 2, 9) * channels]
        gram[pair, :, : lanes.shape[1]] = lanes
    half = channels // 2
    first_half = lax.broadcasted_iota(jnp.int32, (half, 2 * channels), 1) < channels
    for a in range(3):
        top = (2 - a) * channels
        for pair in range(5):
            low = gram[pair, pl.ds(top, half, stride=2), :]
            high = gram[pair, pl.ds(top + 1, half, stride=2), :]
            tap = 9 * a + 2 * pair
            ordered[tap * half : (tap + 1) * half, :] = jnp.where(first_half, low, pltpu.roll(high, channels, axis=1))
            if pair < 4:
                tap += 1
                ordered[tap * half : (tap + 1) * half, :] = jnp.where(
                    first_half, pltpu.roll(low, channels, axis=1), high
                )
    if len(out.shape) == 3:
        rows = out.shape[1]
        for part in range(out.shape[0]):
            out[part] = ordered[part * rows : (part + 1) * rows, :].astype(out.dtype)
    else:
        out[...] = ordered[...].astype(out.dtype)


def plane(slope, before, after, wide_x, row):
    if wide_x == 0:
        return before[0, row]
    if wide_x == slope.shape[0] + 1:
        return after[0, row]
    return slope[wide_x - 1, row]


def gather(parts):
    depth = parts[1].shape[1]
    return parts[1] + pltpu.roll(parts[0], depth - 1, axis=1) + pltpu.roll(parts[2], 1, axis=1)


def edge_kernel(slope, after, before, kernel, down, up, columns, weights):
    width_x, width_y, channels, depth = slope.shape
    for out, row, b in ((down, 0, 0), (up, width_y - 1, 2)):
        for wide_x in range(width_x + 2):
            columns[wide_x * channels : (wide_x + 1) * channels, :] = plane(slope, before, after, wide_x, row)
        for a in range(3):
            for c in range(3):
                weights[c, (2 - a) * channels : (3 - a) * channels, :] = kernel[9 * a + 3 * b + c]
        for x in range(width_x):
            cells = columns[x * channels : (x + 3) * channels, :]
            parts = [lax.dot_general(weights[c], cells, TN, preferred_element_type=jnp.float32) for c in range(3)]
            out[x] = gather(parts).astype(out.dtype)


def source_kernel(parity, slope, after, before, far, near, kernel, out, columns, weights, spread):
    width_x, width_y, channels, depth = slope.shape
    even = parity[0] == 0
    zeros = jnp.zeros((channels, depth), slope.dtype)
    for wide_x in range(width_x + 2):
        for row in range(-1, width_y + 1):
            cells = plane(slope, before, after, wide_x, row) if 0 <= row < width_y else zeros
            for b in range(3):
                y = row + b - 1
                if 0 <= y < width_y:
                    first = (3 * wide_x + b) * channels
                    columns[first : first + channels, y * depth : (y + 1) * depth] = cells
    for a in range(3):
        for b in range(3):
            for c in range(3):
                first = (3 * (2 - a) + b) * channels
                weights[c, first : first + channels, :] = kernel[9 * a + 3 * b + c]
    for x in range(width_x):
        cells = columns[3 * x * channels : 3 * (x + 3) * channels, :]
        for c in range(3):
            spread[c] = lax.dot_general(weights[c], cells, TN, preferred_element_type=jnp.float32)
        for y in range(width_y):
            lanes = slice(y * depth, (y + 1) * depth)
            total = gather([spread[c, :, lanes] for c in range(3)])
            if y == 0:
                total += jnp.where(even, far[x], near[x]).astype(jnp.float32)
            if y == width_y - 1:
                total += jnp.where(even, near[x], far[x]).astype(jnp.float32)
            out[x, y] = total.astype(out.dtype)


def on_device(source, preact, cotangent, kernel):
    channels, width_x, width_y, depth = source.shape
    devices = lax.axis_size("gx") * lax.axis_size("gy")
    cell_count = width_x * width_y * depth
    lines = 27 * channels * channels // 128
    share = (devices, lines // devices, 128) if lines % devices == 0 else (lines, 128)
    parity = (lax.axis_index("gy") & 1).reshape(1)

    slope = jnp.where(preact > 0, cotangent, jnp.zeros_like(cotangent)).transpose(1, 2, 0, 3)
    src = source.transpose(1, 2, 0, 3)
    slope, src = lax.optimization_barrier((slope, src))
    before = to_next(slope[width_x - 1 :], "gx")
    after = to_previous(slope[:1], "gx")
    src_near, src_far = swapped(src[:, 0], src[:, -1], "gy")

    cost = pl.CostEstimate(
        flops=54 * channels * channels * cell_count, bytes_accessed=2 * 1024 * 1024, transcendentals=0
    )
    vmem = pl.BlockSpec(memory_space=pltpu.VMEM)
    smem = pl.BlockSpec(memory_space=pltpu.SMEM)
    partial = pl.pallas_call(
        weight_kernel,
        out_shape=jax.ShapeDtypeStruct(share, jnp.bfloat16),
        in_specs=[smem] + [vmem] * 6,
        out_specs=vmem,
        scratch_shapes=[
            pltpu.VMEM(((width_x + 2) * channels, width_y * depth), jnp.bfloat16),
            pltpu.VMEM((width_x, 9 * channels, width_y * depth), jnp.bfloat16),
            pltpu.VMEM((5, 3 * channels, 2 * channels), jnp.float32),
            pltpu.VMEM((lines, 128), jnp.float32),
        ],
        compiler_params=PARAMS,
        cost_estimate=cost,
        name="weight_grad",
    )(parity, slope, after, before, src, src_near, src_far)
    edge = jax.ShapeDtypeStruct((width_x, channels, depth), jnp.bfloat16)
    down, up = pl.pallas_call(
        edge_kernel,
        out_shape=(edge, edge),
        in_specs=[vmem] * 4,
        out_specs=(vmem, vmem),
        scratch_shapes=[
            pltpu.VMEM(((width_x + 2) * channels, depth), jnp.bfloat16),
            pltpu.VMEM((3, 3 * channels, channels), jnp.bfloat16),
        ],
        compiler_params=PARAMS,
        cost_estimate=pl.CostEstimate(
            flops=36 * channels * channels * width_x * depth, bytes_accessed=256 * 1024, transcendentals=0
        ),
        name="source_edges",
    )(slope, after, before, kernel)
    near, far = swapped(down, up, "gy")
    partial, near, far = lax.optimization_barrier((partial, near, far))
    shares = lax.all_to_all(partial.reshape(devices, -1, *share[2:]), ("gx", "gy"), 0, 0, tiled=True)
    norm_scale = 1.0 / math.sqrt(cell_count * devices)
    grad_kernel = (jnp.sum(shares.astype(jnp.float32), axis=0) * norm_scale).reshape(-1)

    grad_source = pl.pallas_call(
        source_kernel,
        out_shape=jax.ShapeDtypeStruct(slope.shape, jnp.bfloat16),
        in_specs=[smem] + [vmem] * 6,
        out_specs=vmem,
        scratch_shapes=[
            pltpu.VMEM((3 * (width_x + 2) * channels, width_y * depth), jnp.bfloat16),
            pltpu.VMEM((3, 9 * channels, channels), jnp.bfloat16),
            pltpu.VMEM((3, channels, width_y * depth), jnp.float32),
        ],
        compiler_params=PARAMS,
        cost_estimate=cost,
        name="source_grad",
    )(parity, slope, after, before, far, near, kernel)
    return (grad_source.transpose(2, 0, 1, 3), grad_kernel)


def solution(mesh):
    placed = (P(None, "gx", "gy", None), P(None, "gx", "gy", None), P(None, "gx", "gy", None), P())
    return jax.shard_map(
        on_device,
        mesh=mesh,
        in_specs=placed,
        out_specs=(P(None, "gx", "gy", None), P(("gx", "gy"))),
        check_vma=False,
    )
```

```python
import math

import jax
import jax.numpy as jnp
from jax import lax
from jax.experimental import pallas as pl
from jax.experimental.pallas import tpu as pltpu
from jax.sharding import PartitionSpec as P

NT = (((1,), (1,)), ((), ()))
TN = (((0,), (0,)), ((), ()))
PARAMS = pltpu.CompilerParams(vmem_limit_bytes=32 * 1024 * 1024)


def to_next(block, axis):
    count = lax.axis_size(axis)
    return lax.ppermute(block, axis, [(i, (i + 1) % count) for i in range(count)])


def to_previous(block, axis):
    count = lax.axis_size(axis)
    return lax.ppermute(block, axis, [((i + 1) % count, i) for i in range(count)])


def swapped(first, last, axis):
    count = lax.axis_size(axis)
    even = lax.axis_index(axis) & 1 == 0
    near = [(i, i ^ 1) for i in range(count)]
    far = [(i, (i - 1) % count if i % 2 == 0 else (i + 1) % count) for i in range(count)]
    got_far = lax.ppermute(jnp.where(even, first, last), axis, far)
    got_near = lax.ppermute(jnp.where(even, last, first), axis, near)
    return got_near, got_far


def roll_lanes(block, step):
    return pltpu.roll(block.astype(jnp.float32), step % block.shape[-1], axis=1).astype(block.dtype)


def weight_kernel(parity, slope, after, before, source, near, far, out, left, right, gram, ordered):
    width_x, width_y, channels, depth = slope.shape
    even = parity[0] == 0
    for y in range(width_y):
        lanes = slice(y * depth, (y + 1) * depth)
        left[0:channels, lanes] = before[0, y]
        for x in range(width_x):
            left[(x + 1) * channels : (x + 2) * channels, lanes] = slope[x, y]
        left[(width_x + 1) * channels :, lanes] = after[0, y]
    for x in range(width_x):
        for row in range(-1, width_y + 1):
            if row < 0:
                cells = jnp.where(even, far[x], near[x])
            elif row == width_y:
                cells = jnp.where(even, near[x], far[x])
            else:
                cells = source[x, row]
            for c in range(3):
                moved = cells if c == 1 else roll_lanes(cells, 1 - c)
                for b in range(3):
                    y = row + 1 - b
                    if 0 <= y < width_y:
                        first = (3 * b + c) * channels
                        right[x, first : first + channels, y * depth : (y + 1) * depth] = moved
    total = None
    for x in range(width_x):
        part = lax.dot_general(
            left[x * channels : (x + 3) * channels, :], right[x], NT, preferred_element_type=jnp.float32
        )
        total = part if total is None else total + part
    for pair in range(5):
        lanes = total[:, 2 * pair * channels : min(2 * pair + 2, 9) * channels]
        gram[pair, :, : lanes.shape[1]] = lanes
    half = channels // 2
    first_half = lax.broadcasted_iota(jnp.int32, (half, 2 * channels), 1) < channels
    for a in range(3):
        top = (2 - a) * channels
        for pair in range(5):
            low = gram[pair, pl.ds(top, half, stride=2), :]
            high = gram[pair, pl.ds(top + 1, half, stride=2), :]
            tap = 9 * a + 2 * pair
            ordered[tap * half : (tap + 1) * half, :] = jnp.where(first_half, low, pltpu.roll(high, channels, axis=1))
            if pair < 4:
                tap += 1
                ordered[tap * half : (tap + 1) * half, :] = jnp.where(
                    first_half, pltpu.roll(low, channels, axis=1), high
                )
    if len(out.shape) == 5:
        _, pairs, count_y, rows, _ = out.shape
        for part in range(2 * pairs * count_y):
            place = (part // count_y % 2, part // count_y // 2, part % count_y)
            out[place] = ordered[part * rows : (part + 1) * rows, :].astype(out.dtype)
    else:
        out[...] = ordered[...].astype(out.dtype)


def plane(slope, before, after, wide_x, row):
    if wide_x == 0:
        return before[0, row]
    if wide_x == slope.shape[0] + 1:
        return after[0, row]
    return slope[wide_x - 1, row]


def gather(parts):
    depth = parts[1].shape[1]
    return parts[1] + pltpu.roll(parts[0], depth - 1, axis=1) + pltpu.roll(parts[2], 1, axis=1)


def edge_kernel(slope, after, before, kernel, down, up, columns, weights):
    width_x, width_y, channels, depth = slope.shape
    for out, row, b in ((down, 0, 0), (up, width_y - 1, 2)):
        for wide_x in range(width_x + 2):
            columns[wide_x * channels : (wide_x + 1) * channels, :] = plane(slope, before, after, wide_x, row)
        for a in range(3):
            for c in range(3):
                weights[c, (2 - a) * channels : (3 - a) * channels, :] = kernel[9 * a + 3 * b + c]
        for x in range(width_x):
            cells = columns[x * channels : (x + 3) * channels, :]
            parts = [lax.dot_general(weights[c], cells, TN, preferred_element_type=jnp.float32) for c in range(3)]
            out[x] = gather(parts).astype(out.dtype)


def source_kernel(parity, slope, after, before, far, near, kernel, out, columns, weights, spread):
    width_x, width_y, channels, depth = slope.shape
    even = parity[0] == 0
    zeros = jnp.zeros((channels, depth), slope.dtype)
    for wide_x in range(width_x + 2):
        for row in range(-1, width_y + 1):
            cells = plane(slope, before, after, wide_x, row) if 0 <= row < width_y else zeros
            for b in range(3):
                y = row + b - 1
                if 0 <= y < width_y:
                    first = (3 * wide_x + b) * channels
                    columns[first : first + channels, y * depth : (y + 1) * depth] = cells
    for a in range(3):
        for b in range(3):
            for c in range(3):
                first = (3 * (2 - a) + b) * channels
                weights[c, first : first + channels, :] = kernel[9 * a + 3 * b + c]
    for x in range(width_x):
        cells = columns[3 * x * channels : 3 * (x + 3) * channels, :]
        for c in range(3):
            spread[c] = lax.dot_general(weights[c], cells, TN, preferred_element_type=jnp.float32)
        for y in range(width_y):
            lanes = slice(y * depth, (y + 1) * depth)
            total = gather([spread[c, :, lanes] for c in range(3)])
            if y == 0:
                total += jnp.where(even, far[x], near[x]).astype(jnp.float32)
            if y == width_y - 1:
                total += jnp.where(even, near[x], far[x]).astype(jnp.float32)
            out[x, y] = total.astype(out.dtype)


def on_device(source, preact, cotangent, kernel):
    channels, width_x, width_y, depth = source.shape
    devices = lax.axis_size("gx") * lax.axis_size("gy")
    cell_count = width_x * width_y * depth
    lines = 27 * channels * channels // 128
    pairs, count_y = lax.axis_size("gx") // 2, lax.axis_size("gy")
    share = (2, pairs, count_y, lines // devices, 128) if lines % devices == 0 else (lines, 128)
    parity = (lax.axis_index("gy") & 1).reshape(1)

    slope = jnp.where(preact > 0, cotangent, jnp.zeros_like(cotangent)).transpose(1, 2, 0, 3)
    src = source.transpose(1, 2, 0, 3)
    slope, src = lax.optimization_barrier((slope, src))
    before = to_next(slope[width_x - 1 :], "gx")
    after = to_previous(slope[:1], "gx")
    src_near, src_far = swapped(src[:, 0], src[:, -1], "gy")

    cost = pl.CostEstimate(
        flops=54 * channels * channels * cell_count, bytes_accessed=2 * 1024 * 1024, transcendentals=0
    )
    vmem = pl.BlockSpec(memory_space=pltpu.VMEM)
    smem = pl.BlockSpec(memory_space=pltpu.SMEM)
    partial = pl.pallas_call(
        weight_kernel,
        out_shape=jax.ShapeDtypeStruct(share, jnp.bfloat16),
        in_specs=[smem] + [vmem] * 6,
        out_specs=vmem,
        scratch_shapes=[
            pltpu.VMEM(((width_x + 2) * channels, width_y * depth), jnp.bfloat16),
            pltpu.VMEM((width_x, 9 * channels, width_y * depth), jnp.bfloat16),
            pltpu.VMEM((5, 3 * channels, 2 * channels), jnp.float32),
            pltpu.VMEM((lines, 128), jnp.float32),
        ],
        compiler_params=PARAMS,
        cost_estimate=cost,
        name="weight_grad",
    )(parity, slope, after, before, src, src_near, src_far)
    edge = jax.ShapeDtypeStruct((width_x, channels, depth), jnp.bfloat16)
    down, up = pl.pallas_call(
        edge_kernel,
        out_shape=(edge, edge),
        in_specs=[vmem] * 4,
        out_specs=(vmem, vmem),
        scratch_shapes=[
            pltpu.VMEM(((width_x + 2) * channels, depth), jnp.bfloat16),
            pltpu.VMEM((3, 3 * channels, channels), jnp.bfloat16),
        ],
        compiler_params=PARAMS,
        cost_estimate=pl.CostEstimate(
            flops=36 * channels * channels * width_x * depth, bytes_accessed=256 * 1024, transcendentals=0
        ),
        name="source_edges",
    )(slope, after, before, kernel)
    near, far = swapped(down, up, "gy")
    if len(share) == 2:
        partial = partial.reshape(pairs, 2, count_y, -1).transpose(1, 0, 2, 3)
    odd = lax.axis_index("gx") & 1 == 1
    swap = [(i, i ^ 1) for i in range(2 * pairs)]
    other = lax.ppermute(jnp.where(odd, partial[0], partial[1]), "gx", swap)
    own = jnp.where(odd, partial[1], partial[0])
    both = (own.astype(jnp.float32) + other.astype(jnp.float32)).astype(jnp.bfloat16)
    groups = [[(2 * i + c) * count_y + j for i in range(pairs) for j in range(count_y)] for c in range(2)]
    both = both.reshape(pairs * count_y, *both.shape[2:])
    shares = lax.all_to_all(both, ("gx", "gy"), 0, 0, axis_index_groups=groups, tiled=True)
    norm_scale = 1.0 / math.sqrt(cell_count * devices)
    grad_kernel = (jnp.sum(shares.astype(jnp.float32), axis=0) * norm_scale).reshape(-1)

    grad_source = pl.pallas_call(
        source_kernel,
        out_shape=jax.ShapeDtypeStruct(slope.shape, jnp.bfloat16),
        in_specs=[smem] + [vmem] * 6,
        out_specs=vmem,
        scratch_shapes=[
            pltpu.VMEM((3 * (width_x + 2) * channels, width_y * depth), jnp.bfloat16),
            pltpu.VMEM((3, 9 * channels, channels), jnp.bfloat16),
            pltpu.VMEM((3, channels, width_y * depth), jnp.float32),
        ],
        compiler_params=PARAMS,
        cost_estimate=cost,
        name="source_grad",
    )(parity, slope, after, before, far, near, kernel)
    return (grad_source.transpose(2, 0, 1, 3), grad_kernel)


def solution(mesh):
    placed = (P(None, "gx", "gy", None), P(None, "gx", "gy", None), P(None, "gx", "gy", None), P())
    return jax.shard_map(
        on_device,
        mesh=mesh,
        in_specs=placed,
        out_specs=(P(None, "gx", "gy", None), P(("gx", "gy"))),
        check_vma=False,
    )
```

```python
import math

import jax
import jax.numpy as jnp
from jax import lax
from jax.experimental import pallas as pl
from jax.experimental.pallas import tpu as pltpu
from jax.sharding import PartitionSpec as P

NT = (((1,), (1,)), ((), ()))
TN = (((0,), (0,)), ((), ()))
PARAMS = pltpu.CompilerParams(vmem_limit_bytes=32 * 1024 * 1024)


def to_next(block, axis):
    count = lax.axis_size(axis)
    return lax.ppermute(block, axis, [(i, (i + 1) % count) for i in range(count)])


def to_previous(block, axis):
    count = lax.axis_size(axis)
    return lax.ppermute(block, axis, [((i + 1) % count, i) for i in range(count)])


def swapped(first, last, axis):
    count = lax.axis_size(axis)
    even = lax.axis_index(axis) & 1 == 0
    near = [(i, i ^ 1) for i in range(count)]
    far = [(i, (i - 1) % count if i % 2 == 0 else (i + 1) % count) for i in range(count)]
    got_far = lax.ppermute(jnp.where(even, first, last), axis, far)
    got_near = lax.ppermute(jnp.where(even, last, first), axis, near)
    return got_near, got_far


def roll_lanes(block, step):
    return pltpu.roll(block.astype(jnp.float32), step % block.shape[-1], axis=1).astype(block.dtype)


def weight_kernel(parity, slope, after, before, source, near, far, out, left, right, gram, ordered):
    width_x, width_y, channels, depth = slope.shape
    even = parity[0] == 0
    for y in range(width_y):
        lanes = slice(y * depth, (y + 1) * depth)
        left[0:channels, lanes] = before[0, y]
        for x in range(width_x):
            left[(x + 1) * channels : (x + 2) * channels, lanes] = slope[x, y]
        left[(width_x + 1) * channels :, lanes] = after[0, y]
    for x in range(width_x):
        for row in range(-1, width_y + 1):
            if row < 0:
                cells = jnp.where(even, far[x], near[x])
            elif row == width_y:
                cells = jnp.where(even, near[x], far[x])
            else:
                cells = source[x, row]
            for c in range(3):
                moved = cells if c == 1 else roll_lanes(cells, 1 - c)
                for b in range(3):
                    y = row + 1 - b
                    if 0 <= y < width_y:
                        first = (3 * b + c) * channels
                        right[x, first : first + channels, y * depth : (y + 1) * depth] = moved
    total = None
    for x in range(width_x):
        part = lax.dot_general(
            left[x * channels : (x + 3) * channels, :], right[x], NT, preferred_element_type=jnp.float32
        )
        total = part if total is None else total + part
    for pair in range(5):
        lanes = total[:, 2 * pair * channels : min(2 * pair + 2, 9) * channels]
        gram[pair, :, : lanes.shape[1]] = lanes
    half = channels // 2
    first_half = lax.broadcasted_iota(jnp.int32, (half, 2 * channels), 1) < channels
    for a in range(3):
        top = (2 - a) * channels
        for pair in range(5):
            low = gram[pair, pl.ds(top, half, stride=2), :]
            high = gram[pair, pl.ds(top + 1, half, stride=2), :]
            tap = 9 * a + 2 * pair
            ordered[tap * half : (tap + 1) * half, :] = jnp.where(first_half, low, pltpu.roll(high, channels, axis=1))
            if pair < 4:
                tap += 1
                ordered[tap * half : (tap + 1) * half, :] = jnp.where(
                    first_half, pltpu.roll(low, channels, axis=1), high
                )
    if len(out.shape) == 5:
        _, pairs, count_y, rows, _ = out.shape
        for part in range(2 * pairs * count_y):
            place = (part // count_y % 2, part // count_y // 2, part % count_y)
            out[place] = ordered[part * rows : (part + 1) * rows, :].astype(out.dtype)
    else:
        out[...] = ordered[...].astype(out.dtype)


def plane(slope, before, after, wide_x, row):
    if wide_x == 0:
        return before[0, row]
    if wide_x == slope.shape[0] + 1:
        return after[0, row]
    return slope[wide_x - 1, row]


def gather(parts):
    depth = parts[1].shape[1]
    return parts[1] + pltpu.roll(parts[0], depth - 1, axis=1) + pltpu.roll(parts[2], 1, axis=1)


def edge_kernel(slope, after, before, kernel, down, up, columns, weights):
    width_x, width_y, channels, depth = slope.shape
    for out, row, b in ((down, 0, 0), (up, width_y - 1, 2)):
        for wide_x in range(width_x + 2):
            columns[wide_x * channels : (wide_x + 1) * channels, :] = plane(slope, before, after, wide_x, row)
        for a in range(3):
            for c in range(3):
                weights[c, (2 - a) * channels : (3 - a) * channels, :] = kernel[9 * a + 3 * b + c]
        for x in range(width_x):
            cells = columns[x * channels : (x + 3) * channels, :]
            parts = [lax.dot_general(weights[c], cells, TN, preferred_element_type=jnp.float32) for c in range(3)]
            out[x] = gather(parts).astype(out.dtype)


def source_kernel(parity, slope, after, before, far, near, kernel, out, columns, weights, spread):
    width_x, width_y, channels, depth = slope.shape
    even = parity[0] == 0
    zeros = jnp.zeros((channels, depth), slope.dtype)
    for wide_x in range(width_x + 2):
        for row in range(-1, width_y + 1):
            cells = plane(slope, before, after, wide_x, row) if 0 <= row < width_y else zeros
            for b in range(3):
                y = row + b - 1
                if 0 <= y < width_y:
                    first = (3 * wide_x + b) * channels
                    columns[first : first + channels, y * depth : (y + 1) * depth] = cells
    for a in range(3):
        for b in range(3):
            for c in range(3):
                first = (3 * (2 - a) + b) * channels
                weights[c, first : first + channels, :] = kernel[9 * a + 3 * b + c]
    for x in range(width_x):
        cells = columns[3 * x * channels : 3 * (x + 3) * channels, :]
        for c in range(3):
            spread[c] = lax.dot_general(weights[c], cells, TN, preferred_element_type=jnp.float32)
        for y in range(width_y):
            lanes = slice(y * depth, (y + 1) * depth)
            total = gather([spread[c, :, lanes] for c in range(3)])
            if y == 0:
                total += jnp.where(even, far[x], near[x]).astype(jnp.float32)
            if y == width_y - 1:
                total += jnp.where(even, near[x], far[x]).astype(jnp.float32)
            out[x, y] = total.astype(out.dtype)


def on_device(source, preact, cotangent, kernel):
    channels, width_x, width_y, depth = source.shape
    devices = lax.axis_size("gx") * lax.axis_size("gy")
    cell_count = width_x * width_y * depth
    lines = 27 * channels * channels // 128
    pairs, count_y = lax.axis_size("gx") // 2, lax.axis_size("gy")
    share = (2, pairs, count_y, lines // devices, 128) if lines % devices == 0 else (lines, 128)
    parity = (lax.axis_index("gy") & 1).reshape(1)

    slope = jnp.where(preact > 0, cotangent, jnp.zeros_like(cotangent)).transpose(1, 2, 0, 3)
    src = source.transpose(1, 2, 0, 3)
    slope, src = lax.optimization_barrier((slope, src))
    before = to_next(slope[width_x - 1 :], "gx")
    after = to_previous(slope[:1], "gx")
    src_near, src_far = swapped(src[:, 0], src[:, -1], "gy")

    cost = pl.CostEstimate(
        flops=54 * channels * channels * cell_count, bytes_accessed=2 * 1024 * 1024, transcendentals=0
    )
    vmem = pl.BlockSpec(memory_space=pltpu.VMEM)
    smem = pl.BlockSpec(memory_space=pltpu.SMEM)
    partial = pl.pallas_call(
        weight_kernel,
        out_shape=jax.ShapeDtypeStruct(share, jnp.bfloat16),
        in_specs=[smem] + [vmem] * 6,
        out_specs=vmem,
        scratch_shapes=[
            pltpu.VMEM(((width_x + 2) * channels, width_y * depth), jnp.bfloat16),
            pltpu.VMEM((width_x, 9 * channels, width_y * depth), jnp.bfloat16),
            pltpu.VMEM((5, 3 * channels, 2 * channels), jnp.float32),
            pltpu.VMEM((lines, 128), jnp.float32),
        ],
        compiler_params=PARAMS,
        cost_estimate=cost,
        name="weight_grad",
    )(parity, slope, after, before, src, src_near, src_far)
    edge = jax.ShapeDtypeStruct((width_x, channels, depth), jnp.bfloat16)
    down, up = pl.pallas_call(
        edge_kernel,
        out_shape=(edge, edge),
        in_specs=[vmem] * 4,
        out_specs=(vmem, vmem),
        scratch_shapes=[
            pltpu.VMEM(((width_x + 2) * channels, depth), jnp.bfloat16),
            pltpu.VMEM((3, 3 * channels, channels), jnp.bfloat16),
        ],
        compiler_params=PARAMS,
        cost_estimate=pl.CostEstimate(
            flops=36 * channels * channels * width_x * depth, bytes_accessed=256 * 1024, transcendentals=0
        ),
        name="source_edges",
    )(slope, after, before, kernel)
    near, far = swapped(down, up, "gy")
    if len(share) == 2:
        partial = partial.reshape(pairs, 2, count_y, -1).transpose(1, 0, 2, 3)
    odd = lax.axis_index("gx") & 1 == 1
    swap = [(i, i ^ 1) for i in range(2 * pairs)]
    other = lax.ppermute(jnp.where(odd, partial[0], partial[1]), "gx", swap)
    own = jnp.where(odd, partial[1], partial[0])
    both = (own.astype(jnp.float32) + other.astype(jnp.float32)).astype(jnp.bfloat16)
    groups = [[(2 * i + c) * count_y + j for i in range(pairs) for j in range(count_y)] for c in range(2)]
    both = both.reshape(pairs * count_y, *both.shape[2:])
    shares = lax.all_to_all(both, ("gx", "gy"), 0, 0, axis_index_groups=groups, tiled=True)
    norm_scale = 1.0 / math.sqrt(cell_count * devices)
    grad_kernel = (jnp.sum(shares.astype(jnp.float32), axis=0) * norm_scale).reshape(-1)

    grad_source = pl.pallas_call(
        source_kernel,
        out_shape=jax.ShapeDtypeStruct(slope.shape, jnp.bfloat16),
        in_specs=[smem] + [vmem] * 6,
        out_specs=vmem,
        scratch_shapes=[
            pltpu.VMEM((3 * (width_x + 2) * channels, width_y * depth), jnp.bfloat16),
            pltpu.VMEM((3, 9 * channels, channels), jnp.bfloat16),
            pltpu.VMEM((3, channels, width_y * depth), jnp.float32),
        ],
        compiler_params=PARAMS,
        cost_estimate=pl.CostEstimate(
            flops=5400 * channels * channels * cell_count, bytes_accessed=2 * 1024 * 1024, transcendentals=0
        ),
        name="source_grad",
    )(parity, slope, after, before, far, near, kernel)
    return (grad_source.transpose(2, 0, 1, 3), grad_kernel)


def solution(mesh):
    placed = (P(None, "gx", "gy", None), P(None, "gx", "gy", None), P(None, "gx", "gy", None), P())
    return jax.shard_map(
        on_device,
        mesh=mesh,
        in_specs=placed,
        out_specs=(P(None, "gx", "gy", None), P(("gx", "gy"))),
        check_vma=False,
    )
```

```python
import math

import jax
import jax.numpy as jnp
from jax import lax
from jax.experimental import pallas as pl
from jax.experimental.pallas import tpu as pltpu
from jax.sharding import PartitionSpec as P

NT = (((1,), (1,)), ((), ()))
TN = (((0,), (0,)), ((), ()))
PARAMS = pltpu.CompilerParams(vmem_limit_bytes=32 * 1024 * 1024)


def to_next(block, axis):
    count = lax.axis_size(axis)
    return lax.ppermute(block, axis, [(i, (i + 1) % count) for i in range(count)])


def to_previous(block, axis):
    count = lax.axis_size(axis)
    return lax.ppermute(block, axis, [((i + 1) % count, i) for i in range(count)])


def swapped(first, last, axis):
    count = lax.axis_size(axis)
    even = lax.axis_index(axis) & 1 == 0
    near = [(i, i ^ 1) for i in range(count)]
    far = [(i, (i - 1) % count if i % 2 == 0 else (i + 1) % count) for i in range(count)]
    got_far = lax.ppermute(jnp.where(even, first, last), axis, far)
    got_near = lax.ppermute(jnp.where(even, last, first), axis, near)
    return got_near, got_far


def roll_lanes(block, step):
    if step == 0:
        return block
    return pltpu.roll(block.astype(jnp.float32), step % block.shape[-1], axis=1).astype(block.dtype)


def plane(slope, before, after, wide_x, row):
    if wide_x == 0:
        return before[0, row]
    if wide_x == slope.shape[0] + 1:
        return after[0, row]
    return slope[wide_x - 1, row]


def gather(parts):
    depth = parts[1].shape[1]
    return parts[1] + pltpu.roll(parts[0], depth - 1, axis=1) + pltpu.roll(parts[2], 1, axis=1)


def inner_kernel(slope, before, after, source, out, left, right):
    width_x, width_y, channels, depth = slope.shape
    for wide_x in range(width_x + 2):
        for y in range(width_y):
            left[wide_x * channels : (wide_x + 1) * channels, y * depth : (y + 1) * depth] = plane(
                slope, before, after, wide_x, y
            )
    zeros = jnp.zeros((3 * channels, depth), source.dtype)
    for x in range(width_x):
        right[x, 0 : 3 * channels, 0:depth] = zeros
        right[x, 6 * channels :, (width_y - 1) * depth :] = zeros
        for row in range(width_y):
            for c in range(3):
                moved = roll_lanes(source[x, row], 1 - c)
                for b in range(3):
                    y = row + 1 - b
                    if 0 <= y < width_y:
                        first = (3 * b + c) * channels
                        right[x, first : first + channels, y * depth : (y + 1) * depth] = moved
    total = None
    for x in range(width_x):
        part = lax.dot_general(
            left[x * channels : (x + 3) * channels, :], right[x], NT, preferred_element_type=jnp.float32
        )
        total = part if total is None else total + part
    out[...] = total


def weight_kernel(parity, inner, slope, before, after, far, near, out, left, right, gram, ordered):
    width_x, width_y, channels, depth = slope.shape
    even = parity[0] == 0
    sides = []
    for row in (0, width_y - 1):
        total = None
        for wide_x in range(width_x + 2):
            left[wide_x * channels : (wide_x + 1) * channels, :] = plane(slope, before, after, wide_x, row)
        for x in range(width_x):
            cells = jnp.where(even, far[x], near[x]) if row == 0 else jnp.where(even, near[x], far[x])
            for c in range(3):
                right[c * channels : (c + 1) * channels, :] = roll_lanes(cells, 1 - c)
            part = lax.dot_general(
                left[x * channels : (x + 3) * channels, :], right[...], NT, preferred_element_type=jnp.float32
            )
            total = part if total is None else total + part
        sides.append(total)
    total = jnp.concatenate(
        [
            inner[:, : 3 * channels] + sides[0],
            inner[:, 3 * channels : 6 * channels],
            inner[:, 6 * channels :] + sides[1],
        ],
        axis=1,
    )
    for pair in range(5):
        lanes = total[:, 2 * pair * channels : min(2 * pair + 2, 9) * channels]
        gram[pair, :, : lanes.shape[1]] = lanes
    half = channels // 2
    first_half = lax.broadcasted_iota(jnp.int32, (half, 2 * channels), 1) < channels
    for a in range(3):
        top = (2 - a) * channels
        for pair in range(5):
            low = gram[pair, pl.ds(top, half, stride=2), :]
            high = gram[pair, pl.ds(top + 1, half, stride=2), :]
            tap = 9 * a + 2 * pair
            ordered[tap * half : (tap + 1) * half, :] = jnp.where(first_half, low, pltpu.roll(high, channels, axis=1))
            if pair < 4:
                tap += 1
                ordered[tap * half : (tap + 1) * half, :] = jnp.where(
                    first_half, pltpu.roll(low, channels, axis=1), high
                )
    if len(out.shape) == 5:
        _, pairs, count_y, rows, _ = out.shape
        for part in range(2 * pairs * count_y):
            place = (part // count_y % 2, part // count_y // 2, part % count_y)
            out[place] = ordered[part * rows : (part + 1) * rows, :].astype(out.dtype)
    else:
        out[...] = ordered[...].astype(out.dtype)


def edge_kernel(slope, before, after, kernel, down, up, columns, weights):
    width_x, width_y, channels, depth = slope.shape
    for out, row, b in ((down, 0, 0), (up, width_y - 1, 2)):
        for wide_x in range(width_x + 2):
            columns[wide_x * channels : (wide_x + 1) * channels, :] = plane(slope, before, after, wide_x, row)
        for a in range(3):
            for c in range(3):
                weights[c, (2 - a) * channels : (3 - a) * channels, :] = kernel[9 * a + 3 * b + c]
        for x in range(width_x):
            cells = columns[x * channels : (x + 3) * channels, :]
            parts = [lax.dot_general(weights[c], cells, TN, preferred_element_type=jnp.float32) for c in range(3)]
            out[x] = gather(parts).astype(out.dtype)


def source_kernel(parity, slope, before, after, far, near, kernel, out, columns, weights, spread):
    width_x, width_y, channels, depth = slope.shape
    even = parity[0] == 0
    zeros = jnp.zeros((channels, depth), slope.dtype)
    for wide_x in range(width_x + 2):
        for row in range(-1, width_y + 1):
            cells = plane(slope, before, after, wide_x, row) if 0 <= row < width_y else zeros
            for b in range(3):
                y = row + b - 1
                if 0 <= y < width_y:
                    first = (3 * wide_x + b) * channels
                    columns[first : first + channels, y * depth : (y + 1) * depth] = cells
    for a in range(3):
        for b in range(3):
            for c in range(3):
                first = (3 * (2 - a) + b) * channels
                weights[c, first : first + channels, :] = kernel[9 * a + 3 * b + c]
    for x in range(width_x):
        cells = columns[3 * x * channels : 3 * (x + 3) * channels, :]
        for c in range(3):
            spread[c] = lax.dot_general(weights[c], cells, TN, preferred_element_type=jnp.float32)
        for y in range(width_y):
            lanes = slice(y * depth, (y + 1) * depth)
            total = gather([spread[c, :, lanes] for c in range(3)])
            if y == 0:
                total += jnp.where(even, far[x], near[x]).astype(jnp.float32)
            if y == width_y - 1:
                total += jnp.where(even, near[x], far[x]).astype(jnp.float32)
            out[x, y] = total.astype(out.dtype)


def on_device(source, preact, cotangent, kernel):
    channels, width_x, width_y, depth = source.shape
    devices = lax.axis_size("gx") * lax.axis_size("gy")
    cell_count = width_x * width_y * depth
    lines = 27 * channels * channels // 128
    pairs, count_y = lax.axis_size("gx") // 2, lax.axis_size("gy")
    share = (2, pairs, count_y, lines // devices, 128) if lines % devices == 0 else (lines, 128)
    parity = (lax.axis_index("gy") & 1).reshape(1)

    slope = jnp.where(preact > 0, cotangent, jnp.zeros_like(cotangent)).transpose(1, 2, 0, 3)
    src = source.transpose(1, 2, 0, 3)
    slope, src = lax.optimization_barrier((slope, src))
    before = to_next(slope[width_x - 1 :], "gx")
    after = to_previous(slope[:1], "gx")
    src_near, src_far = swapped(src[:, 0], src[:, -1], "gy")

    cost = pl.CostEstimate(
        flops=54 * channels * channels * cell_count, bytes_accessed=2 * 1024 * 1024, transcendentals=0
    )
    vmem = pl.BlockSpec(memory_space=pltpu.VMEM)
    smem = pl.BlockSpec(memory_space=pltpu.SMEM)
    inner = pl.pallas_call(
        inner_kernel,
        out_shape=jax.ShapeDtypeStruct((3 * channels, 9 * channels), jnp.float32),
        in_specs=[vmem] * 4,
        out_specs=vmem,
        scratch_shapes=[
            pltpu.VMEM(((width_x + 2) * channels, width_y * depth), jnp.bfloat16),
            pltpu.VMEM((width_x, 9 * channels, width_y * depth), jnp.bfloat16),
        ],
        compiler_params=PARAMS,
        cost_estimate=cost,
        name="weight_inner",
    )(slope, before, after, src)
    partial = pl.pallas_call(
        weight_kernel,
        out_shape=jax.ShapeDtypeStruct(share, jnp.bfloat16),
        in_specs=[smem] + [vmem] * 6,
        out_specs=vmem,
        scratch_shapes=[
            pltpu.VMEM(((width_x + 2) * channels, depth), jnp.bfloat16),
            pltpu.VMEM((3 * channels, depth), jnp.bfloat16),
            pltpu.VMEM((5, 3 * channels, 2 * channels), jnp.float32),
            pltpu.VMEM((lines, 128), jnp.float32),
        ],
        compiler_params=PARAMS,
        cost_estimate=cost,
        name="weight_grad",
    )(parity, inner, slope, before, after, src_far, src_near)
    edge = jax.ShapeDtypeStruct((width_x, channels, depth), jnp.bfloat16)
    down, up = pl.pallas_call(
        edge_kernel,
        out_shape=(edge, edge),
        in_specs=[vmem] * 4,
        out_specs=(vmem, vmem),
        scratch_shapes=[
            pltpu.VMEM(((width_x + 2) * channels, depth), jnp.bfloat16),
            pltpu.VMEM((3, 3 * channels, channels), jnp.bfloat16),
        ],
        compiler_params=PARAMS,
        cost_estimate=pl.CostEstimate(
            flops=36 * channels * channels * width_x * depth, bytes_accessed=256 * 1024, transcendentals=0
        ),
        name="source_edges",
    )(slope, before, after, kernel)
    near, far = swapped(down, up, "gy")
    if len(share) == 2:
        partial = partial.reshape(pairs, 2, count_y, -1).transpose(1, 0, 2, 3)
    odd = lax.axis_index("gx") & 1 == 1
    swap = [(i, i ^ 1) for i in range(2 * pairs)]
    other = lax.ppermute(jnp.where(odd, partial[0], partial[1]), "gx", swap)
    own = jnp.where(odd, partial[1], partial[0])
    both = (own.astype(jnp.float32) + other.astype(jnp.float32)).astype(jnp.bfloat16)
    groups = [[(2 * i + c) * count_y + j for i in range(pairs) for j in range(count_y)] for c in range(2)]
    both = both.reshape(pairs * count_y, *both.shape[2:])
    shares = lax.all_to_all(both, ("gx", "gy"), 0, 0, axis_index_groups=groups, tiled=True)
    norm_scale = 1.0 / math.sqrt(cell_count * devices)
    grad_kernel = (jnp.sum(shares.astype(jnp.float32), axis=0) * norm_scale).reshape(-1)

    grad_source = pl.pallas_call(
        source_kernel,
        out_shape=jax.ShapeDtypeStruct(slope.shape, jnp.bfloat16),
        in_specs=[smem] + [vmem] * 6,
        out_specs=vmem,
        scratch_shapes=[
            pltpu.VMEM((3 * (width_x + 2) * channels, width_y * depth), jnp.bfloat16),
            pltpu.VMEM((3, 9 * channels, channels), jnp.bfloat16),
            pltpu.VMEM((3, channels, width_y * depth), jnp.float32),
        ],
        compiler_params=PARAMS,
        cost_estimate=pl.CostEstimate(
            flops=5400 * channels * channels * cell_count, bytes_accessed=2 * 1024 * 1024, transcendentals=0
        ),
        name="source_grad",
    )(parity, slope, before, after, far, near, kernel)
    return (grad_source.transpose(2, 0, 1, 3), grad_kernel)


def solution(mesh):
    placed = (P(None, "gx", "gy", None), P(None, "gx", "gy", None), P(None, "gx", "gy", None), P())
    return jax.shard_map(
        on_device,
        mesh=mesh,
        in_specs=placed,
        out_specs=(P(None, "gx", "gy", None), P(("gx", "gy"))),
        check_vma=False,
    )
```

```python
import math

import jax
import jax.numpy as jnp
from jax import lax
from jax.experimental import pallas as pl
from jax.experimental.pallas import tpu as pltpu
from jax.sharding import PartitionSpec as P

NT = (((1,), (1,)), ((), ()))
TN = (((0,), (0,)), ((), ()))
PARAMS = pltpu.CompilerParams(vmem_limit_bytes=32 * 1024 * 1024)


def to_next(block, axis):
    count = lax.axis_size(axis)
    return lax.ppermute(block, axis, [(i, (i + 1) % count) for i in range(count)])


def to_previous(block, axis):
    count = lax.axis_size(axis)
    return lax.ppermute(block, axis, [((i + 1) % count, i) for i in range(count)])


def swapped(first, last, axis):
    count = lax.axis_size(axis)
    even = lax.axis_index(axis) & 1 == 0
    near = [(i, i ^ 1) for i in range(count)]
    far = [(i, (i - 1) % count if i % 2 == 0 else (i + 1) % count) for i in range(count)]
    got_far = lax.ppermute(jnp.where(even, first, last), axis, far)
    got_near = lax.ppermute(jnp.where(even, last, first), axis, near)
    return got_near, got_far


def roll_lanes(block, step):
    if step == 0:
        return block
    return pltpu.roll(block.astype(jnp.float32), step % block.shape[-1], axis=1).astype(block.dtype)


def plane(slope, before, after, wide_x, row):
    if wide_x == 0:
        return before[0, row]
    if wide_x == slope.shape[0] + 1:
        return after[0, row]
    return slope[wide_x - 1, row]


def gather(parts):
    depth = parts[1].shape[1]
    return parts[1] + pltpu.roll(parts[0], depth - 1, axis=1) + pltpu.roll(parts[2], 1, axis=1)


def inner_kernel(slope, after, before, source, kernel, out, down, up, left, right, columns, weights):
    width_x, width_y, channels, depth = slope.shape
    for wide_x in range(width_x + 2):
        for y in range(width_y):
            left[wide_x * channels : (wide_x + 1) * channels, y * depth : (y + 1) * depth] = plane(
                slope, before, after, wide_x, y
            )
    zeros = jnp.zeros((3 * channels, depth), source.dtype)
    for x in range(width_x):
        right[x, 0 : 3 * channels, 0:depth] = zeros
        right[x, 6 * channels :, (width_y - 1) * depth :] = zeros
        for row in range(width_y):
            for c in range(3):
                moved = roll_lanes(source[x, row], 1 - c)
                for b in range(3):
                    y = row + 1 - b
                    if 0 <= y < width_y:
                        first = (3 * b + c) * channels
                        right[x, first : first + channels, y * depth : (y + 1) * depth] = moved
    total = None
    for x in range(width_x):
        part = lax.dot_general(
            left[x * channels : (x + 3) * channels, :], right[x], NT, preferred_element_type=jnp.float32
        )
        total = part if total is None else total + part
    out[...] = total
    edge_rows(slope, before, after, kernel, 0, 0, down, columns, weights)
    edge_rows(slope, before, after, kernel, width_y - 1, 2, up, columns, weights)


def weight_kernel(parity, inner, slope, after, before, near, far, out, left, right, gram, ordered):
    width_x, width_y, channels, depth = slope.shape
    even = parity[0] == 0
    sides = []
    for row in (0, width_y - 1):
        total = None
        for wide_x in range(width_x + 2):
            left[wide_x * channels : (wide_x + 1) * channels, :] = plane(slope, before, after, wide_x, row)
        for x in range(width_x):
            cells = jnp.where(even, far[x], near[x]) if row == 0 else jnp.where(even, near[x], far[x])
            for c in range(3):
                right[c * channels : (c + 1) * channels, :] = roll_lanes(cells, 1 - c)
            part = lax.dot_general(
                left[x * channels : (x + 3) * channels, :], right[...], NT, preferred_element_type=jnp.float32
            )
            total = part if total is None else total + part
        sides.append(total)
    total = jnp.concatenate(
        [
            inner[:, : 3 * channels] + sides[0],
            inner[:, 3 * channels : 6 * channels],
            inner[:, 6 * channels :] + sides[1],
        ],
        axis=1,
    )
    for pair in range(5):
        lanes = total[:, 2 * pair * channels : min(2 * pair + 2, 9) * channels]
        gram[pair, :, : lanes.shape[1]] = lanes
    half = channels // 2
    first_half = lax.broadcasted_iota(jnp.int32, (half, 2 * channels), 1) < channels
    for a in range(3):
        top = (2 - a) * channels
        for pair in range(5):
            low = gram[pair, pl.ds(top, half, stride=2), :]
            high = gram[pair, pl.ds(top + 1, half, stride=2), :]
            tap = 9 * a + 2 * pair
            ordered[tap * half : (tap + 1) * half, :] = jnp.where(first_half, low, pltpu.roll(high, channels, axis=1))
            if pair < 4:
                tap += 1
                ordered[tap * half : (tap + 1) * half, :] = jnp.where(
                    first_half, pltpu.roll(low, channels, axis=1), high
                )
    if len(out.shape) == 5:
        _, pairs, count_y, rows, _ = out.shape
        for part in range(2 * pairs * count_y):
            place = (part // count_y % 2, part // count_y // 2, part % count_y)
            out[place] = ordered[part * rows : (part + 1) * rows, :].astype(out.dtype)
    else:
        out[...] = ordered[...].astype(out.dtype)


def edge_rows(slope, before, after, kernel, row, b, out, columns, weights):
    width_x, width_y, channels, depth = slope.shape
    for wide_x in range(width_x + 2):
        columns[wide_x * channels : (wide_x + 1) * channels, :] = plane(slope, before, after, wide_x, row)
    for a in range(3):
        for c in range(3):
            weights[c, (2 - a) * channels : (3 - a) * channels, :] = kernel[9 * a + 3 * b + c]
    for x in range(width_x):
        cells = columns[x * channels : (x + 3) * channels, :]
        parts = [lax.dot_general(weights[c], cells, TN, preferred_element_type=jnp.float32) for c in range(3)]
        out[x] = gather(parts).astype(out.dtype)


def inner_kernel(slope, after, before, source, kernel, out, down, up, left, right, columns, weights):
    width_x, width_y, channels, depth = slope.shape
    for wide_x in range(width_x + 2):
        for y in range(width_y):
            left[wide_x * channels : (wide_x + 1) * channels, y * depth : (y + 1) * depth] = plane(
                slope, before, after, wide_x, y
            )
    zeros = jnp.zeros((3 * channels, depth), source.dtype)
    for x in range(width_x):
        right[x, 0 : 3 * channels, 0:depth] = zeros
        right[x, 6 * channels :, (width_y - 1) * depth :] = zeros
        for row in range(width_y):
            for c in range(3):
                moved = roll_lanes(source[x, row], 1 - c)
                for b in range(3):
                    y = row + 1 - b
                    if 0 <= y < width_y:
                        first = (3 * b + c) * channels
                        right[x, first : first + channels, y * depth : (y + 1) * depth] = moved
    total = None
    for x in range(width_x):
        part = lax.dot_general(
            left[x * channels : (x + 3) * channels, :], right[x], NT, preferred_element_type=jnp.float32
        )
        total = part if total is None else total + part
    out[...] = total
    edge_rows(slope, before, after, kernel, 0, 0, down, columns, weights)
    edge_rows(slope, before, after, kernel, width_y - 1, 2, up, columns, weights)


def weight_kernel(parity, inner, slope, after, before, near, far, out, left, right, gram, ordered):
    width_x, width_y, channels, depth = slope.shape
    even = parity[0] == 0
    sides = []
    for row in (0, width_y - 1):
        total = None
        for wide_x in range(width_x + 2):
            left[wide_x * channels : (wide_x + 1) * channels, :] = plane(slope, before, after, wide_x, row)
        for x in range(width_x):
            cells = jnp.where(even, far[x], near[x]) if row == 0 else jnp.where(even, near[x], far[x])
            for c in range(3):
                right[c * channels : (c + 1) * channels, :] = roll_lanes(cells, 1 - c)
            part = lax.dot_general(
                left[x * channels : (x + 3) * channels, :], right[...], NT, preferred_element_type=jnp.float32
            )
            total = part if total is None else total + part
        sides.append(total)
    total = jnp.concatenate(
        [
            inner[:, : 3 * channels] + sides[0],
            inner[:, 3 * channels : 6 * channels],
            inner[:, 6 * channels :] + sides[1],
        ],
        axis=1,
    )
    for pair in range(5):
        lanes = total[:, 2 * pair * channels : min(2 * pair + 2, 9) * channels]
        gram[pair, :, : lanes.shape[1]] = lanes
    half = channels // 2
    first_half = lax.broadcasted_iota(jnp.int32, (half, 2 * channels), 1) < channels
    for a in range(3):
        top = (2 - a) * channels
        for pair in range(5):
            low = gram[pair, pl.ds(top, half, stride=2), :]
            high = gram[pair, pl.ds(top + 1, half, stride=2), :]
            tap = 9 * a + 2 * pair
            ordered[tap * half : (tap + 1) * half, :] = jnp.where(first_half, low, pltpu.roll(high, channels, axis=1))
            if pair < 4:
                tap += 1
                ordered[tap * half : (tap + 1) * half, :] = jnp.where(
                    first_half, pltpu.roll(low, channels, axis=1), high
                )
    if len(out.shape) == 5:
        _, pairs, count_y, rows, _ = out.shape
        for part in range(2 * pairs * count_y):
            place = (part // count_y % 2, part // count_y // 2, part % count_y)
            out[place] = ordered[part * rows : (part + 1) * rows, :].astype(out.dtype)
    else:
        out[...] = ordered[...].astype(out.dtype)


def edge_kernel(slope, before, after, kernel, down, up, columns, weights):
    width_x, width_y, channels, depth = slope.shape
    for out, row, b in ((down, 0, 0), (up, width_y - 1, 2)):
        for wide_x in range(width_x + 2):
            columns[wide_x * channels : (wide_x + 1) * channels, :] = plane(slope, before, after, wide_x, row)
        for a in range(3):
            for c in range(3):
                weights[c, (2 - a) * channels : (3 - a) * channels, :] = kernel[9 * a + 3 * b + c]
        for x in range(width_x):
            cells = columns[x * channels : (x + 3) * channels, :]
            parts = [lax.dot_general(weights[c], cells, TN, preferred_element_type=jnp.float32) for c in range(3)]
            out[x] = gather(parts).astype(out.dtype)


def source_kernel(parity, slope, after, before, near, far, kernel, out, columns, weights, spread):
    width_x, width_y, channels, depth = slope.shape
    even = parity[0] == 0
    zeros = jnp.zeros((channels, depth), slope.dtype)
    for wide_x in range(width_x + 2):
        for row in range(-1, width_y + 1):
            cells = plane(slope, before, after, wide_x, row) if 0 <= row < width_y else zeros
            for b in range(3):
                y = row + b - 1
                if 0 <= y < width_y:
                    first = (3 * wide_x + b) * channels
                    columns[first : first + channels, y * depth : (y + 1) * depth] = cells
    for a in range(3):
        for b in range(3):
            for c in range(3):
                first = (3 * (2 - a) + b) * channels
                weights[c, first : first + channels, :] = kernel[9 * a + 3 * b + c]
    for x in range(width_x):
        cells = columns[3 * x * channels : 3 * (x + 3) * channels, :]
        for c in range(3):
            spread[c] = lax.dot_general(weights[c], cells, TN, preferred_element_type=jnp.float32)
        for y in range(width_y):
            lanes = slice(y * depth, (y + 1) * depth)
            total = gather([spread[c, :, lanes] for c in range(3)])
            if y == 0:
                total += jnp.where(even, far[x], near[x]).astype(jnp.float32)
            if y == width_y - 1:
                total += jnp.where(even, near[x], far[x]).astype(jnp.float32)
            out[x, y] = total.astype(out.dtype)


def on_device(source, preact, cotangent, kernel):
    channels, width_x, width_y, depth = source.shape
    devices = lax.axis_size("gx") * lax.axis_size("gy")
    cell_count = width_x * width_y * depth
    lines = 27 * channels * channels // 128
    pairs, count_y = lax.axis_size("gx") // 2, lax.axis_size("gy")
    share = (2, pairs, count_y, lines // devices, 128) if lines % devices == 0 else (lines, 128)
    parity = (lax.axis_index("gy") & 1).reshape(1)

    slope = jnp.where(preact > 0, cotangent, jnp.zeros_like(cotangent)).transpose(1, 2, 0, 3)
    src = source.transpose(1, 2, 0, 3)
    slope, src = lax.optimization_barrier((slope, src))
    before = to_next(slope[width_x - 1 :], "gx")
    after = to_previous(slope[:1], "gx")
    src_near, src_far = swapped(src[:, 0], src[:, -1], "gy")

    cost = pl.CostEstimate(
        flops=54 * channels * channels * cell_count, bytes_accessed=2 * 1024 * 1024, transcendentals=0
    )
    vmem = pl.BlockSpec(memory_space=pltpu.VMEM)
    smem = pl.BlockSpec(memory_space=pltpu.SMEM)
    edge = jax.ShapeDtypeStruct((width_x, channels, depth), jnp.bfloat16)
    inner, down, up = pl.pallas_call(
        inner_kernel,
        out_shape=(jax.ShapeDtypeStruct((3 * channels, 9 * channels), jnp.float32), edge, edge),
        in_specs=[vmem] * 5,
        out_specs=(vmem, vmem, vmem),
        scratch_shapes=[
            pltpu.VMEM(((width_x + 2) * channels, width_y * depth), jnp.bfloat16),
            pltpu.VMEM((width_x, 9 * channels, width_y * depth), jnp.bfloat16),
            pltpu.VMEM(((width_x + 2) * channels, depth), jnp.bfloat16),
            pltpu.VMEM((3, 3 * channels, channels), jnp.bfloat16),
        ],
        compiler_params=PARAMS,
        cost_estimate=cost,
        name="weight_inner",
    )(slope, after, before, src, kernel)
    partial = pl.pallas_call(
        weight_kernel,
        out_shape=jax.ShapeDtypeStruct(share, jnp.bfloat16),
        in_specs=[smem] + [vmem] * 6,
        out_specs=vmem,
        scratch_shapes=[
            pltpu.VMEM(((width_x + 2) * channels, depth), jnp.bfloat16),
            pltpu.VMEM((3 * channels, depth), jnp.bfloat16),
            pltpu.VMEM((5, 3 * channels, 2 * channels), jnp.float32),
            pltpu.VMEM((lines, 128), jnp.float32),
        ],
        compiler_params=PARAMS,
        cost_estimate=cost,
        name="weight_grad",
    )(parity, inner, slope, after, before, src_near, src_far)
    near, far = swapped(down, up, "gy")
    if len(share) == 2:
        partial = partial.reshape(pairs, 2, count_y, -1).transpose(1, 0, 2, 3)
    odd = lax.axis_index("gx") & 1 == 1
    swap = [(i, i ^ 1) for i in range(2 * pairs)]
    other = lax.ppermute(jnp.where(odd, partial[0], partial[1]), "gx", swap)
    own = jnp.where(odd, partial[1], partial[0])
    both = (own.astype(jnp.float32) + other.astype(jnp.float32)).astype(jnp.bfloat16)
    groups = [[(2 * i + c) * count_y + j for i in range(pairs) for j in range(count_y)] for c in range(2)]
    both = both.reshape(pairs * count_y, *both.shape[2:])
    shares = lax.all_to_all(both, ("gx", "gy"), 0, 0, axis_index_groups=groups, tiled=True)
    norm_scale = 1.0 / math.sqrt(cell_count * devices)
    grad_kernel = (jnp.sum(shares.astype(jnp.float32), axis=0) * norm_scale).reshape(-1)

    grad_source = pl.pallas_call(
        source_kernel,
        out_shape=jax.ShapeDtypeStruct(slope.shape, jnp.bfloat16),
        in_specs=[smem] + [vmem] * 6,
        out_specs=vmem,
        scratch_shapes=[
            pltpu.VMEM((3 * (width_x + 2) * channels, width_y * depth), jnp.bfloat16),
            pltpu.VMEM((3, 9 * channels, channels), jnp.bfloat16),
            pltpu.VMEM((3, channels, width_y * depth), jnp.float32),
        ],
        compiler_params=PARAMS,
        cost_estimate=pl.CostEstimate(
            flops=5400 * channels * channels * cell_count, bytes_accessed=2 * 1024 * 1024, transcendentals=0
        ),
        name="source_grad",
    )(parity, slope, after, before, near, far, kernel)
    return (grad_source.transpose(2, 0, 1, 3), grad_kernel)


def solution(mesh):
    placed = (P(None, "gx", "gy", None), P(None, "gx", "gy", None), P(None, "gx", "gy", None), P())
    return jax.shard_map(
        on_device,
        mesh=mesh,
        in_specs=placed,
        out_specs=(P(None, "gx", "gy", None), P(("gx", "gy"))),
        check_vma=False,
    )
```

```python
import math

import jax
import jax.numpy as jnp
from jax import lax
from jax.experimental import pallas as pl
from jax.experimental.pallas import tpu as pltpu
from jax.sharding import PartitionSpec as P

NT = (((1,), (1,)), ((), ()))
TN = (((0,), (0,)), ((), ()))
PARAMS = pltpu.CompilerParams(vmem_limit_bytes=32 * 1024 * 1024)


def to_next(block, axis):
    count = lax.axis_size(axis)
    return lax.ppermute(block, axis, [(i, (i + 1) % count) for i in range(count)])


def to_previous(block, axis):
    count = lax.axis_size(axis)
    return lax.ppermute(block, axis, [((i + 1) % count, i) for i in range(count)])


def swapped(first, last, axis):
    count = lax.axis_size(axis)
    even = lax.axis_index(axis) & 1 == 0
    near = [(i, i ^ 1) for i in range(count)]
    far = [(i, (i - 1) % count if i % 2 == 0 else (i + 1) % count) for i in range(count)]
    got_far = lax.ppermute(jnp.where(even, first, last), axis, far)
    got_near = lax.ppermute(jnp.where(even, last, first), axis, near)
    return got_near, got_far


def roll_lanes(block, step):
    if step == 0:
        return block
    return pltpu.roll(block.astype(jnp.float32), step % block.shape[-1], axis=1).astype(block.dtype)


def plane(slope, before, after, wide_x, row):
    if wide_x == 0:
        return before[0, row]
    if wide_x == slope.shape[0] + 1:
        return after[0, row]
    return slope[wide_x - 1, row]


def gather(parts):
    depth = parts[1].shape[1]
    return parts[1] + pltpu.roll(parts[0], depth - 1, axis=1) + pltpu.roll(parts[2], 1, axis=1)


def inner_kernel(slope, after, before, source, kernel, out, down, up, left, right, columns, weights):
    width_x, width_y, channels, depth = slope.shape
    for wide_x in range(width_x + 2):
        for y in range(width_y):
            left[wide_x * channels : (wide_x + 1) * channels, y * depth : (y + 1) * depth] = plane(
                slope, before, after, wide_x, y
            )
    zeros = jnp.zeros((3 * channels, depth), source.dtype)
    for x in range(width_x):
        right[x, 0 : 3 * channels, 0:depth] = zeros
        right[x, 6 * channels :, (width_y - 1) * depth :] = zeros
        for row in range(width_y):
            for c in range(3):
                moved = roll_lanes(source[x, row], 1 - c)
                for b in range(3):
                    y = row + 1 - b
                    if 0 <= y < width_y:
                        first = (3 * b + c) * channels
                        right[x, first : first + channels, y * depth : (y + 1) * depth] = moved
    total = None
    for x in range(width_x):
        part = lax.dot_general(
            left[x * channels : (x + 3) * channels, :], right[x], NT, preferred_element_type=jnp.float32
        )
        total = part if total is None else total + part
    out[...] = total
    edge_rows(slope, before, after, kernel, 0, 0, down, columns, weights)
    edge_rows(slope, before, after, kernel, width_y - 1, 2, up, columns, weights)


def weight_kernel(parity, inner, slope, after, before, far, near, out, left, right, gram, ordered):
    width_x, width_y, channels, depth = slope.shape
    even = parity[0] == 0
    sides = []
    for row in (0, width_y - 1):
        total = None
        for wide_x in range(width_x + 2):
            left[wide_x * channels : (wide_x + 1) * channels, :] = plane(slope, before, after, wide_x, row)
        for x in range(width_x):
            cells = jnp.where(even, far[x], near[x]) if row == 0 else jnp.where(even, near[x], far[x])
            for c in range(3):
                right[c * channels : (c + 1) * channels, :] = roll_lanes(cells, 1 - c)
            part = lax.dot_general(
                left[x * channels : (x + 3) * channels, :], right[...], NT, preferred_element_type=jnp.float32
            )
            total = part if total is None else total + part
        sides.append(total)
    total = jnp.concatenate(
        [
            inner[:, : 3 * channels] + sides[0],
            inner[:, 3 * channels : 6 * channels],
            inner[:, 6 * channels :] + sides[1],
        ],
        axis=1,
    )
    for pair in range(5):
        lanes = total[:, 2 * pair * channels : min(2 * pair + 2, 9) * channels]
        gram[pair, :, : lanes.shape[1]] = lanes
    half = channels // 2
    first_half = lax.broadcasted_iota(jnp.int32, (half, 2 * channels), 1) < channels
    for a in range(3):
        top = (2 - a) * channels
        for pair in range(5):
            low = gram[pair, pl.ds(top, half, stride=2), :]
            high = gram[pair, pl.ds(top + 1, half, stride=2), :]
            tap = 9 * a + 2 * pair
            ordered[tap * half : (tap + 1) * half, :] = jnp.where(first_half, low, pltpu.roll(high, channels, axis=1))
            if pair < 4:
                tap += 1
                ordered[tap * half : (tap + 1) * half, :] = jnp.where(
                    first_half, pltpu.roll(low, channels, axis=1), high
                )
    if len(out.shape) == 5:
        _, pairs, count_y, rows, _ = out.shape
        for part in range(2 * pairs * count_y):
            place = (part // count_y % 2, part // count_y // 2, part % count_y)
            out[place] = ordered[part * rows : (part + 1) * rows, :].astype(out.dtype)
    else:
        out[...] = ordered[...].astype(out.dtype)


def edge_rows(slope, before, after, kernel, row, b, out, columns, weights):
    width_x, width_y, channels, depth = slope.shape
    for wide_x in range(width_x + 2):
        columns[wide_x * channels : (wide_x + 1) * channels, :] = plane(slope, before, after, wide_x, row)
    for a in range(3):
        for c in range(3):
            weights[c, (2 - a) * channels : (3 - a) * channels, :] = kernel[9 * a + 3 * b + c]
    for x in range(width_x):
        cells = columns[x * channels : (x + 3) * channels, :]
        parts = [lax.dot_general(weights[c], cells, TN, preferred_element_type=jnp.float32) for c in range(3)]
        out[x] = gather(parts).astype(out.dtype)


def inner_kernel(slope, after, before, source, kernel, out, down, up, left, right, columns, weights):
    width_x, width_y, channels, depth = slope.shape
    for wide_x in range(width_x + 2):
        for y in range(width_y):
            left[wide_x * channels : (wide_x + 1) * channels, y * depth : (y + 1) * depth] = plane(
                slope, before, after, wide_x, y
            )
    zeros = jnp.zeros((3 * channels, depth), source.dtype)
    for x in range(width_x):
        right[x, 0 : 3 * channels, 0:depth] = zeros
        right[x, 6 * channels :, (width_y - 1) * depth :] = zeros
        for row in range(width_y):
            for c in range(3):
                moved = roll_lanes(source[x, row], 1 - c)
                for b in range(3):
                    y = row + 1 - b
                    if 0 <= y < width_y:
                        first = (3 * b + c) * channels
                        right[x, first : first + channels, y * depth : (y + 1) * depth] = moved
    total = None
    for x in range(width_x):
        part = lax.dot_general(
            left[x * channels : (x + 3) * channels, :], right[x], NT, preferred_element_type=jnp.float32
        )
        total = part if total is None else total + part
    out[...] = total
    edge_rows(slope, before, after, kernel, 0, 0, down, columns, weights)
    edge_rows(slope, before, after, kernel, width_y - 1, 2, up, columns, weights)


def weight_kernel(parity, inner, slope, after, before, far, near, out, left, right, gram, ordered):
    width_x, width_y, channels, depth = slope.shape
    even = parity[0] == 0
    sides = []
    for row in (0, width_y - 1):
        total = None
        for wide_x in range(width_x + 2):
            left[wide_x * channels : (wide_x + 1) * channels, :] = plane(slope, before, after, wide_x, row)
        for x in range(width_x):
            cells = jnp.where(even, far[x], near[x]) if row == 0 else jnp.where(even, near[x], far[x])
            for c in range(3):
                right[c * channels : (c + 1) * channels, :] = roll_lanes(cells, 1 - c)
            part = lax.dot_general(
                left[x * channels : (x + 3) * channels, :], right[...], NT, preferred_element_type=jnp.float32
            )
            total = part if total is None else total + part
        sides.append(total)
    total = jnp.concatenate(
        [
            inner[:, : 3 * channels] + sides[0],
            inner[:, 3 * channels : 6 * channels],
            inner[:, 6 * channels :] + sides[1],
        ],
        axis=1,
    )
    for pair in range(5):
        lanes = total[:, 2 * pair * channels : min(2 * pair + 2, 9) * channels]
        gram[pair, :, : lanes.shape[1]] = lanes
    half = channels // 2
    first_half = lax.broadcasted_iota(jnp.int32, (half, 2 * channels), 1) < channels
    for a in range(3):
        top = (2 - a) * channels
        for pair in range(5):
            low = gram[pair, pl.ds(top, half, stride=2), :]
            high = gram[pair, pl.ds(top + 1, half, stride=2), :]
            tap = 9 * a + 2 * pair
            ordered[tap * half : (tap + 1) * half, :] = jnp.where(first_half, low, pltpu.roll(high, channels, axis=1))
            if pair < 4:
                tap += 1
                ordered[tap * half : (tap + 1) * half, :] = jnp.where(
                    first_half, pltpu.roll(low, channels, axis=1), high
                )
    if len(out.shape) == 5:
        _, pairs, count_y, rows, _ = out.shape
        for part in range(2 * pairs * count_y):
            place = (part // count_y % 2, part // count_y // 2, part % count_y)
            out[place] = ordered[part * rows : (part + 1) * rows, :].astype(out.dtype)
    else:
        out[...] = ordered[...].astype(out.dtype)


def edge_kernel(slope, before, after, kernel, down, up, columns, weights):
    width_x, width_y, channels, depth = slope.shape
    for out, row, b in ((down, 0, 0), (up, width_y - 1, 2)):
        for wide_x in range(width_x + 2):
            columns[wide_x * channels : (wide_x + 1) * channels, :] = plane(slope, before, after, wide_x, row)
        for a in range(3):
            for c in range(3):
                weights[c, (2 - a) * channels : (3 - a) * channels, :] = kernel[9 * a + 3 * b + c]
        for x in range(width_x):
            cells = columns[x * channels : (x + 3) * channels, :]
            parts = [lax.dot_general(weights[c], cells, TN, preferred_element_type=jnp.float32) for c in range(3)]
            out[x] = gather(parts).astype(out.dtype)


def source_kernel(parity, slope, after, before, far, near, kernel, out, columns, weights, spread):
    width_x, width_y, channels, depth = slope.shape
    even = parity[0] == 0
    zeros = jnp.zeros((channels, depth), slope.dtype)
    for wide_x in range(width_x + 2):
        for row in range(-1, width_y + 1):
            cells = plane(slope, before, after, wide_x, row) if 0 <= row < width_y else zeros
            for b in range(3):
                y = row + b - 1
                if 0 <= y < width_y:
                    first = (3 * wide_x + b) * channels
                    columns[first : first + channels, y * depth : (y + 1) * depth] = cells
    for a in range(3):
        for b in range(3):
            for c in range(3):
                first = (3 * (2 - a) + b) * channels
                weights[c, first : first + channels, :] = kernel[9 * a + 3 * b + c]
    for x in range(width_x):
        cells = columns[3 * x * channels : 3 * (x + 3) * channels, :]
        for c in range(3):
            spread[c] = lax.dot_general(weights[c], cells, TN, preferred_element_type=jnp.float32)
        for y in range(width_y):
            lanes = slice(y * depth, (y + 1) * depth)
            total = gather([spread[c, :, lanes] for c in range(3)])
            if y == 0:
                total += jnp.where(even, far[x], near[x]).astype(jnp.float32)
            if y == width_y - 1:
                total += jnp.where(even, near[x], far[x]).astype(jnp.float32)
            out[x, y] = total.astype(out.dtype)


def on_device(source, preact, cotangent, kernel):
    channels, width_x, width_y, depth = source.shape
    devices = lax.axis_size("gx") * lax.axis_size("gy")
    cell_count = width_x * width_y * depth
    lines = 27 * channels * channels // 128
    pairs, count_y = lax.axis_size("gx") // 2, lax.axis_size("gy")
    share = (2, pairs, count_y, lines // devices, 128) if lines % devices == 0 else (lines, 128)
    parity = (lax.axis_index("gy") & 1).reshape(1)

    slope = jnp.where(preact > 0, cotangent, jnp.zeros_like(cotangent)).transpose(1, 2, 0, 3)
    src = source.transpose(1, 2, 0, 3)
    slope, src = lax.optimization_barrier((slope, src))
    before = to_next(slope[width_x - 1 :], "gx")
    after = to_previous(slope[:1], "gx")
    src_near, src_far = swapped(src[:, 0], src[:, -1], "gy")

    cost = pl.CostEstimate(
        flops=54 * channels * channels * cell_count, bytes_accessed=2 * 1024 * 1024, transcendentals=0
    )
    vmem = pl.BlockSpec(memory_space=pltpu.VMEM)
    smem = pl.BlockSpec(memory_space=pltpu.SMEM)
    edge = jax.ShapeDtypeStruct((width_x, channels, depth), jnp.bfloat16)
    inner, down, up = pl.pallas_call(
        inner_kernel,
        out_shape=(jax.ShapeDtypeStruct((3 * channels, 9 * channels), jnp.float32), edge, edge),
        in_specs=[vmem] * 5,
        out_specs=(vmem, vmem, vmem),
        scratch_shapes=[
            pltpu.VMEM(((width_x + 2) * channels, width_y * depth), jnp.bfloat16),
            pltpu.VMEM((width_x, 9 * channels, width_y * depth), jnp.bfloat16),
            pltpu.VMEM(((width_x + 2) * channels, depth), jnp.bfloat16),
            pltpu.VMEM((3, 3 * channels, channels), jnp.bfloat16),
        ],
        compiler_params=PARAMS,
        cost_estimate=cost,
        name="weight_inner",
    )(slope, after, before, src, kernel)
    partial = pl.pallas_call(
        weight_kernel,
        out_shape=jax.ShapeDtypeStruct(share, jnp.bfloat16),
        in_specs=[smem] + [vmem] * 6,
        out_specs=vmem,
        scratch_shapes=[
            pltpu.VMEM(((width_x + 2) * channels, depth), jnp.bfloat16),
            pltpu.VMEM((3 * channels, depth), jnp.bfloat16),
            pltpu.VMEM((5, 3 * channels, 2 * channels), jnp.float32),
            pltpu.VMEM((lines, 128), jnp.float32),
        ],
        compiler_params=PARAMS,
        cost_estimate=cost,
        name="weight_grad",
    )(parity, inner, slope, after, before, src_far, src_near)
    near, far = swapped(down, up, "gy")
    if len(share) == 2:
        partial = partial.reshape(pairs, 2, count_y, -1).transpose(1, 0, 2, 3)
    odd = lax.axis_index("gx") & 1 == 1
    swap = [(i, i ^ 1) for i in range(2 * pairs)]
    other = lax.ppermute(jnp.where(odd, partial[0], partial[1]), "gx", swap)
    own = jnp.where(odd, partial[1], partial[0])
    both = (own.astype(jnp.float32) + other.astype(jnp.float32)).astype(jnp.bfloat16)
    groups = [[(2 * i + c) * count_y + j for i in range(pairs) for j in range(count_y)] for c in range(2)]
    both = both.reshape(pairs * count_y, *both.shape[2:])
    shares = lax.all_to_all(both, ("gx", "gy"), 0, 0, axis_index_groups=groups, tiled=True)
    norm_scale = 1.0 / math.sqrt(cell_count * devices)
    grad_kernel = (jnp.sum(shares.astype(jnp.float32), axis=0) * norm_scale).reshape(-1)

    grad_source = pl.pallas_call(
        source_kernel,
        out_shape=jax.ShapeDtypeStruct(slope.shape, jnp.bfloat16),
        in_specs=[smem] + [vmem] * 6,
        out_specs=vmem,
        scratch_shapes=[
            pltpu.VMEM((3 * (width_x + 2) * channels, width_y * depth), jnp.bfloat16),
            pltpu.VMEM((3, 9 * channels, channels), jnp.bfloat16),
            pltpu.VMEM((3, channels, width_y * depth), jnp.float32),
        ],
        compiler_params=PARAMS,
        cost_estimate=pl.CostEstimate(
            flops=5400 * channels * channels * cell_count, bytes_accessed=2 * 1024 * 1024, transcendentals=0
        ),
        name="source_grad",
    )(parity, slope, after, before, far, near, kernel)
    return (grad_source.transpose(2, 0, 1, 3), grad_kernel)


def solution(mesh):
    placed = (P(None, "gx", "gy", None), P(None, "gx", "gy", None), P(None, "gx", "gy", None), P())
    return jax.shard_map(
        on_device,
        mesh=mesh,
        in_specs=placed,
        out_specs=(P(None, "gx", "gy", None), P(("gx", "gy"))),
        check_vma=False,
    )
```

```python
import functools
import math

import jax
import jax.numpy as jnp
from jax import lax
from jax.experimental import pallas as pl
from jax.experimental.pallas import tpu as pltpu
from jax.sharding import PartitionSpec as P

NT = (((1,), (1,)), ((), ()))
TN = (((0,), (0,)), ((), ()))
PARAMS = pltpu.CompilerParams(vmem_limit_bytes=32 * 1024 * 1024)


def is_even(axis):
    return lax.axis_index(axis) & 1 == 0


def swapped(first, last, axis):
    count = lax.axis_size(axis)
    even = is_even(axis)
    near = [(i, i ^ 1) for i in range(count)]
    far = [(i, (i - 1) % count if i % 2 == 0 else (i + 1) % count) for i in range(count)]
    got_far = lax.ppermute(jnp.where(even, first, last), axis, far)
    got_near = lax.ppermute(jnp.where(even, last, first), axis, near)
    return got_near, got_far


def roll_lanes(block, step):
    if step == 0:
        return block
    return pltpu.roll(block.astype(jnp.float32), step % block.shape[-1], axis=1).astype(block.dtype)


def plane(slope, near, far, even, wide_x, row):
    if wide_x == 0:
        return jnp.where(even, far[0, row], near[0, row])
    if wide_x == slope.shape[0] + 1:
        return jnp.where(even, near[0, row], far[0, row])
    return slope[wide_x - 1, row]


def gather(parts):
    depth = parts[1].shape[1]
    return parts[1] + pltpu.roll(parts[0], depth - 1, axis=1) + pltpu.roll(parts[2], 1, axis=1)


def edge_rows(cells_at, width_x, kernel, row, b, out, columns, weights):
    channels = kernel.shape[1]
    for wide_x in range(width_x + 2):
        columns[wide_x * channels : (wide_x + 1) * channels, :] = cells_at(wide_x, row)
    for a in range(3):
        for c in range(3):
            weights[c, (2 - a) * channels : (3 - a) * channels, :] = kernel[9 * a + 3 * b + c]
    for x in range(width_x):
        cells = columns[x * channels : (x + 3) * channels, :]
        parts = [lax.dot_general(weights[c], cells, TN, preferred_element_type=jnp.float32) for c in range(3)]
        out[x] = gather(parts).astype(out.dtype)


def inner_kernel(slope, x_near, x_far, source, kernel, out, down, up, left, right, columns, weights):
    width_x, width_y, channels, depth = slope.shape
    cells_at = functools.partial(plane, slope, x_near, x_far, is_even("gx"))
    for wide_x in range(width_x + 2):
        for y in range(width_y):
            left[wide_x * channels : (wide_x + 1) * channels, y * depth : (y + 1) * depth] = cells_at(wide_x, y)
    zeros = jnp.zeros((3 * channels, depth), source.dtype)
    for x in range(width_x):
        right[x, 0 : 3 * channels, 0:depth] = zeros
        right[x, 6 * channels :, (width_y - 1) * depth :] = zeros
        for row in range(width_y):
            for c in range(3):
                moved = roll_lanes(source[x, row], 1 - c)
                for b in range(3):
                    y = row + 1 - b
                    if 0 <= y < width_y:
                        first = (3 * b + c) * channels
                        right[x, first : first + channels, y * depth : (y + 1) * depth] = moved
    total = None
    for x in range(width_x):
        part = lax.dot_general(
            left[x * channels : (x + 3) * channels, :], right[x], NT, preferred_element_type=jnp.float32
        )
        total = part if total is None else total + part
    out[...] = total
    edge_rows(cells_at, width_x, kernel, 0, 0, down, columns, weights)
    edge_rows(cells_at, width_x, kernel, width_y - 1, 2, up, columns, weights)


def weight_kernel(order, inner, slope, x_near, x_far, far, near, out, left, right, gram, ordered):
    width_x, width_y, channels, depth = slope.shape
    cells_at = functools.partial(plane, slope, x_near, x_far, is_even("gx"))
    even = is_even("gy")
    sides = []
    for row in (0, width_y - 1):
        total = None
        for wide_x in range(width_x + 2):
            left[wide_x * channels : (wide_x + 1) * channels, :] = cells_at(wide_x, row)
        for x in range(width_x):
            cells = jnp.where(even, far[x], near[x]) if row == 0 else jnp.where(even, near[x], far[x])
            for c in range(3):
                right[c * channels : (c + 1) * channels, :] = roll_lanes(cells, 1 - c)
            part = lax.dot_general(
                left[x * channels : (x + 3) * channels, :], right[...], NT, preferred_element_type=jnp.float32
            )
            total = part if total is None else total + part
        sides.append(total)
    total = jnp.concatenate(
        [
            inner[:, : 3 * channels] + sides[0],
            inner[:, 3 * channels : 6 * channels],
            inner[:, 6 * channels :] + sides[1],
        ],
        axis=1,
    )
    for pair in range(5):
        lanes = total[:, 2 * pair * channels : min(2 * pair + 2, 9) * channels]
        gram[pair, :, : lanes.shape[1]] = lanes
    half = channels // 2
    first_half = lax.broadcasted_iota(jnp.int32, (half, 2 * channels), 1) < channels
    for a in range(3):
        top = (2 - a) * channels
        for pair in range(5):
            low = gram[pair, pl.ds(top, half, stride=2), :]
            high = gram[pair, pl.ds(top + 1, half, stride=2), :]
            tap = 9 * a + 2 * pair
            ordered[tap * half : (tap + 1) * half, :] = jnp.where(first_half, low, pltpu.roll(high, channels, axis=1))
            if pair < 4:
                tap += 1
                ordered[tap * half : (tap + 1) * half, :] = jnp.where(
                    first_half, pltpu.roll(low, channels, axis=1), high
                )
    if len(out.shape) == 4:
        rows = out.shape[2]
        for core in range(2):
            for slot, part in enumerate(order[core]):
                out[core, slot] = ordered[part * rows : (part + 1) * rows, :].astype(out.dtype)
    else:
        out[...] = ordered[...].astype(out.dtype)


def source_kernel(slope, x_near, x_far, far, near, kernel, out, columns, weights, spread):
    width_x, width_y, channels, depth = slope.shape
    cells_at = functools.partial(plane, slope, x_near, x_far, is_even("gx"))
    even = is_even("gy")
    zeros = jnp.zeros((channels, depth), slope.dtype)
    for wide_x in range(width_x + 2):
        for row in range(-1, width_y + 1):
            cells = cells_at(wide_x, row) if 0 <= row < width_y else zeros
            for b in range(3):
                y = row + b - 1
                if 0 <= y < width_y:
                    first = (3 * wide_x + b) * channels
                    columns[first : first + channels, y * depth : (y + 1) * depth] = cells
    for a in range(3):
        for b in range(3):
            for c in range(3):
                first = (3 * (2 - a) + b) * channels
                weights[c, first : first + channels, :] = kernel[9 * a + 3 * b + c]
    for x in range(width_x):
        cells = columns[3 * x * channels : 3 * (x + 3) * channels, :]
        for c in range(3):
            spread[c] = lax.dot_general(weights[c], cells, TN, preferred_element_type=jnp.float32)
        for y in range(width_y):
            lanes = slice(y * depth, (y + 1) * depth)
            total = gather([spread[c, :, lanes] for c in range(3)])
            if y == 0:
                total += jnp.where(even, far[x], near[x]).astype(jnp.float32)
            if y == width_y - 1:
                total += jnp.where(even, near[x], far[x]).astype(jnp.float32)
            out[x, y] = total.astype(out.dtype)


def on_device(source, preact, cotangent, kernel):
    channels, width_x, width_y, depth = source.shape
    devices = lax.axis_size("gx") * lax.axis_size("gy")
    cell_count = width_x * width_y * depth
    lines = 27 * channels * channels // 128
    pairs, count_y = lax.axis_size("gx") // 2, lax.axis_size("gy")
    share = (2, pairs * count_y, lines // devices, 128) if lines % devices == 0 else (lines, 128)
    places = [(i, (i + step) % count_y) for step in range(count_y) for i in range(pairs)]
    order = [[(2 * i + core) * count_y + j for i, j in places] for core in range(2)]

    slope = jnp.where(preact > 0, cotangent, jnp.zeros_like(cotangent)).transpose(1, 2, 0, 3)
    src = source.transpose(1, 2, 0, 3)
    slope, src = lax.optimization_barrier((slope, src))
    x_near, x_far = swapped(slope[:1], slope[width_x - 1 :], "gx")
    src_near, src_far = swapped(src[:, 0], src[:, -1], "gy")

    cost = pl.CostEstimate(
        flops=54 * channels * channels * cell_count, bytes_accessed=2 * 1024 * 1024, transcendentals=0
    )
    vmem = pl.BlockSpec(memory_space=pltpu.VMEM)
    edge = jax.ShapeDtypeStruct((width_x, channels, depth), jnp.bfloat16)
    inner, down, up = pl.pallas_call(
        inner_kernel,
        out_shape=(jax.ShapeDtypeStruct((3 * channels, 9 * channels), jnp.float32), edge, edge),
        in_specs=[vmem] * 5,
        out_specs=(vmem, vmem, vmem),
        scratch_shapes=[
            pltpu.VMEM(((width_x + 2) * channels, width_y * depth), jnp.bfloat16),
            pltpu.VMEM((width_x, 9 * channels, width_y * depth), jnp.bfloat16),
            pltpu.VMEM(((width_x + 2) * channels, depth), jnp.bfloat16),
            pltpu.VMEM((3, 3 * channels, channels), jnp.bfloat16),
        ],
        compiler_params=PARAMS,
        cost_estimate=cost,
        name="weight_inner",
    )(slope, x_near, x_far, src, kernel)
    partial = pl.pallas_call(
        functools.partial(weight_kernel, order),
        out_shape=jax.ShapeDtypeStruct(share, jnp.bfloat16),
        in_specs=[vmem] * 6,
        out_specs=vmem,
        scratch_shapes=[
            pltpu.VMEM(((width_x + 2) * channels, depth), jnp.bfloat16),
            pltpu.VMEM((3 * channels, depth), jnp.bfloat16),
            pltpu.VMEM((5, 3 * channels, 2 * channels), jnp.float32),
            pltpu.VMEM((lines, 128), jnp.float32),
        ],
        compiler_params=PARAMS,
        cost_estimate=cost,
        name="weight_grad",
    )(inner, slope, x_near, x_far, src_far, src_near)
    near, far = swapped(down, up, "gy")
    if len(share) == 2:
        partial = partial.reshape(devices, -1)[jnp.array(order)]
    even = is_even("gx")
    swap = [(i, i ^ 1) for i in range(2 * pairs)]
    other = lax.ppermute(jnp.where(even, partial[1], partial[0]), "gx", swap)
    own = jnp.where(even, partial[0], partial[1])
    both = (own.astype(jnp.float32) + other.astype(jnp.float32)).astype(jnp.bfloat16)
    shares = lax.all_to_all(both, ("gx", "gy"), 0, 0, axis_index_groups=order, tiled=True)
    norm_scale = 1.0 / math.sqrt(cell_count * devices)
    grad_kernel = (jnp.sum(shares.astype(jnp.float32), axis=0) * norm_scale).reshape(-1)

    grad_source = pl.pallas_call(
        source_kernel,
        out_shape=jax.ShapeDtypeStruct(slope.shape, jnp.bfloat16),
        in_specs=[vmem] * 6,
        out_specs=vmem,
        scratch_shapes=[
            pltpu.VMEM((3 * (width_x + 2) * channels, width_y * depth), jnp.bfloat16),
            pltpu.VMEM((3, 9 * channels, channels), jnp.bfloat16),
            pltpu.VMEM((3, channels, width_y * depth), jnp.float32),
        ],
        compiler_params=PARAMS,
        cost_estimate=pl.CostEstimate(
            flops=5400 * channels * channels * cell_count, bytes_accessed=2 * 1024 * 1024, transcendentals=0
        ),
        name="source_grad",
    )(slope, x_near, x_far, far, near, kernel)
    return (grad_source.transpose(2, 0, 1, 3), grad_kernel)


def solution(mesh):
    placed = (P(None, "gx", "gy", None), P(None, "gx", "gy", None), P(None, "gx", "gy", None), P())
    return jax.shard_map(
        on_device,
        mesh=mesh,
        in_specs=placed,
        out_specs=(P(None, "gx", "gy", None), P(("gx", "gy"))),
        check_vma=False,
    )
```

```python
import functools
import math

import jax
import jax.numpy as jnp
from jax import lax
from jax.experimental import pallas as pl
from jax.experimental.pallas import tpu as pltpu
from jax.sharding import PartitionSpec as P

NT = (((1,), (1,)), ((), ()))
TN = (((0,), (0,)), ((), ()))
PARAMS = pltpu.CompilerParams(vmem_limit_bytes=32 * 1024 * 1024)


def is_even(axis):
    return lax.axis_index(axis) & 1 == 0


def swapped(first, last, axis):
    count = lax.axis_size(axis)
    even = is_even(axis)
    near = [(i, i ^ 1) for i in range(count)]
    far = [(i, (i - 1) % count if i % 2 == 0 else (i + 1) % count) for i in range(count)]
    got_far = lax.ppermute(jnp.where(even, first, last), axis, far)
    got_near = lax.ppermute(jnp.where(even, last, first), axis, near)
    return got_near, got_far


def roll_lanes(block, step):
    if step == 0:
        return block
    return pltpu.roll(block.astype(jnp.float32), step % block.shape[-1], axis=1).astype(block.dtype)


def plane(slope, near, far, even, wide_x, row):
    if wide_x == 0:
        return jnp.where(even, far[0, row], near[0, row])
    if wide_x == slope.shape[0] + 1:
        return jnp.where(even, near[0, row], far[0, row])
    return slope[wide_x - 1, row]


def gather(parts):
    depth = parts[1].shape[1]
    return parts[1] + pltpu.roll(parts[0], depth - 1, axis=1) + pltpu.roll(parts[2], 1, axis=1)


def edge_rows(cells_at, width_x, kernel, row, b, out, columns, weights):
    channels = kernel.shape[1]
    for wide_x in range(width_x + 2):
        columns[wide_x * channels : (wide_x + 1) * channels, :] = cells_at(wide_x, row)
    for a in range(3):
        for c in range(3):
            weights[c, (2 - a) * channels : (3 - a) * channels, :] = kernel[9 * a + 3 * b + c]
    for x in range(width_x):
        cells = columns[x * channels : (x + 3) * channels, :]
        parts = [lax.dot_general(weights[c], cells, TN, preferred_element_type=jnp.float32) for c in range(3)]
        out[x] = gather(parts).astype(out.dtype)


def inner_kernel(slope, x_near, x_far, source, kernel, out, down, up, left, right, columns, weights):
    width_x, width_y, channels, depth = slope.shape
    cells_at = functools.partial(plane, slope, x_near, x_far, is_even("gx"))
    for wide_x in range(width_x + 2):
        for y in range(width_y):
            left[wide_x * channels : (wide_x + 1) * channels, y * depth : (y + 1) * depth] = cells_at(wide_x, y)
    zeros = jnp.zeros((3 * channels, depth), source.dtype)
    for x in range(width_x):
        right[x, 0 : 3 * channels, 0:depth] = zeros
        right[x, 6 * channels :, (width_y - 1) * depth :] = zeros
        for row in range(width_y):
            for c in range(3):
                moved = roll_lanes(source[x, row], 1 - c)
                for b in range(3):
                    y = row + 1 - b
                    if 0 <= y < width_y:
                        first = (3 * b + c) * channels
                        right[x, first : first + channels, y * depth : (y + 1) * depth] = moved
    total = None
    for x in range(width_x):
        part = lax.dot_general(
            left[x * channels : (x + 3) * channels, :], right[x], NT, preferred_element_type=jnp.float32
        )
        total = part if total is None else total + part
    out[...] = total
    edge_rows(cells_at, width_x, kernel, 0, 0, down, columns, weights)
    edge_rows(cells_at, width_x, kernel, width_y - 1, 2, up, columns, weights)


def weight_kernel(order, inner, slope, x_near, x_far, far, near, out, left, right, gram, ordered):
    width_x, width_y, channels, depth = slope.shape
    cells_at = functools.partial(plane, slope, x_near, x_far, is_even("gx"))
    even = is_even("gy")
    sides = []
    for row in (0, width_y - 1):
        total = None
        for wide_x in range(width_x + 2):
            left[wide_x * channels : (wide_x + 1) * channels, :] = cells_at(wide_x, row)
        for x in range(width_x):
            cells = jnp.where(even, far[x], near[x]) if row == 0 else jnp.where(even, near[x], far[x])
            for c in range(3):
                right[c * channels : (c + 1) * channels, :] = roll_lanes(cells, 1 - c)
            part = lax.dot_general(
                left[x * channels : (x + 3) * channels, :], right[...], NT, preferred_element_type=jnp.float32
            )
            total = part if total is None else total + part
        sides.append(total)
    total = jnp.concatenate(
        [
            inner[:, : 3 * channels] + sides[0],
            inner[:, 3 * channels : 6 * channels],
            inner[:, 6 * channels :] + sides[1],
        ],
        axis=1,
    )
    for pair in range(5):
        lanes = total[:, 2 * pair * channels : min(2 * pair + 2, 9) * channels]
        gram[pair, :, : lanes.shape[1]] = lanes
    half = channels // 2
    first_half = lax.broadcasted_iota(jnp.int32, (half, 2 * channels), 1) < channels
    for a in range(3):
        top = (2 - a) * channels
        for pair in range(5):
            low = gram[pair, pl.ds(top, half, stride=2), :]
            high = gram[pair, pl.ds(top + 1, half, stride=2), :]
            tap = 9 * a + 2 * pair
            ordered[tap * half : (tap + 1) * half, :] = jnp.where(first_half, low, pltpu.roll(high, channels, axis=1))
            if pair < 4:
                tap += 1
                ordered[tap * half : (tap + 1) * half, :] = jnp.where(
                    first_half, pltpu.roll(low, channels, axis=1), high
                )
    if len(out.shape) == 5:
        _, slots, tiles, height, _ = out.shape
        rows = 9 * half * 3 // (2 * slots)
        ordered[27 * half :, :] = jnp.zeros((8, 2 * channels), jnp.float32)
        for core in range(2):
            for slot, part in enumerate(order[core]):
                for tile in range(tiles):
                    first = part * rows + tile * height
                    out[core, slot, tile] = ordered[first : first + height, :].astype(out.dtype)
    else:
        out[...] = ordered[: 27 * half, :].astype(out.dtype)


def source_kernel(slope, x_near, x_far, far, near, kernel, out, columns, weights, spread):
    width_x, width_y, channels, depth = slope.shape
    cells_at = functools.partial(plane, slope, x_near, x_far, is_even("gx"))
    even = is_even("gy")
    zeros = jnp.zeros((channels, depth), slope.dtype)
    for wide_x in range(width_x + 2):
        for row in range(-1, width_y + 1):
            cells = cells_at(wide_x, row) if 0 <= row < width_y else zeros
            for b in range(3):
                y = row + b - 1
                if 0 <= y < width_y:
                    first = (3 * wide_x + b) * channels
                    columns[first : first + channels, y * depth : (y + 1) * depth] = cells
    for a in range(3):
        for b in range(3):
            for c in range(3):
                first = (3 * (2 - a) + b) * channels
                weights[c, first : first + channels, :] = kernel[9 * a + 3 * b + c]
    for x in range(width_x):
        cells = columns[3 * x * channels : 3 * (x + 3) * channels, :]
        for c in range(3):
            spread[c] = lax.dot_general(weights[c], cells, TN, preferred_element_type=jnp.float32)
        for y in range(width_y):
            lanes = slice(y * depth, (y + 1) * depth)
            total = gather([spread[c, :, lanes] for c in range(3)])
            if y == 0:
                total += jnp.where(even, far[x], near[x]).astype(jnp.float32)
            if y == width_y - 1:
                total += jnp.where(even, near[x], far[x]).astype(jnp.float32)
            out[x, y] = total.astype(out.dtype)


def on_device(source, preact, cotangent, kernel):
    channels, width_x, width_y, depth = source.shape
    devices = lax.axis_size("gx") * lax.axis_size("gy")
    cell_count = width_x * width_y * depth
    lines = 27 * channels * channels // 128
    pairs, count_y = lax.axis_size("gx") // 2, lax.axis_size("gy")
    whole_rows = lines % devices == 0
    share = (2, pairs * count_y, -(-lines // devices // 4), 4, 128) if whole_rows else (lines, 128)
    places = [(i, (i + step) % count_y) for step in range(count_y) for i in range(pairs)]
    order = [[(2 * i + core) * count_y + j for i, j in places] for core in range(2)]

    slope = jnp.where(preact > 0, cotangent, jnp.zeros_like(cotangent)).transpose(1, 2, 0, 3)
    src = source.transpose(1, 2, 0, 3)
    slope, src = lax.optimization_barrier((slope, src))
    x_near, x_far = swapped(slope[:1], slope[width_x - 1 :], "gx")
    src_near, src_far = swapped(src[:, 0], src[:, -1], "gy")

    cost = pl.CostEstimate(
        flops=54 * channels * channels * cell_count, bytes_accessed=2 * 1024 * 1024, transcendentals=0
    )
    vmem = pl.BlockSpec(memory_space=pltpu.VMEM)
    edge = jax.ShapeDtypeStruct((width_x, channels, depth), jnp.bfloat16)
    inner, down, up = pl.pallas_call(
        inner_kernel,
        out_shape=(jax.ShapeDtypeStruct((3 * channels, 9 * channels), jnp.float32), edge, edge),
        in_specs=[vmem] * 5,
        out_specs=(vmem, vmem, vmem),
        scratch_shapes=[
            pltpu.VMEM(((width_x + 2) * channels, width_y * depth), jnp.bfloat16),
            pltpu.VMEM((width_x, 9 * channels, width_y * depth), jnp.bfloat16),
            pltpu.VMEM(((width_x + 2) * channels, depth), jnp.bfloat16),
            pltpu.VMEM((3, 3 * channels, channels), jnp.bfloat16),
        ],
        compiler_params=PARAMS,
        cost_estimate=cost,
        name="weight_inner",
    )(slope, x_near, x_far, src, kernel)
    partial = pl.pallas_call(
        functools.partial(weight_kernel, order),
        out_shape=jax.ShapeDtypeStruct(share, jnp.bfloat16),
        in_specs=[vmem] * 6,
        out_specs=vmem,
        scratch_shapes=[
            pltpu.VMEM(((width_x + 2) * channels, depth), jnp.bfloat16),
            pltpu.VMEM((3 * channels, depth), jnp.bfloat16),
            pltpu.VMEM((5, 3 * channels, 2 * channels), jnp.float32),
            pltpu.VMEM((lines + 8, 128), jnp.float32),
        ],
        compiler_params=PARAMS,
        cost_estimate=cost,
        name="weight_grad",
    )(inner, slope, x_near, x_far, src_far, src_near)
    near, far = swapped(down, up, "gy")
    if not whole_rows:
        partial = partial.reshape(devices, -1)[jnp.array(order)]
    even = is_even("gx")
    swap = [(i, i ^ 1) for i in range(2 * pairs)]
    other = lax.ppermute(jnp.where(even, partial[1], partial[0]), "gx", swap)
    own = jnp.where(even, partial[0], partial[1])
    both = (own.astype(jnp.float32) + other.astype(jnp.float32)).astype(jnp.bfloat16)
    shares = lax.all_to_all(both, ("gx", "gy"), 0, 0, axis_index_groups=order, tiled=True)
    norm_scale = 1.0 / math.sqrt(cell_count * devices)
    grad_kernel = (jnp.sum(shares.astype(jnp.float32), axis=0) * norm_scale).reshape(-1)
    grad_kernel = grad_kernel[: 27 * channels * channels // devices]

    grad_source = pl.pallas_call(
        source_kernel,
        out_shape=jax.ShapeDtypeStruct(slope.shape, jnp.bfloat16),
        in_specs=[vmem] * 6,
        out_specs=vmem,
        scratch_shapes=[
            pltpu.VMEM((3 * (width_x + 2) * channels, width_y * depth), jnp.bfloat16),
            pltpu.VMEM((3, 9 * channels, channels), jnp.bfloat16),
            pltpu.VMEM((3, channels, width_y * depth), jnp.float32),
        ],
        compiler_params=PARAMS,
        cost_estimate=pl.CostEstimate(
            flops=5400 * channels * channels * cell_count, bytes_accessed=2 * 1024 * 1024, transcendentals=0
        ),
        name="source_grad",
    )(slope, x_near, x_far, far, near, kernel)
    return (grad_source.transpose(2, 0, 1, 3), grad_kernel)


def solution(mesh):
    placed = (P(None, "gx", "gy", None), P(None, "gx", "gy", None), P(None, "gx", "gy", None), P())
    return jax.shard_map(
        on_device,
        mesh=mesh,
        in_specs=placed,
        out_specs=(P(None, "gx", "gy", None), P(("gx", "gy"))),
        check_vma=False,
    )
```

```python
import functools
import math

import jax
import jax.numpy as jnp
from jax import lax
from jax.experimental import pallas as pl
from jax.experimental.pallas import tpu as pltpu
from jax.sharding import PartitionSpec as P

NT = (((1,), (1,)), ((), ()))
TN = (((0,), (0,)), ((), ()))
PARAMS = pltpu.CompilerParams(vmem_limit_bytes=32 * 1024 * 1024)


def is_even(axis):
    return lax.axis_index(axis) & 1 == 0


def swapped(first, last, axis):
    count = lax.axis_size(axis)
    even = is_even(axis)
    near = [(i, i ^ 1) for i in range(count)]
    far = [(i, (i - 1) % count if i % 2 == 0 else (i + 1) % count) for i in range(count)]
    got_far = lax.ppermute(jnp.where(even, first, last), axis, far)
    got_near = lax.ppermute(jnp.where(even, last, first), axis, near)
    return got_near, got_far


def roll_lanes(block, step):
    if step == 0:
        return block
    return pltpu.roll(block.astype(jnp.float32), step % block.shape[-1], axis=1).astype(block.dtype)


def plane(slope, near, far, even, wide_x, row):
    if wide_x == 0:
        return jnp.where(even, far[0, row], near[0, row])
    if wide_x == slope.shape[0] + 1:
        return jnp.where(even, near[0, row], far[0, row])
    return slope[wide_x - 1, row]


def gather(parts):
    depth = parts[1].shape[1]
    return parts[1] + pltpu.roll(parts[0], depth - 1, axis=1) + pltpu.roll(parts[2], 1, axis=1)


def edge_rows(cells_at, width_x, kernel, row, b, out, columns, weights):
    channels = kernel.shape[1]
    for wide_x in range(width_x + 2):
        columns[wide_x * channels : (wide_x + 1) * channels, :] = cells_at(wide_x, row)
    for a in range(3):
        for c in range(3):
            weights[c, (2 - a) * channels : (3 - a) * channels, :] = kernel[9 * a + 3 * b + c]
    for x in range(width_x):
        cells = columns[x * channels : (x + 3) * channels, :]
        parts = [lax.dot_general(weights[c], cells, TN, preferred_element_type=jnp.float32) for c in range(3)]
        out[x] = gather(parts).astype(out.dtype)


def inner_kernel(slope, x_near, x_far, source, kernel, out, down, up, left, right, columns, weights):
    width_x, width_y, channels, depth = slope.shape
    cells_at = functools.partial(plane, slope, x_near, x_far, is_even("gx"))
    for wide_x in range(width_x + 2):
        for y in range(width_y):
            left[wide_x * channels : (wide_x + 1) * channels, y * depth : (y + 1) * depth] = cells_at(wide_x, y)
    zeros = jnp.zeros((3 * channels, depth), source.dtype)
    for x in range(width_x):
        right[x, 0 : 3 * channels, 0:depth] = zeros
        right[x, 6 * channels :, (width_y - 1) * depth :] = zeros
        for row in range(width_y):
            for c in range(3):
                moved = roll_lanes(source[x, row], 1 - c)
                for b in range(3):
                    y = row + 1 - b
                    if 0 <= y < width_y:
                        first = (3 * b + c) * channels
                        right[x, first : first + channels, y * depth : (y + 1) * depth] = moved
    total = None
    for x in range(width_x):
        part = lax.dot_general(
            left[x * channels : (x + 3) * channels, :], right[x], NT, preferred_element_type=jnp.float32
        )
        total = part if total is None else total + part
    out[...] = total
    edge_rows(cells_at, width_x, kernel, 0, 0, down, columns, weights)
    edge_rows(cells_at, width_x, kernel, width_y - 1, 2, up, columns, weights)


def weight_kernel(order, inner, slope, x_near, x_far, far, near, out, left, right, gram, ordered):
    width_x, width_y, channels, depth = slope.shape
    cells_at = functools.partial(plane, slope, x_near, x_far, is_even("gx"))
    even = is_even("gy")
    sides = []
    for row in (0, width_y - 1):
        total = None
        for wide_x in range(width_x + 2):
            left[wide_x * channels : (wide_x + 1) * channels, :] = cells_at(wide_x, row)
        for x in range(width_x):
            cells = jnp.where(even, far[x], near[x]) if row == 0 else jnp.where(even, near[x], far[x])
            for c in range(3):
                right[c * channels : (c + 1) * channels, :] = roll_lanes(cells, 1 - c)
            part = lax.dot_general(
                left[x * channels : (x + 3) * channels, :], right[...], NT, preferred_element_type=jnp.float32
            )
            total = part if total is None else total + part
        sides.append(total)
    total = jnp.concatenate(
        [
            inner[:, : 3 * channels] + sides[0],
            inner[:, 3 * channels : 6 * channels],
            inner[:, 6 * channels :] + sides[1],
        ],
        axis=1,
    )
    for pair in range(5):
        lanes = total[:, 2 * pair * channels : min(2 * pair + 2, 9) * channels]
        gram[pair, :, : lanes.shape[1]] = lanes
    half = channels // 2
    first_half = lax.broadcasted_iota(jnp.int32, (half, 2 * channels), 1) < channels
    for a in range(3):
        top = (2 - a) * channels
        for pair in range(5):
            low = gram[pair, pl.ds(top, half, stride=2), :]
            high = gram[pair, pl.ds(top + 1, half, stride=2), :]
            tap = 9 * a + 2 * pair
            ordered[tap * half : (tap + 1) * half, :] = jnp.where(first_half, low, pltpu.roll(high, channels, axis=1))
            if pair < 4:
                tap += 1
                ordered[tap * half : (tap + 1) * half, :] = jnp.where(
                    first_half, pltpu.roll(low, channels, axis=1), high
                )
    if len(out.shape) == 4:
        rows = out.shape[2]
        for core in range(2):
            for slot, part in enumerate(order[core]):
                out[core, slot] = ordered[part * rows : (part + 1) * rows, :].astype(out.dtype)
    else:
        out[...] = ordered[...].astype(out.dtype)


def source_kernel(slope, x_near, x_far, far, near, kernel, out, columns, weights, spread):
    width_x, width_y, channels, depth = slope.shape
    cells_at = functools.partial(plane, slope, x_near, x_far, is_even("gx"))
    even = is_even("gy")
    zeros = jnp.zeros((channels, depth), slope.dtype)
    for wide_x in range(width_x + 2):
        for row in range(-1, width_y + 1):
            cells = cells_at(wide_x, row) if 0 <= row < width_y else zeros
            for b in range(3):
                y = row + b - 1
                if 0 <= y < width_y:
                    first = (3 * wide_x + b) * channels
                    columns[first : first + channels, y * depth : (y + 1) * depth] = cells
    for a in range(3):
        for b in range(3):
            for c in range(3):
                first = (3 * (2 - a) + b) * channels
                weights[c, first : first + channels, :] = kernel[9 * a + 3 * b + c]
    for x in range(width_x):
        cells = columns[3 * x * channels : 3 * (x + 3) * channels, :]
        for c in range(3):
            spread[c] = lax.dot_general(weights[c], cells, TN, preferred_element_type=jnp.float32)
        for y in range(width_y):
            lanes = slice(y * depth, (y + 1) * depth)
            total = gather([spread[c, :, lanes] for c in range(3)])
            if y == 0:
                total += jnp.where(even, far[x], near[x]).astype(jnp.float32)
            if y == width_y - 1:
                total += jnp.where(even, near[x], far[x]).astype(jnp.float32)
            out[x, y] = total.astype(out.dtype)


def on_device(source, preact, cotangent, kernel):
    channels, width_x, width_y, depth = source.shape
    devices = lax.axis_size("gx") * lax.axis_size("gy")
    cell_count = width_x * width_y * depth
    lines = 27 * channels * channels // 128
    pairs, count_y = lax.axis_size("gx") // 2, lax.axis_size("gy")
    share = (2, pairs * count_y, lines // devices, 128) if lines % devices == 0 else (lines, 128)
    places = [(i, j) for j in reversed(range(count_y)) for i in reversed(range(pairs))]
    order = [[(2 * i + core) * count_y + j for i, j in places] for core in range(2)]

    slope = jnp.where(preact > 0, cotangent, jnp.zeros_like(cotangent)).transpose(1, 2, 0, 3)
    src = source.transpose(1, 2, 0, 3)
    slope, src = lax.optimization_barrier((slope, src))
    x_near, x_far = swapped(slope[:1], slope[width_x - 1 :], "gx")
    src_near, src_far = swapped(src[:, 0], src[:, -1], "gy")

    cost = pl.CostEstimate(
        flops=54 * channels * channels * cell_count, bytes_accessed=2 * 1024 * 1024, transcendentals=0
    )
    vmem = pl.BlockSpec(memory_space=pltpu.VMEM)
    edge = jax.ShapeDtypeStruct((width_x, channels, depth), jnp.bfloat16)
    inner, down, up = pl.pallas_call(
        inner_kernel,
        out_shape=(jax.ShapeDtypeStruct((3 * channels, 9 * channels), jnp.float32), edge, edge),
        in_specs=[vmem] * 5,
        out_specs=(vmem, vmem, vmem),
        scratch_shapes=[
            pltpu.VMEM(((width_x + 2) * channels, width_y * depth), jnp.bfloat16),
            pltpu.VMEM((width_x, 9 * channels, width_y * depth), jnp.bfloat16),
            pltpu.VMEM(((width_x + 2) * channels, depth), jnp.bfloat16),
            pltpu.VMEM((3, 3 * channels, channels), jnp.bfloat16),
        ],
        compiler_params=PARAMS,
        cost_estimate=cost,
        name="weight_inner",
    )(slope, x_near, x_far, src, kernel)
    partial = pl.pallas_call(
        functools.partial(weight_kernel, order),
        out_shape=jax.ShapeDtypeStruct(share, jnp.bfloat16),
        in_specs=[vmem] * 6,
        out_specs=vmem,
        scratch_shapes=[
            pltpu.VMEM(((width_x + 2) * channels, depth), jnp.bfloat16),
            pltpu.VMEM((3 * channels, depth), jnp.bfloat16),
            pltpu.VMEM((5, 3 * channels, 2 * channels), jnp.float32),
            pltpu.VMEM((lines, 128), jnp.float32),
        ],
        compiler_params=PARAMS,
        cost_estimate=cost,
        name="weight_grad",
    )(inner, slope, x_near, x_far, src_far, src_near)
    near, far = swapped(down, up, "gy")
    if len(share) == 2:
        partial = partial.reshape(devices, -1)[jnp.array(order)]
    even = is_even("gx")
    swap = [(i, i ^ 1) for i in range(2 * pairs)]
    other = lax.ppermute(jnp.where(even, partial[1], partial[0]), "gx", swap)
    own = jnp.where(even, partial[0], partial[1])
    both = (own.astype(jnp.float32) + other.astype(jnp.float32)).astype(jnp.bfloat16)
    shares = lax.all_to_all(both, ("gx", "gy"), 0, 0, axis_index_groups=order, tiled=True)
    norm_scale = 1.0 / math.sqrt(cell_count * devices)
    grad_kernel = (jnp.sum(shares.astype(jnp.float32), axis=0) * norm_scale).reshape(-1)

    grad_source = pl.pallas_call(
        source_kernel,
        out_shape=jax.ShapeDtypeStruct(slope.shape, jnp.bfloat16),
        in_specs=[vmem] * 6,
        out_specs=vmem,
        scratch_shapes=[
            pltpu.VMEM((3 * (width_x + 2) * channels, width_y * depth), jnp.bfloat16),
            pltpu.VMEM((3, 9 * channels, channels), jnp.bfloat16),
            pltpu.VMEM((3, channels, width_y * depth), jnp.float32),
        ],
        compiler_params=PARAMS,
        cost_estimate=pl.CostEstimate(
            flops=5400 * channels * channels * cell_count, bytes_accessed=2 * 1024 * 1024, transcendentals=0
        ),
        name="source_grad",
    )(slope, x_near, x_far, far, near, kernel)
    return (grad_source.transpose(2, 0, 1, 3), grad_kernel)


def solution(mesh):
    placed = (P(None, "gx", "gy", None), P(None, "gx", "gy", None), P(None, "gx", "gy", None), P())
    return jax.shard_map(
        on_device,
        mesh=mesh,
        in_specs=placed,
        out_specs=(P(None, "gx", "gy", None), P(("gx", "gy"))),
        check_vma=False,
    )
```

```python
import functools
import math

import jax
import jax.numpy as jnp
from jax import lax
from jax.experimental import pallas as pl
from jax.experimental.pallas import tpu as pltpu
from jax.sharding import PartitionSpec as P

NT = (((1,), (1,)), ((), ()))
TN = (((0,), (0,)), ((), ()))
PARAMS = pltpu.CompilerParams(vmem_limit_bytes=32 * 1024 * 1024)


def is_even(axis):
    return lax.axis_index(axis) & 1 == 0


def swapped(first, last, axis):
    count = lax.axis_size(axis)
    even = is_even(axis)
    near = [(i, i ^ 1) for i in range(count)]
    far = [(i, (i - 1) % count if i % 2 == 0 else (i + 1) % count) for i in range(count)]
    got_far = lax.ppermute(jnp.where(even, first, last), axis, far)
    got_near = lax.ppermute(jnp.where(even, last, first), axis, near)
    return got_near, got_far


def roll_lanes(block, step):
    if step == 0:
        return block
    return pltpu.roll(block.astype(jnp.float32), step % block.shape[-1], axis=1).astype(block.dtype)


def plane(slope, near, far, even, wide_x, row):
    if wide_x == 0:
        return jnp.where(even, far[0, row], near[0, row])
    if wide_x == slope.shape[0] + 1:
        return jnp.where(even, near[0, row], far[0, row])
    return slope[wide_x - 1, row]


def gather(parts):
    depth = parts[1].shape[1]
    return parts[1] + pltpu.roll(parts[0], depth - 1, axis=1) + pltpu.roll(parts[2], 1, axis=1)


def edge_rows(cells_at, width_x, kernel, row, b, out, columns, weights):
    channels = kernel.shape[1]
    for wide_x in range(width_x + 2):
        columns[wide_x * channels : (wide_x + 1) * channels, :] = cells_at(wide_x, row)
    for a in range(3):
        for c in range(3):
            weights[c, (2 - a) * channels : (3 - a) * channels, :] = kernel[9 * a + 3 * b + c]
    for x in range(width_x):
        cells = columns[x * channels : (x + 3) * channels, :]
        parts = [lax.dot_general(weights[c], cells, TN, preferred_element_type=jnp.float32) for c in range(3)]
        out[x] = gather(parts).astype(out.dtype)


def inner_kernel(slope, x_near, x_far, source, kernel, out, down, up, left, right, columns, weights):
    width_x, width_y, channels, depth = slope.shape
    cells_at = functools.partial(plane, slope, x_near, x_far, is_even("gx"))
    for wide_x in range(width_x + 2):
        for y in range(width_y):
            left[wide_x * channels : (wide_x + 1) * channels, y * depth : (y + 1) * depth] = cells_at(wide_x, y)
    zeros = jnp.zeros((3 * channels, depth), source.dtype)
    for x in range(width_x):
        right[x, 0 : 3 * channels, 0:depth] = zeros
        right[x, 6 * channels :, (width_y - 1) * depth :] = zeros
        for row in range(width_y):
            for c in range(3):
                moved = roll_lanes(source[x, row], 1 - c)
                for b in range(3):
                    y = row + 1 - b
                    if 0 <= y < width_y:
                        first = (3 * b + c) * channels
                        right[x, first : first + channels, y * depth : (y + 1) * depth] = moved
    total = None
    for x in range(width_x):
        part = lax.dot_general(
            left[x * channels : (x + 3) * channels, :], right[x], NT, preferred_element_type=jnp.float32
        )
        total = part if total is None else total + part
    out[...] = total
    edge_rows(cells_at, width_x, kernel, 0, 0, down, columns, weights)
    edge_rows(cells_at, width_x, kernel, width_y - 1, 2, up, columns, weights)


def weight_kernel(order, inner, slope, x_near, x_far, far, near, out, left, right, gram, ordered):
    width_x, width_y, channels, depth = slope.shape
    cells_at = functools.partial(plane, slope, x_near, x_far, is_even("gx"))
    even = is_even("gy")
    sides = []
    for row in (0, width_y - 1):
        total = None
        for wide_x in range(width_x + 2):
            left[wide_x * channels : (wide_x + 1) * channels, :] = cells_at(wide_x, row)
        for x in range(width_x):
            cells = jnp.where(even, far[x], near[x]) if row == 0 else jnp.where(even, near[x], far[x])
            for c in range(3):
                right[c * channels : (c + 1) * channels, :] = roll_lanes(cells, 1 - c)
            part = lax.dot_general(
                left[x * channels : (x + 3) * channels, :], right[...], NT, preferred_element_type=jnp.float32
            )
            total = part if total is None else total + part
        sides.append(total)
    total = jnp.concatenate(
        [
            inner[:, : 3 * channels] + sides[0],
            inner[:, 3 * channels : 6 * channels],
            inner[:, 6 * channels :] + sides[1],
        ],
        axis=1,
    )
    for pair in range(5):
        lanes = total[:, 2 * pair * channels : min(2 * pair + 2, 9) * channels]
        gram[pair, :, : lanes.shape[1]] = lanes
    half = channels // 2
    first_half = lax.broadcasted_iota(jnp.int32, (half, 2 * channels), 1) < channels
    for a in range(3):
        top = (2 - a) * channels
        for pair in range(5):
            low = gram[pair, pl.ds(top, half, stride=2), :]
            high = gram[pair, pl.ds(top + 1, half, stride=2), :]
            tap = 9 * a + 2 * pair
            ordered[tap * half : (tap + 1) * half, :] = jnp.where(first_half, low, pltpu.roll(high, channels, axis=1))
            if pair < 4:
                tap += 1
                ordered[tap * half : (tap + 1) * half, :] = jnp.where(
                    first_half, pltpu.roll(low, channels, axis=1), high
                )
    if len(out.shape) == 4:
        rows = out.shape[2]
        for core in range(2):
            for slot, part in enumerate(order[core]):
                out[core, slot] = ordered[part * rows : (part + 1) * rows, :].astype(out.dtype)
    else:
        out[...] = ordered[...].astype(out.dtype)


def source_kernel(slope, x_near, x_far, far, near, kernel, out, columns, weights, spread):
    width_x, width_y, channels, depth = slope.shape
    cells_at = functools.partial(plane, slope, x_near, x_far, is_even("gx"))
    even = is_even("gy")
    zeros = jnp.zeros((channels, depth), slope.dtype)
    for wide_x in range(width_x + 2):
        for row in range(-1, width_y + 1):
            cells = cells_at(wide_x, row) if 0 <= row < width_y else zeros
            for b in range(3):
                y = row + b - 1
                if 0 <= y < width_y:
                    first = (3 * wide_x + b) * channels
                    columns[first : first + channels, y * depth : (y + 1) * depth] = cells
    for a in range(3):
        for b in range(3):
            for c in range(3):
                first = (3 * (2 - a) + b) * channels
                weights[c, first : first + channels, :] = kernel[9 * a + 3 * b + c]
    for x in range(width_x):
        cells = columns[3 * x * channels : 3 * (x + 3) * channels, :]
        for c in range(3):
            spread[c] = lax.dot_general(weights[c], cells, TN, preferred_element_type=jnp.float32)
        for y in range(width_y):
            lanes = slice(y * depth, (y + 1) * depth)
            total = gather([spread[c, :, lanes] for c in range(3)])
            if y == 0:
                total += jnp.where(even, far[x], near[x]).astype(jnp.float32)
            if y == width_y - 1:
                total += jnp.where(even, near[x], far[x]).astype(jnp.float32)
            out[x, y] = total.astype(out.dtype)


def on_device(source, preact, cotangent, kernel):
    channels, width_x, width_y, depth = source.shape
    devices = lax.axis_size("gx") * lax.axis_size("gy")
    cell_count = width_x * width_y * depth
    lines = 27 * channels * channels // 128
    pairs, count_y = lax.axis_size("gx") // 2, lax.axis_size("gy")
    share = (2, pairs * count_y, lines // devices, 128) if lines % devices == 0 else (lines, 128)
    places = [((i + pairs // 2) % pairs, j) for j in [*range(count_y - 1, 1, -1), 0, 1][-count_y:] for i in range(pairs)]
    order = [[(2 * i + core) * count_y + j for i, j in places] for core in range(2)]

    slope = jnp.where(preact > 0, cotangent, jnp.zeros_like(cotangent)).transpose(1, 2, 0, 3)
    src = source.transpose(1, 2, 0, 3)
    slope, src = lax.optimization_barrier((slope, src))
    x_near, x_far = swapped(slope[:1], slope[width_x - 1 :], "gx")
    src_near, src_far = swapped(src[:, 0], src[:, -1], "gy")

    cost = pl.CostEstimate(
        flops=54 * channels * channels * cell_count, bytes_accessed=2 * 1024 * 1024, transcendentals=0
    )
    vmem = pl.BlockSpec(memory_space=pltpu.VMEM)
    edge = jax.ShapeDtypeStruct((width_x, channels, depth), jnp.bfloat16)
    inner, down, up = pl.pallas_call(
        inner_kernel,
        out_shape=(jax.ShapeDtypeStruct((3 * channels, 9 * channels), jnp.float32), edge, edge),
        in_specs=[vmem] * 5,
        out_specs=(vmem, vmem, vmem),
        scratch_shapes=[
            pltpu.VMEM(((width_x + 2) * channels, width_y * depth), jnp.bfloat16),
            pltpu.VMEM((width_x, 9 * channels, width_y * depth), jnp.bfloat16),
            pltpu.VMEM(((width_x + 2) * channels, depth), jnp.bfloat16),
            pltpu.VMEM((3, 3 * channels, channels), jnp.bfloat16),
        ],
        compiler_params=PARAMS,
        cost_estimate=cost,
        name="weight_inner",
    )(slope, x_near, x_far, src, kernel)
    partial = pl.pallas_call(
        functools.partial(weight_kernel, order),
        out_shape=jax.ShapeDtypeStruct(share, jnp.bfloat16),
        in_specs=[vmem] * 6,
        out_specs=vmem,
        scratch_shapes=[
            pltpu.VMEM(((width_x + 2) * channels, depth), jnp.bfloat16),
            pltpu.VMEM((3 * channels, depth), jnp.bfloat16),
            pltpu.VMEM((5, 3 * channels, 2 * channels), jnp.float32),
            pltpu.VMEM((lines, 128), jnp.float32),
        ],
        compiler_params=PARAMS,
        cost_estimate=cost,
        name="weight_grad",
    )(inner, slope, x_near, x_far, src_far, src_near)
    near, far = swapped(down, up, "gy")
    if len(share) == 2:
        partial = partial.reshape(devices, -1)[jnp.array(order)]
    even = is_even("gx")
    swap = [(i, i ^ 1) for i in range(2 * pairs)]
    other = lax.ppermute(jnp.where(even, partial[1], partial[0]), "gx", swap)
    own = jnp.where(even, partial[0], partial[1])
    both = (own.astype(jnp.float32) + other.astype(jnp.float32)).astype(jnp.bfloat16)
    shares = lax.all_to_all(both, ("gx", "gy"), 0, 0, axis_index_groups=order, tiled=True)
    norm_scale = 1.0 / math.sqrt(cell_count * devices)
    grad_kernel = (jnp.sum(shares.astype(jnp.float32), axis=0) * norm_scale).reshape(-1)

    grad_source = pl.pallas_call(
        source_kernel,
        out_shape=jax.ShapeDtypeStruct(slope.shape, jnp.bfloat16),
        in_specs=[vmem] * 6,
        out_specs=vmem,
        scratch_shapes=[
            pltpu.VMEM((3 * (width_x + 2) * channels, width_y * depth), jnp.bfloat16),
            pltpu.VMEM((3, 9 * channels, channels), jnp.bfloat16),
            pltpu.VMEM((3, channels, width_y * depth), jnp.float32),
        ],
        compiler_params=PARAMS,
        cost_estimate=pl.CostEstimate(
            flops=5400 * channels * channels * cell_count, bytes_accessed=2 * 1024 * 1024, transcendentals=0
        ),
        name="source_grad",
    )(slope, x_near, x_far, far, near, kernel)
    return (grad_source.transpose(2, 0, 1, 3), grad_kernel)


def solution(mesh):
    placed = (P(None, "gx", "gy", None), P(None, "gx", "gy", None), P(None, "gx", "gy", None), P())
    return jax.shard_map(
        on_device,
        mesh=mesh,
        in_specs=placed,
        out_specs=(P(None, "gx", "gy", None), P(("gx", "gy"))),
        check_vma=False,
    )
```

```python
import functools
import math

import jax
import jax.numpy as jnp
from jax import lax
from jax.experimental import pallas as pl
from jax.experimental.pallas import tpu as pltpu
from jax.sharding import PartitionSpec as P

NT = (((1,), (1,)), ((), ()))
TN = (((0,), (0,)), ((), ()))
PARAMS = pltpu.CompilerParams(vmem_limit_bytes=32 * 1024 * 1024)


def is_even(axis):
    return lax.axis_index(axis) & 1 == 0


def swapped(first, last, axis):
    count = lax.axis_size(axis)
    even = is_even(axis)
    near = [(i, i ^ 1) for i in range(count)]
    far = [(i, (i - 1) % count if i % 2 == 0 else (i + 1) % count) for i in range(count)]
    got_far = lax.ppermute(jnp.where(even, first, last), axis, far)
    got_near = lax.ppermute(jnp.where(even, last, first), axis, near)
    return got_near, got_far


def roll_lanes(block, step):
    if step == 0:
        return block
    return pltpu.roll(block.astype(jnp.float32), step % block.shape[-1], axis=1).astype(block.dtype)


def plane(slope, near, far, even, wide_x, row):
    if wide_x == 0:
        return jnp.where(even, far[0, row], near[0, row])
    if wide_x == slope.shape[0] + 1:
        return jnp.where(even, near[0, row], far[0, row])
    return slope[wide_x - 1, row]


def gather(parts):
    depth = parts[1].shape[1]
    return parts[1] + pltpu.roll(parts[0], depth - 1, axis=1) + pltpu.roll(parts[2], 1, axis=1)


def edge_rows(cells_at, width_x, kernel, row, b, out, columns, weights):
    channels = kernel.shape[1]
    for wide_x in range(width_x + 2):
        columns[wide_x * channels : (wide_x + 1) * channels, :] = cells_at(wide_x, row)
    for a in range(3):
        for c in range(3):
            weights[c, (2 - a) * channels : (3 - a) * channels, :] = kernel[9 * a + 3 * b + c]
    for x in range(width_x):
        cells = columns[x * channels : (x + 3) * channels, :]
        parts = [lax.dot_general(weights[c], cells, TN, preferred_element_type=jnp.float32) for c in range(3)]
        out[x] = gather(parts).astype(out.dtype)


def inner_kernel(slope, x_near, x_far, source, kernel, out, down, up, left, right, columns, weights):
    width_x, width_y, channels, depth = slope.shape
    cells_at = functools.partial(plane, slope, x_near, x_far, is_even("gx"))
    for wide_x in range(width_x + 2):
        for y in range(width_y):
            left[wide_x * channels : (wide_x + 1) * channels, y * depth : (y + 1) * depth] = cells_at(wide_x, y)
    zeros = jnp.zeros((3 * channels, depth), source.dtype)
    for x in range(width_x):
        right[x, 0 : 3 * channels, 0:depth] = zeros
        right[x, 6 * channels :, (width_y - 1) * depth :] = zeros
        for row in range(width_y):
            for c in range(3):
                moved = roll_lanes(source[x, row], 1 - c)
                for b in range(3):
                    y = row + 1 - b
                    if 0 <= y < width_y:
                        first = (3 * b + c) * channels
                        right[x, first : first + channels, y * depth : (y + 1) * depth] = moved
    total = None
    for x in range(width_x):
        part = lax.dot_general(
            left[x * channels : (x + 3) * channels, :], right[x], NT, preferred_element_type=jnp.float32
        )
        total = part if total is None else total + part
    out[...] = total
    edge_rows(cells_at, width_x, kernel, 0, 0, down, columns, weights)
    edge_rows(cells_at, width_x, kernel, width_y - 1, 2, up, columns, weights)


def weight_kernel(order, inner, slope, x_near, x_far, far, near, out, left, right, gram, ordered):
    width_x, width_y, channels, depth = slope.shape
    cells_at = functools.partial(plane, slope, x_near, x_far, is_even("gx"))
    even = is_even("gy")
    sides = []
    for row in (0, width_y - 1):
        total = None
        for wide_x in range(width_x + 2):
            left[wide_x * channels : (wide_x + 1) * channels, :] = cells_at(wide_x, row)
        for x in range(width_x):
            cells = jnp.where(even, far[x], near[x]) if row == 0 else jnp.where(even, near[x], far[x])
            for c in range(3):
                right[c * channels : (c + 1) * channels, :] = roll_lanes(cells, 1 - c)
            part = lax.dot_general(
                left[x * channels : (x + 3) * channels, :], right[...], NT, preferred_element_type=jnp.float32
            )
            total = part if total is None else total + part
        sides.append(total)
    total = jnp.concatenate(
        [
            inner[:, : 3 * channels] + sides[0],
            inner[:, 3 * channels : 6 * channels],
            inner[:, 6 * channels :] + sides[1],
        ],
        axis=1,
    )
    for pair in range(5):
        lanes = total[:, 2 * pair * channels : min(2 * pair + 2, 9) * channels]
        gram[pair, :, : lanes.shape[1]] = lanes
    half = channels // 2
    first_half = lax.broadcasted_iota(jnp.int32, (half, 2 * channels), 1) < channels
    for a in range(3):
        top = (2 - a) * channels
        for pair in range(5):
            low = gram[pair, pl.ds(top, half, stride=2), :]
            high = gram[pair, pl.ds(top + 1, half, stride=2), :]
            tap = 9 * a + 2 * pair
            ordered[tap * half : (tap + 1) * half, :] = jnp.where(first_half, low, pltpu.roll(high, channels, axis=1))
            if pair < 4:
                tap += 1
                ordered[tap * half : (tap + 1) * half, :] = jnp.where(
                    first_half, pltpu.roll(low, channels, axis=1), high
                )
    if len(out.shape) == 4:
        rows = out.shape[2]
        for core in range(2):
            for slot, part in enumerate(order[core]):
                out[core, slot] = ordered[part * rows : (part + 1) * rows, :].astype(out.dtype)
    else:
        out[...] = ordered[...].astype(out.dtype)


def source_kernel(slope, x_near, x_far, far, near, kernel, out, columns, weights, spread):
    width_x, width_y, channels, depth = slope.shape
    cells_at = functools.partial(plane, slope, x_near, x_far, is_even("gx"))
    even = is_even("gy")
    zeros = jnp.zeros((channels, depth), slope.dtype)
    for wide_x in range(width_x + 2):
        for row in range(-1, width_y + 1):
            cells = cells_at(wide_x, row) if 0 <= row < width_y else zeros
            for b in range(3):
                y = row + b - 1
                if 0 <= y < width_y:
                    first = (3 * wide_x + b) * channels
                    columns[first : first + channels, y * depth : (y + 1) * depth] = cells
    for a in range(3):
        for b in range(3):
            for c in range(3):
                first = (3 * (2 - a) + b) * channels
                weights[c, first : first + channels, :] = kernel[9 * a + 3 * b + c]
    for x in range(width_x):
        cells = columns[3 * x * channels : 3 * (x + 3) * channels, :]
        for c in range(3):
            spread[c] = lax.dot_general(weights[c], cells, TN, preferred_element_type=jnp.float32)
        for y in range(width_y):
            lanes = slice(y * depth, (y + 1) * depth)
            total = gather([spread[c, :, lanes] for c in range(3)])
            if y == 0:
                total += jnp.where(even, far[x], near[x]).astype(jnp.float32)
            if y == width_y - 1:
                total += jnp.where(even, near[x], far[x]).astype(jnp.float32)
            out[x, y] = total.astype(out.dtype)


def on_device(source, preact, cotangent, kernel):
    channels, width_x, width_y, depth = source.shape
    devices = lax.axis_size("gx") * lax.axis_size("gy")
    cell_count = width_x * width_y * depth
    lines = 27 * channels * channels // 128
    pairs, count_y = lax.axis_size("gx") // 2, lax.axis_size("gy")
    share = (2, pairs * count_y, lines // devices, 128) if lines % devices == 0 else (lines, 128)
    places = [(i, (i + step) % count_y) for step in range(count_y) for i in range(pairs)][::-1]
    order = [[(2 * i + core) * count_y + j for i, j in places] for core in range(2)]

    slope = jnp.where(preact > 0, cotangent, jnp.zeros_like(cotangent)).transpose(1, 2, 0, 3)
    src = source.transpose(1, 2, 0, 3)
    slope, src = lax.optimization_barrier((slope, src))
    x_near, x_far = swapped(slope[:1], slope[width_x - 1 :], "gx")
    src_near, src_far = swapped(src[:, 0], src[:, -1], "gy")

    cost = pl.CostEstimate(
        flops=54 * channels * channels * cell_count, bytes_accessed=2 * 1024 * 1024, transcendentals=0
    )
    vmem = pl.BlockSpec(memory_space=pltpu.VMEM)
    edge = jax.ShapeDtypeStruct((width_x, channels, depth), jnp.bfloat16)
    inner, down, up = pl.pallas_call(
        inner_kernel,
        out_shape=(jax.ShapeDtypeStruct((3 * channels, 9 * channels), jnp.float32), edge, edge),
        in_specs=[vmem] * 5,
        out_specs=(vmem, vmem, vmem),
        scratch_shapes=[
            pltpu.VMEM(((width_x + 2) * channels, width_y * depth), jnp.bfloat16),
            pltpu.VMEM((width_x, 9 * channels, width_y * depth), jnp.bfloat16),
            pltpu.VMEM(((width_x + 2) * channels, depth), jnp.bfloat16),
            pltpu.VMEM((3, 3 * channels, channels), jnp.bfloat16),
        ],
        compiler_params=PARAMS,
        cost_estimate=cost,
        name="weight_inner",
    )(slope, x_near, x_far, src, kernel)
    partial = pl.pallas_call(
        functools.partial(weight_kernel, order),
        out_shape=jax.ShapeDtypeStruct(share, jnp.bfloat16),
        in_specs=[vmem] * 6,
        out_specs=vmem,
        scratch_shapes=[
            pltpu.VMEM(((width_x + 2) * channels, depth), jnp.bfloat16),
            pltpu.VMEM((3 * channels, depth), jnp.bfloat16),
            pltpu.VMEM((5, 3 * channels, 2 * channels), jnp.float32),
            pltpu.VMEM((lines, 128), jnp.float32),
        ],
        compiler_params=PARAMS,
        cost_estimate=cost,
        name="weight_grad",
    )(inner, slope, x_near, x_far, src_far, src_near)
    near, far = swapped(down, up, "gy")
    if len(share) == 2:
        partial = partial.reshape(devices, -1)[jnp.array(order)]
    even = is_even("gx")
    swap = [(i, i ^ 1) for i in range(2 * pairs)]
    other = lax.ppermute(jnp.where(even, partial[1], partial[0]), "gx", swap)
    own = jnp.where(even, partial[0], partial[1])
    both = (own.astype(jnp.float32) + other.astype(jnp.float32)).astype(jnp.bfloat16)
    shares = lax.all_to_all(both, ("gx", "gy"), 0, 0, axis_index_groups=order, tiled=True)
    norm_scale = 1.0 / math.sqrt(cell_count * devices)
    grad_kernel = (jnp.sum(shares.astype(jnp.float32), axis=0) * norm_scale).reshape(-1)

    grad_source = pl.pallas_call(
        source_kernel,
        out_shape=jax.ShapeDtypeStruct(slope.shape, jnp.bfloat16),
        in_specs=[vmem] * 6,
        out_specs=vmem,
        scratch_shapes=[
            pltpu.VMEM((3 * (width_x + 2) * channels, width_y * depth), jnp.bfloat16),
            pltpu.VMEM((3, 9 * channels, channels), jnp.bfloat16),
            pltpu.VMEM((3, channels, width_y * depth), jnp.float32),
        ],
        compiler_params=PARAMS,
        cost_estimate=pl.CostEstimate(
            flops=5400 * channels * channels * cell_count, bytes_accessed=2 * 1024 * 1024, transcendentals=0
        ),
        name="source_grad",
    )(slope, x_near, x_far, far, near, kernel)
    return (grad_source.transpose(2, 0, 1, 3), grad_kernel)


def solution(mesh):
    placed = (P(None, "gx", "gy", None), P(None, "gx", "gy", None), P(None, "gx", "gy", None), P())
    return jax.shard_map(
        on_device,
        mesh=mesh,
        in_specs=placed,
        out_specs=(P(None, "gx", "gy", None), P(("gx", "gy"))),
        check_vma=False,
    )
```

```python
import functools
import math

import jax
import jax.numpy as jnp
from jax import lax
from jax.experimental import pallas as pl
from jax.experimental.pallas import tpu as pltpu
from jax.sharding import PartitionSpec as P

NT = (((1,), (1,)), ((), ()))
TN = (((0,), (0,)), ((), ()))
PARAMS = pltpu.CompilerParams(vmem_limit_bytes=32 * 1024 * 1024)


def is_even(axis):
    return lax.axis_index(axis) & 1 == 0


def swapped(first, last, axis):
    count = lax.axis_size(axis)
    even = is_even(axis)
    near = [(i, i ^ 1) for i in range(count)]
    far = [(i, (i - 1) % count if i % 2 == 0 else (i + 1) % count) for i in range(count)]
    got_far = lax.ppermute(jnp.where(even, first, last), axis, far)
    got_near = lax.ppermute(jnp.where(even, last, first), axis, near)
    return got_near, got_far


def roll_lanes(block, step):
    if step == 0:
        return block
    return pltpu.roll(block.astype(jnp.float32), step % block.shape[-1], axis=1).astype(block.dtype)


def plane(slope, near, far, even, wide_x, row):
    if wide_x == 0:
        return jnp.where(even, far[0, row], near[0, row])
    if wide_x == slope.shape[0] + 1:
        return jnp.where(even, near[0, row], far[0, row])
    return slope[wide_x - 1, row]


def gather(parts):
    depth = parts[1].shape[1]
    return parts[1] + pltpu.roll(parts[0], depth - 1, axis=1) + pltpu.roll(parts[2], 1, axis=1)


def edge_rows(cells_at, width_x, kernel, row, b, out, columns, weights):
    channels = kernel.shape[1]
    for wide_x in range(width_x + 2):
        columns[wide_x * channels : (wide_x + 1) * channels, :] = cells_at(wide_x, row)
    for a in range(3):
        for c in range(3):
            weights[c, (2 - a) * channels : (3 - a) * channels, :] = kernel[9 * a + 3 * b + c]
    for x in range(width_x):
        cells = columns[x * channels : (x + 3) * channels, :]
        parts = [lax.dot_general(weights[c], cells, TN, preferred_element_type=jnp.float32) for c in range(3)]
        out[x] = gather(parts).astype(out.dtype)


def inner_kernel(slope, x_near, x_far, source, kernel, out, down, up, left, right, columns, weights):
    width_x, width_y, channels, depth = slope.shape
    cells_at = functools.partial(plane, slope, x_near, x_far, is_even("gx"))
    for wide_x in range(width_x + 2):
        for y in range(width_y):
            left[wide_x * channels : (wide_x + 1) * channels, y * depth : (y + 1) * depth] = cells_at(wide_x, y)
    zeros = jnp.zeros((3 * channels, depth), source.dtype)
    for x in range(width_x):
        right[x, 0 : 3 * channels, 0:depth] = zeros
        right[x, 6 * channels :, (width_y - 1) * depth :] = zeros
        for row in range(width_y):
            for c in range(3):
                moved = roll_lanes(source[x, row], 1 - c)
                for b in range(3):
                    y = row + 1 - b
                    if 0 <= y < width_y:
                        first = (3 * b + c) * channels
                        right[x, first : first + channels, y * depth : (y + 1) * depth] = moved
    total = None
    for x in range(width_x):
        part = lax.dot_general(
            left[x * channels : (x + 3) * channels, :], right[x], NT, preferred_element_type=jnp.float32
        )
        total = part if total is None else total + part
    out[...] = total
    edge_rows(cells_at, width_x, kernel, 0, 0, down, columns, weights)
    edge_rows(cells_at, width_x, kernel, width_y - 1, 2, up, columns, weights)


def weight_kernel(order, inner, slope, x_near, x_far, near, far, out, left, right, gram, ordered):
    width_x, width_y, channels, depth = slope.shape
    cells_at = functools.partial(plane, slope, x_near, x_far, is_even("gx"))
    even = is_even("gy")
    sides = []
    for row in (0, width_y - 1):
        total = None
        for wide_x in range(width_x + 2):
            left[wide_x * channels : (wide_x + 1) * channels, :] = cells_at(wide_x, row)
        for x in range(width_x):
            cells = jnp.where(even, far[x], near[x]) if row == 0 else jnp.where(even, near[x], far[x])
            for c in range(3):
                right[c * channels : (c + 1) * channels, :] = roll_lanes(cells, 1 - c)
            part = lax.dot_general(
                left[x * channels : (x + 3) * channels, :], right[...], NT, preferred_element_type=jnp.float32
            )
            total = part if total is None else total + part
        sides.append(total)
    total = jnp.concatenate(
        [
            inner[:, : 3 * channels] + sides[0],
            inner[:, 3 * channels : 6 * channels],
            inner[:, 6 * channels :] + sides[1],
        ],
        axis=1,
    )
    for pair in range(5):
        lanes = total[:, 2 * pair * channels : min(2 * pair + 2, 9) * channels]
        gram[pair, :, : lanes.shape[1]] = lanes
    half = channels // 2
    first_half = lax.broadcasted_iota(jnp.int32, (half, 2 * channels), 1) < channels
    for a in range(3):
        top = (2 - a) * channels
        for pair in range(5):
            low = gram[pair, pl.ds(top, half, stride=2), :]
            high = gram[pair, pl.ds(top + 1, half, stride=2), :]
            tap = 9 * a + 2 * pair
            ordered[tap * half : (tap + 1) * half, :] = jnp.where(first_half, low, pltpu.roll(high, channels, axis=1))
            if pair < 4:
                tap += 1
                ordered[tap * half : (tap + 1) * half, :] = jnp.where(
                    first_half, pltpu.roll(low, channels, axis=1), high
                )
    if len(out.shape) == 4:
        rows = out.shape[2]
        for core in range(2):
            for slot, part in enumerate(order[core]):
                out[core, slot] = ordered[part * rows : (part + 1) * rows, :].astype(out.dtype)
    else:
        out[...] = ordered[...].astype(out.dtype)


def source_kernel(slope, x_near, x_far, far, near, kernel, out, columns, weights, spread):
    width_x, width_y, channels, depth = slope.shape
    cells_at = functools.partial(plane, slope, x_near, x_far, is_even("gx"))
    even = is_even("gy")
    zeros = jnp.zeros((channels, depth), slope.dtype)
    for wide_x in range(width_x + 2):
        for row in range(-1, width_y + 1):
            cells = cells_at(wide_x, row) if 0 <= row < width_y else zeros
            for b in range(3):
                y = row + b - 1
                if 0 <= y < width_y:
                    first = (3 * wide_x + b) * channels
                    columns[first : first + channels, y * depth : (y + 1) * depth] = cells
    for a in range(3):
        for b in range(3):
            for c in range(3):
                first = (3 * (2 - a) + b) * channels
                weights[c, first : first + channels, :] = kernel[9 * a + 3 * b + c]
    for x in range(width_x):
        cells = columns[3 * x * channels : 3 * (x + 3) * channels, :]
        for c in range(3):
            spread[c] = lax.dot_general(weights[c], cells, TN, preferred_element_type=jnp.float32)
        for y in range(width_y):
            lanes = slice(y * depth, (y + 1) * depth)
            total = gather([spread[c, :, lanes] for c in range(3)])
            if y == 0:
                total += jnp.where(even, far[x], near[x]).astype(jnp.float32)
            if y == width_y - 1:
                total += jnp.where(even, near[x], far[x]).astype(jnp.float32)
            out[x, y] = total.astype(out.dtype)


def on_device(source, preact, cotangent, kernel):
    channels, width_x, width_y, depth = source.shape
    devices = lax.axis_size("gx") * lax.axis_size("gy")
    cell_count = width_x * width_y * depth
    lines = 27 * channels * channels // 128
    pairs, count_y = lax.axis_size("gx") // 2, lax.axis_size("gy")
    share = (2, pairs * count_y, lines // devices, 128) if lines % devices == 0 else (lines, 128)
    places = [(i, (i + step) % count_y) for step in range(count_y) for i in range(pairs)][::-1]
    order = [[(2 * i + core) * count_y + j for i, j in places] for core in range(2)]

    slope = jnp.where(preact > 0, cotangent, jnp.zeros_like(cotangent)).transpose(1, 2, 0, 3)
    src = source.transpose(1, 2, 0, 3)
    slope, src = lax.optimization_barrier((slope, src))
    x_near, x_far = swapped(slope[:1], slope[width_x - 1 :], "gx")
    src_near, src_far = swapped(src[:, 0], src[:, -1], "gy")

    cost = pl.CostEstimate(
        flops=54 * channels * channels * cell_count, bytes_accessed=2 * 1024 * 1024, transcendentals=0
    )
    vmem = pl.BlockSpec(memory_space=pltpu.VMEM)
    edge = jax.ShapeDtypeStruct((width_x, channels, depth), jnp.bfloat16)
    inner, down, up = pl.pallas_call(
        inner_kernel,
        out_shape=(jax.ShapeDtypeStruct((3 * channels, 9 * channels), jnp.float32), edge, edge),
        in_specs=[vmem] * 5,
        out_specs=(vmem, vmem, vmem),
        scratch_shapes=[
            pltpu.VMEM(((width_x + 2) * channels, width_y * depth), jnp.bfloat16),
            pltpu.VMEM((width_x, 9 * channels, width_y * depth), jnp.bfloat16),
            pltpu.VMEM(((width_x + 2) * channels, depth), jnp.bfloat16),
            pltpu.VMEM((3, 3 * channels, channels), jnp.bfloat16),
        ],
        compiler_params=PARAMS,
        cost_estimate=cost,
        name="weight_inner",
    )(slope, x_near, x_far, src, kernel)
    partial = pl.pallas_call(
        functools.partial(weight_kernel, order),
        out_shape=jax.ShapeDtypeStruct(share, jnp.bfloat16),
        in_specs=[vmem] * 6,
        out_specs=vmem,
        scratch_shapes=[
            pltpu.VMEM(((width_x + 2) * channels, depth), jnp.bfloat16),
            pltpu.VMEM((3 * channels, depth), jnp.bfloat16),
            pltpu.VMEM((5, 3 * channels, 2 * channels), jnp.float32),
            pltpu.VMEM((lines, 128), jnp.float32),
        ],
        compiler_params=PARAMS,
        cost_estimate=cost,
        name="weight_grad",
    )(inner, slope, x_near, x_far, src_near, src_far)
    near, far = swapped(down, up, "gy")
    if len(share) == 2:
        partial = partial.reshape(devices, -1)[jnp.array(order)]
    even = is_even("gx")
    swap = [(i, i ^ 1) for i in range(2 * pairs)]
    other = lax.ppermute(jnp.where(even, partial[1], partial[0]), "gx", swap)
    own = jnp.where(even, partial[0], partial[1])
    both = (own.astype(jnp.float32) + other.astype(jnp.float32)).astype(jnp.bfloat16)
    shares = lax.all_to_all(both, ("gx", "gy"), 0, 0, axis_index_groups=order, tiled=True)
    norm_scale = 1.0 / math.sqrt(cell_count * devices)
    grad_kernel = (jnp.sum(shares.astype(jnp.float32), axis=0) * norm_scale).reshape(-1)

    grad_source = pl.pallas_call(
        source_kernel,
        out_shape=jax.ShapeDtypeStruct(slope.shape, jnp.bfloat16),
        in_specs=[vmem] * 6,
        out_specs=vmem,
        scratch_shapes=[
            pltpu.VMEM((3 * (width_x + 2) * channels, width_y * depth), jnp.bfloat16),
            pltpu.VMEM((3, 9 * channels, channels), jnp.bfloat16),
            pltpu.VMEM((3, channels, width_y * depth), jnp.float32),
        ],
        compiler_params=PARAMS,
        cost_estimate=pl.CostEstimate(
            flops=5400 * channels * channels * cell_count, bytes_accessed=2 * 1024 * 1024, transcendentals=0
        ),
        name="source_grad",
    )(slope, x_near, x_far, far, near, kernel)
    return (grad_source.transpose(2, 0, 1, 3), grad_kernel)


def solution(mesh):
    placed = (P(None, "gx", "gy", None), P(None, "gx", "gy", None), P(None, "gx", "gy", None), P())
    return jax.shard_map(
        on_device,
        mesh=mesh,
        in_specs=placed,
        out_specs=(P(None, "gx", "gy", None), P(("gx", "gy"))),
        check_vma=False,
    )
```

```python
import functools
import math

import jax
import jax.numpy as jnp
from jax import lax
from jax.experimental import pallas as pl
from jax.experimental.pallas import tpu as pltpu
from jax.sharding import PartitionSpec as P

NT = (((1,), (1,)), ((), ()))
TN = (((0,), (0,)), ((), ()))
PARAMS = pltpu.CompilerParams(vmem_limit_bytes=32 * 1024 * 1024)


def is_even(axis):
    return lax.axis_index(axis) & 1 == 0


def swapped(first, last, axis):
    count = lax.axis_size(axis)
    even = is_even(axis)
    near = [(i, i ^ 1) for i in range(count)]
    far = [(i, (i - 1) % count if i % 2 == 0 else (i + 1) % count) for i in range(count)]
    got_far = lax.ppermute(jnp.where(even, first, last), axis, far)
    got_near = lax.ppermute(jnp.where(even, last, first), axis, near)
    return got_near, got_far


def roll_lanes(block, step):
    if step == 0:
        return block
    return pltpu.roll(block.astype(jnp.float32), step % block.shape[-1], axis=1).astype(block.dtype)


def plane(slope, near, far, even, wide_x, row):
    if wide_x == 0:
        return jnp.where(even, far[0, row], near[0, row])
    if wide_x == slope.shape[0] + 1:
        return jnp.where(even, near[0, row], far[0, row])
    return slope[wide_x - 1, row]


def gather(parts):
    depth = parts[1].shape[1]
    return parts[1] + pltpu.roll(parts[0], depth - 1, axis=1) + pltpu.roll(parts[2], 1, axis=1)


def edge_rows(cells_at, width_x, kernel, row, b, out, columns, weights):
    channels = kernel.shape[1]
    for wide_x in range(width_x + 2):
        columns[wide_x * channels : (wide_x + 1) * channels, :] = cells_at(wide_x, row)
    for a in range(3):
        for c in range(3):
            weights[c, (2 - a) * channels : (3 - a) * channels, :] = kernel[9 * a + 3 * b + c]
    for x in range(width_x):
        cells = columns[x * channels : (x + 3) * channels, :]
        parts = [lax.dot_general(weights[c], cells, TN, preferred_element_type=jnp.float32) for c in range(3)]
        out[x] = gather(parts).astype(out.dtype)


def inner_kernel(slope, x_near, x_far, source, kernel, out, down, up, left, right, columns, weights):
    width_x, width_y, channels, depth = slope.shape
    cells_at = functools.partial(plane, slope, x_near, x_far, is_even("gx"))
    for wide_x in range(width_x + 2):
        for y in range(width_y):
            left[wide_x * channels : (wide_x + 1) * channels, y * depth : (y + 1) * depth] = cells_at(wide_x, y)
    zeros = jnp.zeros((3 * channels, depth), source.dtype)
    for x in range(width_x):
        right[x, 0 : 3 * channels, 0:depth] = zeros
        right[x, 6 * channels :, (width_y - 1) * depth :] = zeros
        for row in range(width_y):
            for c in range(3):
                moved = roll_lanes(source[x, row], 1 - c)
                for b in range(3):
                    y = row + 1 - b
                    if 0 <= y < width_y:
                        first = (3 * b + c) * channels
                        right[x, first : first + channels, y * depth : (y + 1) * depth] = moved
    total = None
    for x in range(width_x):
        part = lax.dot_general(
            left[x * channels : (x + 3) * channels, :], right[x], NT, preferred_element_type=jnp.float32
        )
        total = part if total is None else total + part
    out[...] = total
    edge_rows(cells_at, width_x, kernel, 0, 0, down, columns, weights)
    edge_rows(cells_at, width_x, kernel, width_y - 1, 2, up, columns, weights)


def weight_kernel(order, inner, slope, x_near, x_far, near, far, out, left, right, gram, ordered):
    width_x, width_y, channels, depth = slope.shape
    cells_at = functools.partial(plane, slope, x_near, x_far, is_even("gx"))
    even = is_even("gy")
    sides = []
    for row in (0, width_y - 1):
        total = None
        for wide_x in range(width_x + 2):
            left[wide_x * channels : (wide_x + 1) * channels, :] = cells_at(wide_x, row)
        for x in range(width_x):
            cells = jnp.where(even, far[x], near[x]) if row == 0 else jnp.where(even, near[x], far[x])
            for c in range(3):
                right[c * channels : (c + 1) * channels, :] = roll_lanes(cells, 1 - c)
            part = lax.dot_general(
                left[x * channels : (x + 3) * channels, :], right[...], NT, preferred_element_type=jnp.float32
            )
            total = part if total is None else total + part
        sides.append(total)
    total = jnp.concatenate(
        [
            inner[:, : 3 * channels] + sides[0],
            inner[:, 3 * channels : 6 * channels],
            inner[:, 6 * channels :] + sides[1],
        ],
        axis=1,
    )
    for pair in range(5):
        lanes = total[:, 2 * pair * channels : min(2 * pair + 2, 9) * channels]
        gram[pair, :, : lanes.shape[1]] = lanes
    half = channels // 2
    first_half = lax.broadcasted_iota(jnp.int32, (half, 2 * channels), 1) < channels
    for a in range(3):
        top = (2 - a) * channels
        for pair in range(5):
            low = gram[pair, pl.ds(top, half, stride=2), :]
            high = gram[pair, pl.ds(top + 1, half, stride=2), :]
            tap = 9 * a + 2 * pair
            ordered[tap * half : (tap + 1) * half, :] = jnp.where(first_half, low, pltpu.roll(high, channels, axis=1))
            if pair < 4:
                tap += 1
                ordered[tap * half : (tap + 1) * half, :] = jnp.where(
                    first_half, pltpu.roll(low, channels, axis=1), high
                )
    if len(out.shape) == 4:
        rows = out.shape[2]
        for core in range(2):
            for slot, part in enumerate(order[core]):
                out[core, slot] = ordered[part * rows : (part + 1) * rows, :].astype(out.dtype)
    else:
        out[...] = ordered[...].astype(out.dtype)


def source_kernel(slope, x_near, x_far, far, near, kernel, out, columns, weights, spread):
    width_x, width_y, channels, depth = slope.shape
    cells_at = functools.partial(plane, slope, x_near, x_far, is_even("gx"))
    even = is_even("gy")
    zeros = jnp.zeros((channels, depth), slope.dtype)
    for wide_x in range(width_x + 2):
        for row in range(-1, width_y + 1):
            cells = cells_at(wide_x, row) if 0 <= row < width_y else zeros
            for b in range(3):
                y = row + b - 1
                if 0 <= y < width_y:
                    first = (3 * wide_x + b) * channels
                    columns[first : first + channels, y * depth : (y + 1) * depth] = cells
    for a in range(3):
        for b in range(3):
            for c in range(3):
                first = (3 * (2 - a) + b) * channels
                weights[c, first : first + channels, :] = kernel[9 * a + 3 * b + c]
    for x in range(width_x):
        cells = columns[3 * x * channels : 3 * (x + 3) * channels, :]
        for c in range(3):
            spread[c] = lax.dot_general(weights[c], cells, TN, preferred_element_type=jnp.float32)
        for y in range(width_y):
            lanes = slice(y * depth, (y + 1) * depth)
            total = gather([spread[c, :, lanes] for c in range(3)])
            if y == 0:
                total += jnp.where(even, far[x], near[x]).astype(jnp.float32)
            if y == width_y - 1:
                total += jnp.where(even, near[x], far[x]).astype(jnp.float32)
            out[x, y] = total.astype(out.dtype)


def on_device(source, preact, cotangent, kernel):
    channels, width_x, width_y, depth = source.shape
    devices = lax.axis_size("gx") * lax.axis_size("gy")
    cell_count = width_x * width_y * depth
    lines = 27 * channels * channels // 128
    pairs, count_y = lax.axis_size("gx") // 2, lax.axis_size("gy")
    share = (2, pairs * count_y, lines // devices, 128) if lines % devices == 0 else (lines, 128)
    places = [(i, (i + step) % count_y) for step in range(count_y) for i in range(pairs)][::-1]
    places = places[len(places) // 2 :] + places[: len(places) // 2]
    order = [[(2 * i + core) * count_y + j for i, j in places] for core in range(2)]

    slope = jnp.where(preact > 0, cotangent, jnp.zeros_like(cotangent)).transpose(1, 2, 0, 3)
    src = source.transpose(1, 2, 0, 3)
    slope, src = lax.optimization_barrier((slope, src))
    x_near, x_far = swapped(slope[:1], slope[width_x - 1 :], "gx")
    src_near, src_far = swapped(src[:, 0], src[:, -1], "gy")

    cost = pl.CostEstimate(
        flops=54 * channels * channels * cell_count, bytes_accessed=2 * 1024 * 1024, transcendentals=0
    )
    vmem = pl.BlockSpec(memory_space=pltpu.VMEM)
    edge = jax.ShapeDtypeStruct((width_x, channels, depth), jnp.bfloat16)
    inner, down, up = pl.pallas_call(
        inner_kernel,
        out_shape=(jax.ShapeDtypeStruct((3 * channels, 9 * channels), jnp.float32), edge, edge),
        in_specs=[vmem] * 5,
        out_specs=(vmem, vmem, vmem),
        scratch_shapes=[
            pltpu.VMEM(((width_x + 2) * channels, width_y * depth), jnp.bfloat16),
            pltpu.VMEM((width_x, 9 * channels, width_y * depth), jnp.bfloat16),
            pltpu.VMEM(((width_x + 2) * channels, depth), jnp.bfloat16),
            pltpu.VMEM((3, 3 * channels, channels), jnp.bfloat16),
        ],
        compiler_params=PARAMS,
        cost_estimate=cost,
        name="weight_inner",
    )(slope, x_near, x_far, src, kernel)
    partial = pl.pallas_call(
        functools.partial(weight_kernel, order),
        out_shape=jax.ShapeDtypeStruct(share, jnp.bfloat16),
        in_specs=[vmem] * 6,
        out_specs=vmem,
        scratch_shapes=[
            pltpu.VMEM(((width_x + 2) * channels, depth), jnp.bfloat16),
            pltpu.VMEM((3 * channels, depth), jnp.bfloat16),
            pltpu.VMEM((5, 3 * channels, 2 * channels), jnp.float32),
            pltpu.VMEM((lines, 128), jnp.float32),
        ],
        compiler_params=PARAMS,
        cost_estimate=cost,
        name="weight_grad",
    )(inner, slope, x_near, x_far, src_near, src_far)
    near, far = swapped(down, up, "gy")
    if len(share) == 2:
        partial = partial.reshape(devices, -1)[jnp.array(order)]
    even = is_even("gx")
    swap = [(i, i ^ 1) for i in range(2 * pairs)]
    other = lax.ppermute(jnp.where(even, partial[1], partial[0]), "gx", swap)
    own = jnp.where(even, partial[0], partial[1])
    both = (own.astype(jnp.float32) + other.astype(jnp.float32)).astype(jnp.bfloat16)
    shares = lax.all_to_all(both, ("gx", "gy"), 0, 0, axis_index_groups=order, tiled=True)
    norm_scale = 1.0 / math.sqrt(cell_count * devices)
    grad_kernel = (jnp.sum(shares.astype(jnp.float32), axis=0) * norm_scale).reshape(-1)

    grad_source = pl.pallas_call(
        source_kernel,
        out_shape=jax.ShapeDtypeStruct(slope.shape, jnp.bfloat16),
        in_specs=[vmem] * 6,
        out_specs=vmem,
        scratch_shapes=[
            pltpu.VMEM((3 * (width_x + 2) * channels, width_y * depth), jnp.bfloat16),
            pltpu.VMEM((3, 9 * channels, channels), jnp.bfloat16),
            pltpu.VMEM((3, channels, width_y * depth), jnp.float32),
        ],
        compiler_params=PARAMS,
        cost_estimate=pl.CostEstimate(
            flops=5400 * channels * channels * cell_count, bytes_accessed=2 * 1024 * 1024, transcendentals=0
        ),
        name="source_grad",
    )(slope, x_near, x_far, far, near, kernel)
    return (grad_source.transpose(2, 0, 1, 3), grad_kernel)


def solution(mesh):
    placed = (P(None, "gx", "gy", None), P(None, "gx", "gy", None), P(None, "gx", "gy", None), P())
    return jax.shard_map(
        on_device,
        mesh=mesh,
        in_specs=placed,
        out_specs=(P(None, "gx", "gy", None), P(("gx", "gy"))),
        check_vma=False,
    )
```

```python
import functools
import math

import jax
import jax.numpy as jnp
from jax import lax
from jax.experimental import pallas as pl
from jax.experimental.pallas import tpu as pltpu
from jax.sharding import PartitionSpec as P

NT = (((1,), (1,)), ((), ()))
TN = (((0,), (0,)), ((), ()))
PARAMS = pltpu.CompilerParams(vmem_limit_bytes=24 * 1024 * 1024)


def is_even(axis):
    return lax.axis_index(axis) & 1 == 0


def swapped(first, last, axis):
    count = lax.axis_size(axis)
    even = is_even(axis)
    near = [(i, i ^ 1) for i in range(count)]
    far = [(i, (i - 1) % count if i % 2 == 0 else (i + 1) % count) for i in range(count)]
    got_far = lax.ppermute(jnp.where(even, first, last), axis, far)
    got_near = lax.ppermute(jnp.where(even, last, first), axis, near)
    return got_near, got_far


def roll_lanes(block, step):
    if step == 0:
        return block
    return pltpu.roll(block.astype(jnp.float32), step % block.shape[-1], axis=1).astype(block.dtype)


def plane(slope, near, far, even, wide_x, row):
    if wide_x == 0:
        return jnp.where(even, far[0, row], near[0, row])
    if wide_x == slope.shape[0] + 1:
        return jnp.where(even, near[0, row], far[0, row])
    return slope[wide_x - 1, row]


def gather(parts):
    depth = parts[1].shape[1]
    return parts[1] + pltpu.roll(parts[0], depth - 1, axis=1) + pltpu.roll(parts[2], 1, axis=1)


def edge_rows(cells_at, width_x, kernel, row, b, out, columns, weights):
    channels = kernel.shape[1]
    for wide_x in range(width_x + 2):
        columns[wide_x * channels : (wide_x + 1) * channels, :] = cells_at(wide_x, row)
    for a in range(3):
        for c in range(3):
            weights[c, (2 - a) * channels : (3 - a) * channels, :] = kernel[9 * a + 3 * b + c]
    for x in range(width_x):
        cells = columns[x * channels : (x + 3) * channels, :]
        parts = [lax.dot_general(weights[c], cells, TN, preferred_element_type=jnp.float32) for c in range(3)]
        out[x] = gather(parts).astype(out.dtype)


def own_kernel(slope, source, out, right, left):
    width_x, width_y, channels, depth = slope.shape
    for x in range(width_x):
        for y in range(width_y):
            left[x * channels : (x + 1) * channels, y * depth : (y + 1) * depth] = slope[x, y]
    zeros = jnp.zeros((3 * channels, depth), source.dtype)
    for x in range(width_x):
        right[x, 0 : 3 * channels, 0:depth] = zeros
        right[x, 6 * channels :, (width_y - 1) * depth :] = zeros
        for row in range(width_y):
            for c in range(3):
                moved = roll_lanes(source[x, row], 1 - c)
                for b in range(3):
                    y = row + 1 - b
                    if 0 <= y < width_y:
                        first = (3 * b + c) * channels
                        right[x, first : first + channels, y * depth : (y + 1) * depth] = moved
    out[...] = jnp.zeros(out.shape, out.dtype)
    for x in range(width_x):
        low, high = max(0, x - 1), min(width_x, x + 2)
        out[(low + 1 - x) * channels : (high + 1 - x) * channels, :] += lax.dot_general(
            left[low * channels : high * channels, :], right[x], NT, preferred_element_type=jnp.float32
        )


def inner_kernel(own, right, slope, x_near, x_far, kernel, out, down, up, left, columns, weights):
    width_x, width_y, channels, depth = slope.shape
    cells_at = functools.partial(plane, slope, x_near, x_far, is_even("gx"))
    for side, wide_x in enumerate((0, width_x + 1)):
        for y in range(width_y):
            left[side, :, y * depth : (y + 1) * depth] = cells_at(wide_x, y)
    out[...] = own[...]
    for side, x in enumerate((0, width_x - 1)):
        out[2 * side * channels : (2 * side + 1) * channels, :] += lax.dot_general(
            left[side], right[x], NT, preferred_element_type=jnp.float32
        )
    edge_rows(cells_at, width_x, kernel, 0, 0, down, columns, weights)
    edge_rows(cells_at, width_x, kernel, width_y - 1, 2, up, columns, weights)


def weight_kernel(order, inner, slope, x_near, x_far, near, far, out, left, right, gram, ordered):
    width_x, width_y, channels, depth = slope.shape
    cells_at = functools.partial(plane, slope, x_near, x_far, is_even("gx"))
    even = is_even("gy")
    sides = []
    for row in (0, width_y - 1):
        total = None
        for wide_x in range(width_x + 2):
            left[wide_x * channels : (wide_x + 1) * channels, :] = cells_at(wide_x, row)
        for x in range(width_x):
            cells = jnp.where(even, far[x], near[x]) if row == 0 else jnp.where(even, near[x], far[x])
            for c in range(3):
                right[c * channels : (c + 1) * channels, :] = roll_lanes(cells, 1 - c)
            part = lax.dot_general(
                left[x * channels : (x + 3) * channels, :], right[...], NT, preferred_element_type=jnp.float32
            )
            total = part if total is None else total + part
        sides.append(total)
    total = jnp.concatenate(
        [
            inner[:, : 3 * channels] + sides[0],
            inner[:, 3 * channels : 6 * channels],
            inner[:, 6 * channels :] + sides[1],
        ],
        axis=1,
    )
    for pair in range(5):
        lanes = total[:, 2 * pair * channels : min(2 * pair + 2, 9) * channels]
        gram[pair, :, : lanes.shape[1]] = lanes
    half = channels // 2
    first_half = lax.broadcasted_iota(jnp.int32, (half, 2 * channels), 1) < channels
    for a in range(3):
        top = (2 - a) * channels
        for pair in range(5):
            low = gram[pair, pl.ds(top, half, stride=2), :]
            high = gram[pair, pl.ds(top + 1, half, stride=2), :]
            tap = 9 * a + 2 * pair
            ordered[tap * half : (tap + 1) * half, :] = jnp.where(first_half, low, pltpu.roll(high, channels, axis=1))
            if pair < 4:
                tap += 1
                ordered[tap * half : (tap + 1) * half, :] = jnp.where(
                    first_half, pltpu.roll(low, channels, axis=1), high
                )
    if len(out.shape) == 4:
        rows = out.shape[2]
        for core in range(2):
            for slot, part in enumerate(order[core]):
                out[core, slot] = ordered[part * rows : (part + 1) * rows, :].astype(out.dtype)
    else:
        out[...] = ordered[...].astype(out.dtype)


def source_kernel(slope, x_near, x_far, far, near, kernel, out, columns, weights, spread):
    width_x, width_y, channels, depth = slope.shape
    cells_at = functools.partial(plane, slope, x_near, x_far, is_even("gx"))
    even = is_even("gy")
    zeros = jnp.zeros((channels, depth), slope.dtype)
    for wide_x in range(width_x + 2):
        for row in range(-1, width_y + 1):
            cells = cells_at(wide_x, row) if 0 <= row < width_y else zeros
            for b in range(3):
                y = row + b - 1
                if 0 <= y < width_y:
                    first = (3 * wide_x + b) * channels
                    columns[first : first + channels, y * depth : (y + 1) * depth] = cells
    for a in range(3):
        for b in range(3):
            for c in range(3):
                first = (3 * (2 - a) + b) * channels
                weights[c, first : first + channels, :] = kernel[9 * a + 3 * b + c]
    for x in range(width_x):
        cells = columns[3 * x * channels : 3 * (x + 3) * channels, :]
        for c in range(3):
            spread[c] = lax.dot_general(weights[c], cells, TN, preferred_element_type=jnp.float32)
        for y in range(width_y):
            lanes = slice(y * depth, (y + 1) * depth)
            total = gather([spread[c, :, lanes] for c in range(3)])
            if y == 0:
                total += jnp.where(even, far[x], near[x]).astype(jnp.float32)
            if y == width_y - 1:
                total += jnp.where(even, near[x], far[x]).astype(jnp.float32)
            out[x, y] = total.astype(out.dtype)


def on_device(source, preact, cotangent, kernel):
    channels, width_x, width_y, depth = source.shape
    devices = lax.axis_size("gx") * lax.axis_size("gy")
    cell_count = width_x * width_y * depth
    lines = 27 * channels * channels // 128
    pairs, count_y = lax.axis_size("gx") // 2, lax.axis_size("gy")
    share = (2, pairs * count_y, lines // devices, 128) if lines % devices == 0 else (lines, 128)
    places = [(i, (i + step) % count_y) for step in range(count_y) for i in range(pairs)][::-1]
    order = [[(2 * i + core) * count_y + j for i, j in places] for core in range(2)]

    slope = jnp.where(preact > 0, cotangent, jnp.zeros_like(cotangent)).transpose(1, 2, 0, 3)
    src = source.transpose(1, 2, 0, 3)
    slope, src = lax.optimization_barrier((slope, src))
    x_near, x_far = swapped(slope[:1], slope[width_x - 1 :], "gx")
    src_near, src_far = swapped(src[:, 0], src[:, -1], "gy")

    cost = pl.CostEstimate(
        flops=54 * channels * channels * cell_count, bytes_accessed=2 * 1024 * 1024, transcendentals=0
    )
    vmem = pl.BlockSpec(memory_space=pltpu.VMEM)
    edge = jax.ShapeDtypeStruct((width_x, channels, depth), jnp.bfloat16)
    total = jax.ShapeDtypeStruct((3 * channels, 9 * channels), jnp.float32)
    own, right = pl.pallas_call(
        own_kernel,
        out_shape=(total, jax.ShapeDtypeStruct((width_x, 9 * channels, width_y * depth), jnp.bfloat16)),
        in_specs=[vmem] * 2,
        out_specs=(vmem, vmem),
        scratch_shapes=[pltpu.VMEM((width_x * channels, width_y * depth), jnp.bfloat16)],
        compiler_params=PARAMS,
        cost_estimate=cost,
        name="weight_own",
    )(slope, src)
    inner, down, up = pl.pallas_call(
        inner_kernel,
        out_shape=(total, edge, edge),
        in_specs=[vmem] * 6,
        out_specs=(vmem, vmem, vmem),
        scratch_shapes=[
            pltpu.VMEM((2, channels, width_y * depth), jnp.bfloat16),
            pltpu.VMEM(((width_x + 2) * channels, depth), jnp.bfloat16),
            pltpu.VMEM((3, 3 * channels, channels), jnp.bfloat16),
        ],
        compiler_params=PARAMS,
        cost_estimate=cost,
        name="weight_inner",
    )(own, right, slope, x_near, x_far, kernel)
    partial = pl.pallas_call(
        functools.partial(weight_kernel, order),
        out_shape=jax.ShapeDtypeStruct(share, jnp.bfloat16),
        in_specs=[vmem] * 6,
        out_specs=vmem,
        scratch_shapes=[
            pltpu.VMEM(((width_x + 2) * channels, depth), jnp.bfloat16),
            pltpu.VMEM((3 * channels, depth), jnp.bfloat16),
            pltpu.VMEM((5, 3 * channels, 2 * channels), jnp.float32),
            pltpu.VMEM((lines, 128), jnp.float32),
        ],
        compiler_params=PARAMS,
        cost_estimate=cost,
        name="weight_grad",
    )(inner, slope, x_near, x_far, src_near, src_far)
    near, far = swapped(down, up, "gy")
    if len(share) == 2:
        partial = partial.reshape(devices, -1)[jnp.array(order)]
    even = is_even("gx")
    swap = [(i, i ^ 1) for i in range(2 * pairs)]
    other = lax.ppermute(jnp.where(even, partial[1], partial[0]), "gx", swap)
    own = jnp.where(even, partial[0], partial[1])
    both = (own.astype(jnp.float32) + other.astype(jnp.float32)).astype(jnp.bfloat16)
    shares = lax.all_to_all(both, ("gx", "gy"), 0, 0, axis_index_groups=order, tiled=True)
    norm_scale = 1.0 / math.sqrt(cell_count * devices)
    grad_kernel = (jnp.sum(shares.astype(jnp.float32), axis=0) * norm_scale).reshape(-1)

    grad_source = pl.pallas_call(
        source_kernel,
        out_shape=jax.ShapeDtypeStruct(slope.shape, jnp.bfloat16),
        in_specs=[vmem] * 6,
        out_specs=vmem,
        scratch_shapes=[
            pltpu.VMEM((3 * (width_x + 2) * channels, width_y * depth), jnp.bfloat16),
            pltpu.VMEM((3, 9 * channels, channels), jnp.bfloat16),
            pltpu.VMEM((3, channels, width_y * depth), jnp.float32),
        ],
        compiler_params=PARAMS,
        cost_estimate=pl.CostEstimate(
            flops=5400 * channels * channels * cell_count, bytes_accessed=2 * 1024 * 1024, transcendentals=0
        ),
        name="source_grad",
    )(slope, x_near, x_far, far, near, kernel)
    return (grad_source.transpose(2, 0, 1, 3), grad_kernel)


def solution(mesh):
    placed = (P(None, "gx", "gy", None), P(None, "gx", "gy", None), P(None, "gx", "gy", None), P())
    return jax.shard_map(
        on_device,
        mesh=mesh,
        in_specs=placed,
        out_specs=(P(None, "gx", "gy", None), P(("gx", "gy"))),
        check_vma=False,
    )
```

```python
import functools
import math

import jax
import jax.numpy as jnp
from jax import lax
from jax.experimental import pallas as pl
from jax.experimental.pallas import tpu as pltpu
from jax.sharding import PartitionSpec as P

NT = (((1,), (1,)), ((), ()))
TN = (((0,), (0,)), ((), ()))
PARAMS = pltpu.CompilerParams(vmem_limit_bytes=32 * 1024 * 1024)


def is_even(axis):
    return lax.axis_index(axis) & 1 == 0


def swapped(first, last, axis):
    count = lax.axis_size(axis)
    even = is_even(axis)
    near = [(i, i ^ 1) for i in range(count)]
    far = [(i, (i - 1) % count if i % 2 == 0 else (i + 1) % count) for i in range(count)]
    got_far = lax.ppermute(jnp.where(even, first, last), axis, far)
    got_near = lax.ppermute(jnp.where(even, last, first), axis, near)
    return got_near, got_far


def roll_lanes(block, step):
    if step == 0:
        return block
    return pltpu.roll(block.astype(jnp.float32), step % block.shape[-1], axis=1).astype(block.dtype)


def plane(slope, near, far, even, wide_x, row):
    if wide_x == 0:
        return jnp.where(even, far[0, row], near[0, row])
    if wide_x == slope.shape[0] + 1:
        return jnp.where(even, near[0, row], far[0, row])
    return slope[wide_x - 1, row]


def gather(parts):
    depth = parts[1].shape[1]
    return parts[1] + pltpu.roll(parts[0], depth - 1, axis=1) + pltpu.roll(parts[2], 1, axis=1)


def edge_rows(cells_at, width_x, kernel, row, b, out, columns, weights):
    channels = kernel.shape[1]
    for wide_x in range(width_x + 2):
        columns[wide_x * channels : (wide_x + 1) * channels, :] = cells_at(wide_x, row)
    for a in range(3):
        for c in range(3):
            weights[c, (2 - a) * channels : (3 - a) * channels, :] = kernel[9 * a + 3 * b + c]
    for x in range(width_x):
        cells = columns[x * channels : (x + 3) * channels, :]
        parts = [lax.dot_general(weights[c], cells, TN, preferred_element_type=jnp.float32) for c in range(3)]
        out[x] = gather(parts).astype(out.dtype)


def fill_columns(cells_at, width_x, width_y, zeros, columns):
    channels, depth = zeros.shape
    for wide_x in range(width_x + 2):
        for row in range(-1, width_y + 1):
            cells = cells_at(wide_x, row) if 0 <= row < width_y else zeros
            for b in range(3):
                y = row + b - 1
                if 0 <= y < width_y:
                    first = (3 * wide_x + b) * channels
                    columns[first : first + channels, y * depth : (y + 1) * depth] = cells


def inner_kernel(slope, x_near, x_far, source, kernel, out, down, up, columns, moved, cells, weights):
    width_x, width_y, channels, depth = slope.shape
    cells_at = functools.partial(plane, slope, x_near, x_far, is_even("gx"))
    fill_columns(cells_at, width_x, width_y, jnp.zeros((channels, depth), slope.dtype), columns)
    for x in range(width_x):
        for y in range(width_y):
            for c in range(3):
                moved[x, c * channels : (c + 1) * channels, y * depth : (y + 1) * depth] = roll_lanes(
                    source[x, y], 1 - c
                )
    total = None
    for x in range(width_x):
        part = lax.dot_general(
            columns[3 * x * channels : 3 * (x + 3) * channels, :], moved[x], NT, preferred_element_type=jnp.float32
        )
        total = part if total is None else total + part
    out[...] = total
    edge_rows(cells_at, width_x, kernel, 0, 0, down, cells, weights)
    edge_rows(cells_at, width_x, kernel, width_y - 1, 2, up, cells, weights)


def weight_kernel(order, inner, slope, x_near, x_far, near, far, out, left, right, gram, ordered):
    width_x, width_y, channels, depth = slope.shape
    cells_at = functools.partial(plane, slope, x_near, x_far, is_even("gx"))
    even = is_even("gy")
    sides = {}
    for b, row in ((0, 0), (2, width_y - 1)):
        total = None
        for wide_x in range(width_x + 2):
            left[wide_x * channels : (wide_x + 1) * channels, :] = cells_at(wide_x, row)
        for x in range(width_x):
            cells = jnp.where(even, far[x], near[x]) if row == 0 else jnp.where(even, near[x], far[x])
            for c in range(3):
                right[c * channels : (c + 1) * channels, :] = roll_lanes(cells, 1 - c)
            part = lax.dot_general(
                left[x * channels : (x + 3) * channels, :], right[...], NT, preferred_element_type=jnp.float32
            )
            total = part if total is None else total + part
        sides[b] = total
    for k in range(3):
        for b in range(3):
            rows = slice((3 * k + b) * channels, (3 * k + b + 1) * channels)
            block = inner[rows, :]
            if b in sides:
                block += sides[b][k * channels : (k + 1) * channels, :]
            gram[0, rows, :] = block[:, : 2 * channels]
            gram[1, rows, :channels] = block[:, 2 * channels :]
    half = channels // 2
    first_half = lax.broadcasted_iota(jnp.int32, (half, 2 * channels), 1) < channels
    for a in range(3):
        for b in range(3):
            top = (3 * (2 - a) + b) * channels
            line = (9 * a + 3 * b) * half
            low = gram[0, pl.ds(top, half, stride=2), :]
            high = gram[0, pl.ds(top + 1, half, stride=2), :]
            ordered[line : line + half, :] = jnp.where(first_half, low, pltpu.roll(high, channels, axis=1))
            ordered[line + half : line + 2 * half, :] = jnp.where(first_half, pltpu.roll(low, channels, axis=1), high)
            low = gram[1, pl.ds(top, half, stride=2), :]
            high = gram[1, pl.ds(top + 1, half, stride=2), :]
            ordered[line + 2 * half : line + 3 * half, :] = jnp.where(
                first_half, low, pltpu.roll(high, channels, axis=1)
            )
    if len(out.shape) == 4:
        rows = out.shape[2]
        for core in range(2):
            for slot, part in enumerate(order[core]):
                out[core, slot] = ordered[part * rows : (part + 1) * rows, :].astype(out.dtype)
    else:
        out[...] = ordered[...].astype(out.dtype)


def source_kernel(slope, x_near, x_far, far, near, kernel, out, columns, weights, spread):
    width_x, width_y, channels, depth = slope.shape
    cells_at = functools.partial(plane, slope, x_near, x_far, is_even("gx"))
    even = is_even("gy")
    fill_columns(cells_at, width_x, width_y, jnp.zeros((channels, depth), slope.dtype), columns)
    for a in range(3):
        for b in range(3):
            for c in range(3):
                first = (3 * (2 - a) + b) * channels
                weights[c, first : first + channels, :] = kernel[9 * a + 3 * b + c]
    for x in range(width_x):
        cells = columns[3 * x * channels : 3 * (x + 3) * channels, :]
        for c in range(3):
            spread[c] = lax.dot_general(weights[c], cells, TN, preferred_element_type=jnp.float32)
        for y in range(width_y):
            lanes = slice(y * depth, (y + 1) * depth)
            total = gather([spread[c, :, lanes] for c in range(3)])
            if y == 0:
                total += jnp.where(even, far[x], near[x]).astype(jnp.float32)
            if y == width_y - 1:
                total += jnp.where(even, near[x], far[x]).astype(jnp.float32)
            out[x, y] = total.astype(out.dtype)


def on_device(source, preact, cotangent, kernel):
    channels, width_x, width_y, depth = source.shape
    devices = lax.axis_size("gx") * lax.axis_size("gy")
    cell_count = width_x * width_y * depth
    lines = 27 * channels * channels // 128
    pairs, count_y = lax.axis_size("gx") // 2, lax.axis_size("gy")
    share = (2, pairs * count_y, lines // devices, 128) if lines % devices == 0 else (lines, 128)
    places = [(i, (i + step) % count_y) for step in range(count_y) for i in range(pairs)][::-1]
    order = [[(2 * i + core) * count_y + j for i, j in places] for core in range(2)]

    slope = jnp.where(preact > 0, cotangent, jnp.zeros_like(cotangent)).transpose(1, 2, 0, 3)
    src = source.transpose(1, 2, 0, 3)
    slope, src = lax.optimization_barrier((slope, src))
    x_near, x_far = swapped(slope[:1], slope[width_x - 1 :], "gx")
    src_near, src_far = swapped(src[:, 0], src[:, -1], "gy")

    cost = pl.CostEstimate(
        flops=54 * channels * channels * cell_count, bytes_accessed=2 * 1024 * 1024, transcendentals=0
    )
    vmem = pl.BlockSpec(memory_space=pltpu.VMEM)
    edge = jax.ShapeDtypeStruct((width_x, channels, depth), jnp.bfloat16)
    columns = pltpu.VMEM((3 * (width_x + 2) * channels, width_y * depth), jnp.bfloat16)
    inner, down, up = pl.pallas_call(
        inner_kernel,
        out_shape=(jax.ShapeDtypeStruct((9 * channels, 3 * channels), jnp.float32), edge, edge),
        in_specs=[vmem] * 5,
        out_specs=(vmem, vmem, vmem),
        scratch_shapes=[
            columns,
            pltpu.VMEM((width_x, 3 * channels, width_y * depth), jnp.bfloat16),
            pltpu.VMEM(((width_x + 2) * channels, depth), jnp.bfloat16),
            pltpu.VMEM((3, 3 * channels, channels), jnp.bfloat16),
        ],
        compiler_params=PARAMS,
        cost_estimate=cost,
        name="weight_inner",
    )(slope, x_near, x_far, src, kernel)
    partial = pl.pallas_call(
        functools.partial(weight_kernel, order),
        out_shape=jax.ShapeDtypeStruct(share, jnp.bfloat16),
        in_specs=[vmem] * 6,
        out_specs=vmem,
        scratch_shapes=[
            pltpu.VMEM(((width_x + 2) * channels, depth), jnp.bfloat16),
            pltpu.VMEM((3 * channels, depth), jnp.bfloat16),
            pltpu.VMEM((2, 9 * channels, 2 * channels), jnp.float32),
            pltpu.VMEM((lines, 128), jnp.float32),
        ],
        compiler_params=PARAMS,
        cost_estimate=cost,
        name="weight_grad",
    )(inner, slope, x_near, x_far, src_near, src_far)
    near, far = swapped(down, up, "gy")
    if len(share) == 2:
        partial = partial.reshape(devices, -1)[jnp.array(order)]
    even = is_even("gx")
    swap = [(i, i ^ 1) for i in range(2 * pairs)]
    other = lax.ppermute(jnp.where(even, partial[1], partial[0]), "gx", swap)
    own = jnp.where(even, partial[0], partial[1])
    both = (own.astype(jnp.float32) + other.astype(jnp.float32)).astype(jnp.bfloat16)
    shares = lax.all_to_all(both, ("gx", "gy"), 0, 0, axis_index_groups=order, tiled=True)
    norm_scale = 1.0 / math.sqrt(cell_count * devices)
    grad_kernel = (jnp.sum(shares.astype(jnp.float32), axis=0) * norm_scale).reshape(-1)

    grad_source = pl.pallas_call(
        source_kernel,
        out_shape=jax.ShapeDtypeStruct(slope.shape, jnp.bfloat16),
        in_specs=[vmem] * 6,
        out_specs=vmem,
        scratch_shapes=[
            columns,
            pltpu.VMEM((3, 9 * channels, channels), jnp.bfloat16),
            pltpu.VMEM((3, channels, width_y * depth), jnp.float32),
        ],
        compiler_params=PARAMS,
        cost_estimate=pl.CostEstimate(
            flops=5400 * channels * channels * cell_count, bytes_accessed=2 * 1024 * 1024, transcendentals=0
        ),
        name="source_grad",
    )(slope, x_near, x_far, far, near, kernel)
    return (grad_source.transpose(2, 0, 1, 3), grad_kernel)


def solution(mesh):
    placed = (P(None, "gx", "gy", None), P(None, "gx", "gy", None), P(None, "gx", "gy", None), P())
    return jax.shard_map(
        on_device,
        mesh=mesh,
        in_specs=placed,
        out_specs=(P(None, "gx", "gy", None), P(("gx", "gy"))),
        check_vma=False,
    )
```

```python
import functools
import math

import jax
import jax.numpy as jnp
from jax import lax
from jax.experimental import pallas as pl
from jax.experimental.pallas import tpu as pltpu
from jax.sharding import PartitionSpec as P

NT = (((1,), (1,)), ((), ()))
TN = (((0,), (0,)), ((), ()))
PARAMS = pltpu.CompilerParams(vmem_limit_bytes=32 * 1024 * 1024)


def is_even(axis):
    return lax.axis_index(axis) & 1 == 0


def swapped(first, last, axis):
    count = lax.axis_size(axis)
    even = is_even(axis)
    near = [(i, i ^ 1) for i in range(count)]
    far = [(i, (i - 1) % count if i % 2 == 0 else (i + 1) % count) for i in range(count)]
    got_far = lax.ppermute(jnp.where(even, first, last), axis, far)
    got_near = lax.ppermute(jnp.where(even, last, first), axis, near)
    return got_near, got_far


def roll_lanes(block, step):
    if step == 0:
        return block
    return pltpu.roll(block.astype(jnp.float32), step % block.shape[-1], axis=1).astype(block.dtype)


def plane(slope, near, far, even, wide_x, row):
    if wide_x == 0:
        return jnp.where(even, far[0, row], near[0, row])
    if wide_x == slope.shape[0] + 1:
        return jnp.where(even, near[0, row], far[0, row])
    return slope[wide_x - 1, row]


def gather(parts):
    depth = parts[1].shape[1]
    return parts[1] + pltpu.roll(parts[0], depth - 1, axis=1) + pltpu.roll(parts[2], 1, axis=1)


def edge_rows(cells_at, width_x, kernel, row, b, out, columns, weights):
    channels = kernel.shape[1]
    for wide_x in range(width_x + 2):
        columns[wide_x * channels : (wide_x + 1) * channels, :] = cells_at(wide_x, row)
    for a in range(3):
        for c in range(3):
            weights[c, (2 - a) * channels : (3 - a) * channels, :] = kernel[9 * a + 3 * b + c]
    for x in range(width_x):
        cells = columns[x * channels : (x + 3) * channels, :]
        parts = [lax.dot_general(weights[c], cells, TN, preferred_element_type=jnp.float32) for c in range(3)]
        out[x] = gather(parts).astype(out.dtype)


def fill_columns(planes, width_y, zeros, columns):
    channels, depth = zeros.shape
    for place, cells_at in enumerate(planes):
        for row in range(-1, width_y + 1):
            cells = cells_at(row) if 0 <= row < width_y else zeros
            for b in range(3):
                y = row + b - 1
                if 0 <= y < width_y:
                    first = (3 * place + b) * channels
                    columns[first : first + channels, y * depth : (y + 1) * depth] = cells


def own_kernel(slope, source, out, moved, columns):
    width_x, width_y, channels, depth = slope.shape
    planes = [functools.partial(lambda x, row: slope[x, row], x) for x in range(width_x)]
    fill_columns(planes, width_y, jnp.zeros((channels, depth), slope.dtype), columns)
    for x in range(width_x):
        for y in range(width_y):
            for c in range(3):
                moved[x, c * channels : (c + 1) * channels, y * depth : (y + 1) * depth] = roll_lanes(
                    source[x, y], 1 - c
                )
    out[...] = jnp.zeros(out.shape, out.dtype)
    block = 3 * channels
    for x in range(width_x):
        low, high = max(0, x - 1), min(width_x, x + 2)
        out[(low + 1 - x) * block : (high + 1 - x) * block, :] += lax.dot_general(
            columns[low * block : high * block, :], moved[x], NT, preferred_element_type=jnp.float32
        )


def inner_kernel(own, moved, slope, x_near, x_far, kernel, out, down, up, columns, cells, weights):
    width_x, width_y, channels, depth = slope.shape
    cells_at = functools.partial(plane, slope, x_near, x_far, is_even("gx"))
    planes = [functools.partial(cells_at, wide_x) for wide_x in (0, width_x + 1)]
    fill_columns(planes, width_y, jnp.zeros((channels, depth), slope.dtype), columns)
    out[...] = own[...]
    block = 3 * channels
    for side, x in enumerate((0, width_x - 1)):
        out[2 * side * block : (2 * side + 1) * block, :] += lax.dot_general(
            columns[side * block : (side + 1) * block, :], moved[x], NT, preferred_element_type=jnp.float32
        )
    edge_rows(cells_at, width_x, kernel, 0, 0, down, cells, weights)
    edge_rows(cells_at, width_x, kernel, width_y - 1, 2, up, cells, weights)


def weight_kernel(order, inner, slope, x_near, x_far, near, far, out, left, right, gram, ordered):
    width_x, width_y, channels, depth = slope.shape
    cells_at = functools.partial(plane, slope, x_near, x_far, is_even("gx"))
    even = is_even("gy")
    sides = {}
    for b, row in ((0, 0), (2, width_y - 1)):
        total = None
        for wide_x in range(width_x + 2):
            left[wide_x * channels : (wide_x + 1) * channels, :] = cells_at(wide_x, row)
        for x in range(width_x):
            cells = jnp.where(even, far[x], near[x]) if row == 0 else jnp.where(even, near[x], far[x])
            for c in range(3):
                right[c * channels : (c + 1) * channels, :] = roll_lanes(cells, 1 - c)
            part = lax.dot_general(
                left[x * channels : (x + 3) * channels, :], right[...], NT, preferred_element_type=jnp.float32
            )
            total = part if total is None else total + part
        sides[b] = total
    for k in range(3):
        for b in range(3):
            rows = slice((3 * k + b) * channels, (3 * k + b + 1) * channels)
            block = inner[rows, :]
            if b in sides:
                block += sides[b][k * channels : (k + 1) * channels, :]
            gram[0, rows, :] = block[:, : 2 * channels]
            gram[1, rows, :channels] = block[:, 2 * channels :]
    half = channels // 2
    first_half = lax.broadcasted_iota(jnp.int32, (half, 2 * channels), 1) < channels
    for a in range(3):
        for b in range(3):
            top = (3 * (2 - a) + b) * channels
            line = (9 * a + 3 * b) * half
            low = gram[0, pl.ds(top, half, stride=2), :]
            high = gram[0, pl.ds(top + 1, half, stride=2), :]
            ordered[line : line + half, :] = jnp.where(first_half, low, pltpu.roll(high, channels, axis=1))
            ordered[line + half : line + 2 * half, :] = jnp.where(first_half, pltpu.roll(low, channels, axis=1), high)
            low = gram[1, pl.ds(top, half, stride=2), :]
            high = gram[1, pl.ds(top + 1, half, stride=2), :]
            ordered[line + 2 * half : line + 3 * half, :] = jnp.where(
                first_half, low, pltpu.roll(high, channels, axis=1)
            )
    if len(out.shape) == 4:
        rows = out.shape[2]
        for core in range(2):
            for slot, part in enumerate(order[core]):
                out[core, slot] = ordered[part * rows : (part + 1) * rows, :].astype(out.dtype)
    else:
        out[...] = ordered[...].astype(out.dtype)


def source_kernel(slope, x_near, x_far, far, near, kernel, out, columns, weights, spread):
    width_x, width_y, channels, depth = slope.shape
    cells_at = functools.partial(plane, slope, x_near, x_far, is_even("gx"))
    even = is_even("gy")
    planes = [functools.partial(cells_at, wide_x) for wide_x in range(width_x + 2)]
    fill_columns(planes, width_y, jnp.zeros((channels, depth), slope.dtype), columns)
    for a in range(3):
        for b in range(3):
            for c in range(3):
                first = (3 * (2 - a) + b) * channels
                weights[c, first : first + channels, :] = kernel[9 * a + 3 * b + c]
    for x in range(width_x):
        cells = columns[3 * x * channels : 3 * (x + 3) * channels, :]
        for c in range(3):
            spread[c] = lax.dot_general(weights[c], cells, TN, preferred_element_type=jnp.float32)
        for y in range(width_y):
            lanes = slice(y * depth, (y + 1) * depth)
            total = gather([spread[c, :, lanes] for c in range(3)])
            if y == 0:
                total += jnp.where(even, far[x], near[x]).astype(jnp.float32)
            if y == width_y - 1:
                total += jnp.where(even, near[x], far[x]).astype(jnp.float32)
            out[x, y] = total.astype(out.dtype)


def on_device(source, preact, cotangent, kernel):
    channels, width_x, width_y, depth = source.shape
    devices = lax.axis_size("gx") * lax.axis_size("gy")
    cell_count = width_x * width_y * depth
    lines = 27 * channels * channels // 128
    pairs, count_y = lax.axis_size("gx") // 2, lax.axis_size("gy")
    share = (2, pairs * count_y, lines // devices, 128) if lines % devices == 0 else (lines, 128)
    places = [(i, (i + step) % count_y) for step in range(count_y) for i in range(pairs)][::-1]
    order = [[(2 * i + core) * count_y + j for i, j in places] for core in range(2)]

    slope = jnp.where(preact > 0, cotangent, jnp.zeros_like(cotangent)).transpose(1, 2, 0, 3)
    src = source.transpose(1, 2, 0, 3)
    slope, src = lax.optimization_barrier((slope, src))
    x_near, x_far = swapped(slope[:1], slope[width_x - 1 :], "gx")
    src_near, src_far = swapped(src[:, 0], src[:, -1], "gy")

    cost = pl.CostEstimate(
        flops=54 * channels * channels * cell_count, bytes_accessed=2 * 1024 * 1024, transcendentals=0
    )
    vmem = pl.BlockSpec(memory_space=pltpu.VMEM)
    edge = jax.ShapeDtypeStruct((width_x, channels, depth), jnp.bfloat16)
    total = jax.ShapeDtypeStruct((9 * channels, 3 * channels), jnp.float32)
    own, moved = pl.pallas_call(
        own_kernel,
        out_shape=(total, jax.ShapeDtypeStruct((width_x, 3 * channels, width_y * depth), jnp.bfloat16)),
        in_specs=[vmem] * 2,
        out_specs=(vmem, vmem),
        scratch_shapes=[pltpu.VMEM((3 * width_x * channels, width_y * depth), jnp.bfloat16)],
        compiler_params=PARAMS,
        cost_estimate=cost,
        name="weight_own",
    )(slope, src)
    inner, down, up = pl.pallas_call(
        inner_kernel,
        out_shape=(total, edge, edge),
        in_specs=[vmem] * 6,
        out_specs=(vmem, vmem, vmem),
        scratch_shapes=[
            pltpu.VMEM((6 * channels, width_y * depth), jnp.bfloat16),
            pltpu.VMEM(((width_x + 2) * channels, depth), jnp.bfloat16),
            pltpu.VMEM((3, 3 * channels, channels), jnp.bfloat16),
        ],
        compiler_params=PARAMS,
        cost_estimate=cost,
        name="weight_inner",
    )(own, moved, slope, x_near, x_far, kernel)
    partial = pl.pallas_call(
        functools.partial(weight_kernel, order),
        out_shape=jax.ShapeDtypeStruct(share, jnp.bfloat16),
        in_specs=[vmem] * 6,
        out_specs=vmem,
        scratch_shapes=[
            pltpu.VMEM(((width_x + 2) * channels, depth), jnp.bfloat16),
            pltpu.VMEM((3 * channels, depth), jnp.bfloat16),
            pltpu.VMEM((2, 9 * channels, 2 * channels), jnp.float32),
            pltpu.VMEM((lines, 128), jnp.float32),
        ],
        compiler_params=PARAMS,
        cost_estimate=cost,
        name="weight_grad",
    )(inner, slope, x_near, x_far, src_near, src_far)
    near, far = swapped(down, up, "gy")
    if len(share) == 2:
        partial = partial.reshape(devices, -1)[jnp.array(order)]
    even = is_even("gx")
    swap = [(i, i ^ 1) for i in range(2 * pairs)]
    other = lax.ppermute(jnp.where(even, partial[1], partial[0]), "gx", swap)
    own = jnp.where(even, partial[0], partial[1])
    both = (own.astype(jnp.float32) + other.astype(jnp.float32)).astype(jnp.bfloat16)
    shares = lax.all_to_all(both, ("gx", "gy"), 0, 0, axis_index_groups=order, tiled=True)
    norm_scale = 1.0 / math.sqrt(cell_count * devices)
    grad_kernel = (jnp.sum(shares.astype(jnp.float32), axis=0) * norm_scale).reshape(-1)

    grad_source = pl.pallas_call(
        source_kernel,
        out_shape=jax.ShapeDtypeStruct(slope.shape, jnp.bfloat16),
        in_specs=[vmem] * 6,
        out_specs=vmem,
        scratch_shapes=[
            pltpu.VMEM((3 * (width_x + 2) * channels, width_y * depth), jnp.bfloat16),
            pltpu.VMEM((3, 9 * channels, channels), jnp.bfloat16),
            pltpu.VMEM((3, channels, width_y * depth), jnp.float32),
        ],
        compiler_params=PARAMS,
        cost_estimate=pl.CostEstimate(
            flops=5400 * channels * channels * cell_count, bytes_accessed=2 * 1024 * 1024, transcendentals=0
        ),
        name="source_grad",
    )(slope, x_near, x_far, far, near, kernel)
    return (grad_source.transpose(2, 0, 1, 3), grad_kernel)


def solution(mesh):
    placed = (P(None, "gx", "gy", None), P(None, "gx", "gy", None), P(None, "gx", "gy", None), P())
    return jax.shard_map(
        on_device,
        mesh=mesh,
        in_specs=placed,
        out_specs=(P(None, "gx", "gy", None), P(("gx", "gy"))),
        check_vma=False,
    )
```

```python
import functools
import math

import jax
import jax.numpy as jnp
from jax import lax
from jax.experimental import pallas as pl
from jax.experimental.pallas import tpu as pltpu
from jax.sharding import PartitionSpec as P

NT = (((1,), (1,)), ((), ()))
TN = (((0,), (0,)), ((), ()))
PARAMS = pltpu.CompilerParams(vmem_limit_bytes=32 * 1024 * 1024)


def is_even(axis):
    return lax.axis_index(axis) & 1 == 0


def swapped(first, last, axis):
    count = lax.axis_size(axis)
    even = is_even(axis)
    near = [(i, i ^ 1) for i in range(count)]
    far = [(i, (i - 1) % count if i % 2 == 0 else (i + 1) % count) for i in range(count)]
    got_far = lax.ppermute(jnp.where(even, first, last), axis, far)
    got_near = lax.ppermute(jnp.where(even, last, first), axis, near)
    return got_near, got_far


def roll_lanes(block, step):
    if step == 0:
        return block
    return pltpu.roll(block.astype(jnp.float32), step % block.shape[-1], axis=1).astype(block.dtype)


def plane(slope, near, far, even, wide_x, row):
    if wide_x == 0:
        return jnp.where(even, far[0, row], near[0, row])
    if wide_x == slope.shape[0] + 1:
        return jnp.where(even, near[0, row], far[0, row])
    return slope[wide_x - 1, row]


def gather(parts):
    depth = parts[1].shape[1]
    return parts[1] + pltpu.roll(parts[0], depth - 1, axis=1) + pltpu.roll(parts[2], 1, axis=1)


def edge_rows(cells_at, width_x, kernel, row, b, out, columns, weights):
    channels = kernel.shape[1]
    for wide_x in range(width_x + 2):
        columns[wide_x * channels : (wide_x + 1) * channels, :] = cells_at(wide_x, row)
    for a in range(3):
        for c in range(3):
            weights[c, (2 - a) * channels : (3 - a) * channels, :] = kernel[9 * a + 3 * b + c]
    for x in range(width_x):
        cells = columns[x * channels : (x + 3) * channels, :]
        parts = [lax.dot_general(weights[c], cells, TN, preferred_element_type=jnp.float32) for c in range(3)]
        out[x] = gather(parts).astype(out.dtype)


def fill_columns(planes, width_y, zeros, columns):
    channels, depth = zeros.shape
    for place, cells_at in enumerate(planes):
        for row in range(-1, width_y + 1):
            cells = cells_at(row) if 0 <= row < width_y else zeros
            for b in range(3):
                y = row + b - 1
                if 0 <= y < width_y:
                    first = (3 * place + b) * channels
                    columns[first : first + channels, y * depth : (y + 1) * depth] = cells


def own_kernel(slope, source, out, moved, columns):
    width_x, width_y, channels, depth = slope.shape
    planes = [functools.partial(lambda x, row: slope[x, row], x) for x in range(width_x)]
    fill_columns(planes, width_y, jnp.zeros((channels, depth), slope.dtype), columns)
    for x in range(width_x):
        for y in range(width_y):
            for c in range(3):
                moved[x, c * channels : (c + 1) * channels, y * depth : (y + 1) * depth] = roll_lanes(
                    source[x, y], 1 - c
                )
    out[...] = jnp.zeros(out.shape, out.dtype)
    block = 3 * channels
    for x in range(width_x):
        low, high = max(0, x - 1), min(width_x, x + 2)
        out[(low + 1 - x) * block : (high + 1 - x) * block, :] += lax.dot_general(
            columns[low * block : high * block, :], moved[x], NT, preferred_element_type=jnp.float32
        )


def inner_kernel(own, moved, slope, x_near, x_far, kernel, out, down, up, columns, cells, weights):
    width_x, width_y, channels, depth = slope.shape
    cells_at = functools.partial(plane, slope, x_near, x_far, is_even("gx"))
    planes = [functools.partial(cells_at, wide_x) for wide_x in (0, width_x + 1)]
    fill_columns(planes, width_y, jnp.zeros((channels, depth), slope.dtype), columns)
    out[...] = own[...]
    block = 3 * channels
    for side, x in enumerate((0, width_x - 1)):
        out[2 * side * block : (2 * side + 1) * block, :] += lax.dot_general(
            columns[side * block : (side + 1) * block, :], moved[x], NT, preferred_element_type=jnp.float32
        )
    edge_rows(cells_at, width_x, kernel, 0, 0, down, cells, weights)
    edge_rows(cells_at, width_x, kernel, width_y - 1, 2, up, cells, weights)


def weight_kernel(order, inner, slope, x_near, x_far, far, near, out, left, right, gram, ordered):
    width_x, width_y, channels, depth = slope.shape
    cells_at = functools.partial(plane, slope, x_near, x_far, is_even("gx"))
    even = is_even("gy")
    sides = {}
    for b, row in ((0, 0), (2, width_y - 1)):
        total = None
        for wide_x in range(width_x + 2):
            left[wide_x * channels : (wide_x + 1) * channels, :] = cells_at(wide_x, row)
        for x in range(width_x):
            cells = jnp.where(even, far[x], near[x]) if row == 0 else jnp.where(even, near[x], far[x])
            for c in range(3):
                right[c * channels : (c + 1) * channels, :] = roll_lanes(cells, 1 - c)
            part = lax.dot_general(
                left[x * channels : (x + 3) * channels, :], right[...], NT, preferred_element_type=jnp.float32
            )
            total = part if total is None else total + part
        sides[b] = total
    for k in range(3):
        for b in range(3):
            rows = slice((3 * k + b) * channels, (3 * k + b + 1) * channels)
            block = inner[rows, :]
            if b in sides:
                block += sides[b][k * channels : (k + 1) * channels, :]
            gram[0, rows, :] = block[:, : 2 * channels]
            gram[1, rows, :channels] = block[:, 2 * channels :]
    half = channels // 2
    first_half = lax.broadcasted_iota(jnp.int32, (half, 2 * channels), 1) < channels
    for a in range(3):
        for b in range(3):
            top = (3 * (2 - a) + b) * channels
            line = (9 * a + 3 * b) * half
            low = gram[0, pl.ds(top, half, stride=2), :]
            high = gram[0, pl.ds(top + 1, half, stride=2), :]
            ordered[line : line + half, :] = jnp.where(first_half, low, pltpu.roll(high, channels, axis=1))
            ordered[line + half : line + 2 * half, :] = jnp.where(first_half, pltpu.roll(low, channels, axis=1), high)
            low = gram[1, pl.ds(top, half, stride=2), :]
            high = gram[1, pl.ds(top + 1, half, stride=2), :]
            ordered[line + 2 * half : line + 3 * half, :] = jnp.where(
                first_half, low, pltpu.roll(high, channels, axis=1)
            )
    if len(out.shape) == 4:
        rows = out.shape[2]
        for core in range(2):
            for slot, part in enumerate(order[core]):
                out[core, slot] = ordered[part * rows : (part + 1) * rows, :].astype(out.dtype)
    else:
        out[...] = ordered[...].astype(out.dtype)


def source_kernel(slope, x_near, x_far, far, near, kernel, out, columns, weights, spread):
    width_x, width_y, channels, depth = slope.shape
    cells_at = functools.partial(plane, slope, x_near, x_far, is_even("gx"))
    even = is_even("gy")
    planes = [functools.partial(cells_at, wide_x) for wide_x in range(width_x + 2)]
    fill_columns(planes, width_y, jnp.zeros((channels, depth), slope.dtype), columns)
    for a in range(3):
        for b in range(3):
            for c in range(3):
                first = (3 * (2 - a) + b) * channels
                weights[c, first : first + channels, :] = kernel[9 * a + 3 * b + c]
    for x in range(width_x):
        cells = columns[3 * x * channels : 3 * (x + 3) * channels, :]
        for c in range(3):
            spread[c] = lax.dot_general(weights[c], cells, TN, preferred_element_type=jnp.float32)
        for y in range(width_y):
            lanes = slice(y * depth, (y + 1) * depth)
            total = gather([spread[c, :, lanes] for c in range(3)])
            if y == 0:
                total += jnp.where(even, far[x], near[x]).astype(jnp.float32)
            if y == width_y - 1:
                total += jnp.where(even, near[x], far[x]).astype(jnp.float32)
            out[x, y] = total.astype(out.dtype)


def on_device(source, preact, cotangent, kernel):
    channels, width_x, width_y, depth = source.shape
    devices = lax.axis_size("gx") * lax.axis_size("gy")
    cell_count = width_x * width_y * depth
    lines = 27 * channels * channels // 128
    pairs, count_y = lax.axis_size("gx") // 2, lax.axis_size("gy")
    share = (2, pairs * count_y, lines // devices, 128) if lines % devices == 0 else (lines, 128)
    places = [(i, (i + step) % count_y) for step in range(count_y) for i in range(pairs)][::-1]
    order = [[(2 * i + core) * count_y + j for i, j in places] for core in range(2)]

    slope = jnp.where(preact > 0, cotangent, jnp.zeros_like(cotangent)).transpose(1, 2, 0, 3)
    src = source.transpose(1, 2, 0, 3)
    slope, src = lax.optimization_barrier((slope, src))
    x_near, x_far = swapped(slope[:1], slope[width_x - 1 :], "gx")
    src_near, src_far = swapped(src[:, 0], src[:, -1], "gy")

    cost = pl.CostEstimate(
        flops=54 * channels * channels * cell_count, bytes_accessed=2 * 1024 * 1024, transcendentals=0
    )
    vmem = pl.BlockSpec(memory_space=pltpu.VMEM)
    edge = jax.ShapeDtypeStruct((width_x, channels, depth), jnp.bfloat16)
    total = jax.ShapeDtypeStruct((9 * channels, 3 * channels), jnp.float32)
    own, moved = pl.pallas_call(
        own_kernel,
        out_shape=(total, jax.ShapeDtypeStruct((width_x, 3 * channels, width_y * depth), jnp.bfloat16)),
        in_specs=[vmem] * 2,
        out_specs=(vmem, vmem),
        scratch_shapes=[pltpu.VMEM((3 * width_x * channels, width_y * depth), jnp.bfloat16)],
        compiler_params=PARAMS,
        cost_estimate=cost,
        name="weight_own",
    )(slope, src)
    inner, down, up = pl.pallas_call(
        inner_kernel,
        out_shape=(total, edge, edge),
        in_specs=[vmem] * 6,
        out_specs=(vmem, vmem, vmem),
        scratch_shapes=[
            pltpu.VMEM((6 * channels, width_y * depth), jnp.bfloat16),
            pltpu.VMEM(((width_x + 2) * channels, depth), jnp.bfloat16),
            pltpu.VMEM((3, 3 * channels, channels), jnp.bfloat16),
        ],
        compiler_params=PARAMS,
        cost_estimate=cost,
        name="weight_inner",
    )(own, moved, slope, x_near, x_far, kernel)
    partial = pl.pallas_call(
        functools.partial(weight_kernel, order),
        out_shape=jax.ShapeDtypeStruct(share, jnp.bfloat16),
        in_specs=[vmem] * 6,
        out_specs=vmem,
        scratch_shapes=[
            pltpu.VMEM(((width_x + 2) * channels, depth), jnp.bfloat16),
            pltpu.VMEM((3 * channels, depth), jnp.bfloat16),
            pltpu.VMEM((2, 9 * channels, 2 * channels), jnp.float32),
            pltpu.VMEM((lines, 128), jnp.float32),
        ],
        compiler_params=PARAMS,
        cost_estimate=cost,
        name="weight_grad",
    )(inner, slope, x_near, x_far, src_far, src_near)
    near, far = swapped(down, up, "gy")
    if len(share) == 2:
        partial = partial.reshape(devices, -1)[jnp.array(order)]
    even = is_even("gx")
    swap = [(i, i ^ 1) for i in range(2 * pairs)]
    other = lax.ppermute(jnp.where(even, partial[1], partial[0]), "gx", swap)
    own = jnp.where(even, partial[0], partial[1])
    both = (own.astype(jnp.float32) + other.astype(jnp.float32)).astype(jnp.bfloat16)
    shares = lax.all_to_all(both, ("gx", "gy"), 0, 0, axis_index_groups=order, tiled=True)
    norm_scale = 1.0 / math.sqrt(cell_count * devices)
    grad_kernel = (jnp.sum(shares.astype(jnp.float32), axis=0) * norm_scale).reshape(-1)

    grad_source = pl.pallas_call(
        source_kernel,
        out_shape=jax.ShapeDtypeStruct(slope.shape, jnp.bfloat16),
        in_specs=[vmem] * 6,
        out_specs=vmem,
        scratch_shapes=[
            pltpu.VMEM((3 * (width_x + 2) * channels, width_y * depth), jnp.bfloat16),
            pltpu.VMEM((3, 9 * channels, channels), jnp.bfloat16),
            pltpu.VMEM((3, channels, width_y * depth), jnp.float32),
        ],
        compiler_params=PARAMS,
        cost_estimate=pl.CostEstimate(
            flops=5400 * channels * channels * cell_count, bytes_accessed=2 * 1024 * 1024, transcendentals=0
        ),
        name="source_grad",
    )(slope, x_near, x_far, far, near, kernel)
    return (grad_source.transpose(2, 0, 1, 3), grad_kernel)


def solution(mesh):
    placed = (P(None, "gx", "gy", None), P(None, "gx", "gy", None), P(None, "gx", "gy", None), P())
    return jax.shard_map(
        on_device,
        mesh=mesh,
        in_specs=placed,
        out_specs=(P(None, "gx", "gy", None), P(("gx", "gy"))),
        check_vma=False,
    )
```

```python
import functools
import math

import jax
import jax.numpy as jnp
from jax import lax
from jax.experimental import pallas as pl
from jax.experimental.pallas import tpu as pltpu
from jax.sharding import PartitionSpec as P

NT = (((1,), (1,)), ((), ()))
TN = (((0,), (0,)), ((), ()))
PARAMS = pltpu.CompilerParams(vmem_limit_bytes=32 * 1024 * 1024)


def is_even(axis):
    return lax.axis_index(axis) & 1 == 0


def swapped(first, last, axis):
    count = lax.axis_size(axis)
    even = is_even(axis)
    near = [(i, i ^ 1) for i in range(count)]
    far = [(i, (i - 1) % count if i % 2 == 0 else (i + 1) % count) for i in range(count)]
    got_far = lax.ppermute(jnp.where(even, first, last), axis, far)
    got_near = lax.ppermute(jnp.where(even, last, first), axis, near)
    return got_near, got_far


def roll_lanes(block, step):
    if step == 0:
        return block
    return pltpu.roll(block.astype(jnp.float32), step % block.shape[-1], axis=1).astype(block.dtype)


def plane(slope, near, far, even, wide_x, row):
    if wide_x == 0:
        return jnp.where(even, far[0, row], near[0, row])
    if wide_x == slope.shape[0] + 1:
        return jnp.where(even, near[0, row], far[0, row])
    return slope[wide_x - 1, row]


def gather(parts):
    depth = parts[1].shape[1]
    return parts[1] + pltpu.roll(parts[0], depth - 1, axis=1) + pltpu.roll(parts[2], 1, axis=1)


def edge_rows(cells_at, width_x, kernel, row, b, out, columns, weights):
    channels = kernel.shape[1]
    for wide_x in range(width_x + 2):
        columns[wide_x * channels : (wide_x + 1) * channels, :] = cells_at(wide_x, row)
    for a in range(3):
        for c in range(3):
            weights[c, (2 - a) * channels : (3 - a) * channels, :] = kernel[9 * a + 3 * b + c]
    for x in range(width_x):
        cells = columns[x * channels : (x + 3) * channels, :]
        parts = [lax.dot_general(weights[c], cells, TN, preferred_element_type=jnp.float32) for c in range(3)]
        out[x] = gather(parts).astype(out.dtype)


def fill_columns(planes, width_y, zeros, columns):
    channels, depth = zeros.shape
    for place, cells_at in enumerate(planes):
        for row in range(-1, width_y + 1):
            cells = cells_at(row) if 0 <= row < width_y else zeros
            for b in range(3):
                y = row + b - 1
                if 0 <= y < width_y:
                    first = (3 * place + b) * channels
                    columns[first : first + channels, y * depth : (y + 1) * depth] = cells


def own_kernel(slope, source, out, moved, columns):
    width_x, width_y, channels, depth = slope.shape
    planes = [functools.partial(lambda x, row: slope[x, row], x) for x in range(width_x)]
    fill_columns(planes, width_y, jnp.zeros((channels, depth), slope.dtype), columns)
    for x in range(width_x):
        for y in range(width_y):
            for c in range(3):
                moved[x, c * channels : (c + 1) * channels, y * depth : (y + 1) * depth] = roll_lanes(
                    source[x, y], 1 - c
                )
    out[...] = jnp.zeros(out.shape, out.dtype)
    block = 3 * channels
    for x in range(width_x):
        low, high = max(0, x - 1), min(width_x, x + 2)
        out[(low + 1 - x) * block : (high + 1 - x) * block, :] += lax.dot_general(
            columns[low * block : high * block, :], moved[x], NT, preferred_element_type=jnp.float32
        )


def inner_kernel(own, moved, slope, x_near, x_far, kernel, out, down, up, columns, cells, weights):
    width_x, width_y, channels, depth = slope.shape
    cells_at = functools.partial(plane, slope, x_near, x_far, is_even("gx"))
    planes = [functools.partial(cells_at, wide_x) for wide_x in (0, width_x + 1)]
    fill_columns(planes, width_y, jnp.zeros((channels, depth), slope.dtype), columns)
    out[...] = own[...]
    block = 3 * channels
    for side, x in enumerate((0, width_x - 1)):
        out[2 * side * block : (2 * side + 1) * block, :] += lax.dot_general(
            columns[side * block : (side + 1) * block, :], moved[x], NT, preferred_element_type=jnp.float32
        )
    edge_rows(cells_at, width_x, kernel, 0, 0, down, cells, weights)
    edge_rows(cells_at, width_x, kernel, width_y - 1, 2, up, cells, weights)


def weight_kernel(order, inner, slope, x_near, x_far, near, far, out, left, right, gram, ordered):
    width_x, width_y, channels, depth = slope.shape
    cells_at = functools.partial(plane, slope, x_near, x_far, is_even("gx"))
    even = is_even("gy")
    sides = {}
    for b, row in ((0, 0), (2, width_y - 1)):
        total = None
        for wide_x in range(width_x + 2):
            left[wide_x * channels : (wide_x + 1) * channels, :] = cells_at(wide_x, row)
        for x in range(width_x):
            cells = jnp.where(even, far[x], near[x]) if row == 0 else jnp.where(even, near[x], far[x])
            for c in range(3):
                right[c * channels : (c + 1) * channels, :] = roll_lanes(cells, 1 - c)
            part = lax.dot_general(
                left[x * channels : (x + 3) * channels, :], right[...], NT, preferred_element_type=jnp.float32
            )
            total = part if total is None else total + part
        sides[b] = total
    for k in range(3):
        for b in range(3):
            rows = slice((3 * k + b) * channels, (3 * k + b + 1) * channels)
            block = inner[rows, :]
            if b in sides:
                block += sides[b][k * channels : (k + 1) * channels, :]
            gram[0, rows, :] = block[:, : 2 * channels]
            gram[1, rows, :channels] = block[:, 2 * channels :]
    half = channels // 2
    first_half = lax.broadcasted_iota(jnp.int32, (half, 2 * channels), 1) < channels
    for a in range(3):
        for b in range(3):
            top = (3 * (2 - a) + b) * channels
            line = (9 * a + 3 * b) * half
            low = gram[0, pl.ds(top, half, stride=2), :]
            high = gram[0, pl.ds(top + 1, half, stride=2), :]
            ordered[line : line + half, :] = jnp.where(first_half, low, pltpu.roll(high, channels, axis=1))
            ordered[line + half : line + 2 * half, :] = jnp.where(first_half, pltpu.roll(low, channels, axis=1), high)
            low = gram[1, pl.ds(top, half, stride=2), :]
            high = gram[1, pl.ds(top + 1, half, stride=2), :]
            ordered[line + 2 * half : line + 3 * half, :] = jnp.where(
                first_half, low, pltpu.roll(high, channels, axis=1)
            )
    if len(out.shape) == 4:
        rows = out.shape[2]
        for core in range(2):
            for slot, part in enumerate(order[core]):
                out[core, slot] = ordered[part * rows : (part + 1) * rows, :].astype(out.dtype)
    else:
        out[...] = ordered[...].astype(out.dtype)


def source_kernel(slope, x_near, x_far, far, near, kernel, out, columns, weights, spread):
    width_x, width_y, channels, depth = slope.shape
    cells_at = functools.partial(plane, slope, x_near, x_far, is_even("gx"))
    even = is_even("gy")
    planes = [functools.partial(cells_at, wide_x) for wide_x in range(width_x + 2)]
    fill_columns(planes, width_y, jnp.zeros((channels, depth), slope.dtype), columns)
    for a in range(3):
        for b in range(3):
            for c in range(3):
                first = (3 * (2 - a) + b) * channels
                weights[c, first : first + channels, :] = kernel[9 * a + 3 * b + c]
    for x in range(width_x):
        cells = columns[3 * x * channels : 3 * (x + 3) * channels, :]
        for c in range(3):
            spread[c] = lax.dot_general(weights[c], cells, TN, preferred_element_type=jnp.float32)
        for y in range(width_y):
            lanes = slice(y * depth, (y + 1) * depth)
            total = gather([spread[c, :, lanes] for c in range(3)])
            if y == 0:
                total += jnp.where(even, far[x], near[x]).astype(jnp.float32)
            if y == width_y - 1:
                total += jnp.where(even, near[x], far[x]).astype(jnp.float32)
            out[x, y] = total.astype(out.dtype)


def on_device(source, preact, cotangent, kernel):
    channels, width_x, width_y, depth = source.shape
    devices = lax.axis_size("gx") * lax.axis_size("gy")
    cell_count = width_x * width_y * depth
    lines = 27 * channels * channels // 128
    pairs, count_y = lax.axis_size("gx") // 2, lax.axis_size("gy")
    share = (2, pairs * count_y, lines // devices, 128) if lines % devices == 0 else (lines, 128)
    places = [(i, j) for i in reversed(range(pairs)) for j in reversed(range(count_y))]
    order = [[(2 * i + core) * count_y + j for i, j in places] for core in range(2)]

    slope = jnp.where(preact > 0, cotangent, jnp.zeros_like(cotangent)).transpose(1, 2, 0, 3)
    src = source.transpose(1, 2, 0, 3)
    slope, src = lax.optimization_barrier((slope, src))
    x_near, x_far = swapped(slope[:1], slope[width_x - 1 :], "gx")
    src_near, src_far = swapped(src[:, 0], src[:, -1], "gy")

    cost = pl.CostEstimate(
        flops=54 * channels * channels * cell_count, bytes_accessed=2 * 1024 * 1024, transcendentals=0
    )
    vmem = pl.BlockSpec(memory_space=pltpu.VMEM)
    edge = jax.ShapeDtypeStruct((width_x, channels, depth), jnp.bfloat16)
    total = jax.ShapeDtypeStruct((9 * channels, 3 * channels), jnp.float32)
    own, moved = pl.pallas_call(
        own_kernel,
        out_shape=(total, jax.ShapeDtypeStruct((width_x, 3 * channels, width_y * depth), jnp.bfloat16)),
        in_specs=[vmem] * 2,
        out_specs=(vmem, vmem),
        scratch_shapes=[pltpu.VMEM((3 * width_x * channels, width_y * depth), jnp.bfloat16)],
        compiler_params=PARAMS,
        cost_estimate=cost,
        name="weight_own",
    )(slope, src)
    inner, down, up = pl.pallas_call(
        inner_kernel,
        out_shape=(total, edge, edge),
        in_specs=[vmem] * 6,
        out_specs=(vmem, vmem, vmem),
        scratch_shapes=[
            pltpu.VMEM((6 * channels, width_y * depth), jnp.bfloat16),
            pltpu.VMEM(((width_x + 2) * channels, depth), jnp.bfloat16),
            pltpu.VMEM((3, 3 * channels, channels), jnp.bfloat16),
        ],
        compiler_params=PARAMS,
        cost_estimate=cost,
        name="weight_inner",
    )(own, moved, slope, x_near, x_far, kernel)
    partial = pl.pallas_call(
        functools.partial(weight_kernel, order),
        out_shape=jax.ShapeDtypeStruct(share, jnp.bfloat16),
        in_specs=[vmem] * 6,
        out_specs=vmem,
        scratch_shapes=[
            pltpu.VMEM(((width_x + 2) * channels, depth), jnp.bfloat16),
            pltpu.VMEM((3 * channels, depth), jnp.bfloat16),
            pltpu.VMEM((2, 9 * channels, 2 * channels), jnp.float32),
            pltpu.VMEM((lines, 128), jnp.float32),
        ],
        compiler_params=PARAMS,
        cost_estimate=cost,
        name="weight_grad",
    )(inner, slope, x_near, x_far, src_near, src_far)
    near, far = swapped(down, up, "gy")
    if len(share) == 2:
        partial = partial.reshape(devices, -1)[jnp.array(order)]
    even = is_even("gx")
    swap = [(i, i ^ 1) for i in range(2 * pairs)]
    other = lax.ppermute(jnp.where(even, partial[1], partial[0]), "gx", swap)
    own = jnp.where(even, partial[0], partial[1])
    both = (own.astype(jnp.float32) + other.astype(jnp.float32)).astype(jnp.bfloat16)
    shares = lax.all_to_all(both, ("gx", "gy"), 0, 0, axis_index_groups=order, tiled=True)
    norm_scale = 1.0 / math.sqrt(cell_count * devices)
    grad_kernel = (jnp.sum(shares.astype(jnp.float32), axis=0) * norm_scale).reshape(-1)

    grad_source = pl.pallas_call(
        source_kernel,
        out_shape=jax.ShapeDtypeStruct(slope.shape, jnp.bfloat16),
        in_specs=[vmem] * 6,
        out_specs=vmem,
        scratch_shapes=[
            pltpu.VMEM((3 * (width_x + 2) * channels, width_y * depth), jnp.bfloat16),
            pltpu.VMEM((3, 9 * channels, channels), jnp.bfloat16),
            pltpu.VMEM((3, channels, width_y * depth), jnp.float32),
        ],
        compiler_params=PARAMS,
        cost_estimate=pl.CostEstimate(
            flops=5400 * channels * channels * cell_count, bytes_accessed=2 * 1024 * 1024, transcendentals=0
        ),
        name="source_grad",
    )(slope, x_near, x_far, far, near, kernel)
    return (grad_source.transpose(2, 0, 1, 3), grad_kernel)


def solution(mesh):
    placed = (P(None, "gx", "gy", None), P(None, "gx", "gy", None), P(None, "gx", "gy", None), P())
    return jax.shard_map(
        on_device,
        mesh=mesh,
        in_specs=placed,
        out_specs=(P(None, "gx", "gy", None), P(("gx", "gy"))),
        check_vma=False,
    )
```

```python
import functools
import math

import jax
import jax.numpy as jnp
from jax import lax
from jax.experimental import pallas as pl
from jax.experimental.pallas import tpu as pltpu
from jax.sharding import PartitionSpec as P

NT = (((1,), (1,)), ((), ()))
TN = (((0,), (0,)), ((), ()))
PARAMS = pltpu.CompilerParams(vmem_limit_bytes=32 * 1024 * 1024)


def is_even(axis):
    return lax.axis_index(axis) & 1 == 0


def swapped(first, last, axis):
    count = lax.axis_size(axis)
    even = is_even(axis)
    near = [(i, i ^ 1) for i in range(count)]
    far = [(i, (i - 1) % count if i % 2 == 0 else (i + 1) % count) for i in range(count)]
    got_far = lax.ppermute(jnp.where(even, first, last), axis, far)
    got_near = lax.ppermute(jnp.where(even, last, first), axis, near)
    return got_near, got_far


def roll_lanes(block, step):
    if step == 0:
        return block
    return pltpu.roll(block.astype(jnp.float32), step % block.shape[-1], axis=1).astype(block.dtype)


def plane(slope, near, far, even, wide_x, row):
    if wide_x == 0:
        return jnp.where(even, far[0, row], near[0, row])
    if wide_x == slope.shape[0] + 1:
        return jnp.where(even, near[0, row], far[0, row])
    return slope[wide_x - 1, row]


def gather(parts):
    depth = parts[1].shape[1]
    return parts[1] + pltpu.roll(parts[0], depth - 1, axis=1) + pltpu.roll(parts[2], 1, axis=1)


def edge_rows(cells_at, width_x, kernel, row, b, out, columns, weights):
    channels = kernel.shape[1]
    for wide_x in range(width_x + 2):
        columns[wide_x * channels : (wide_x + 1) * channels, :] = cells_at(wide_x, row)
    for a in range(3):
        for c in range(3):
            weights[c, (2 - a) * channels : (3 - a) * channels, :] = kernel[9 * a + 3 * b + c]
    for x in range(width_x):
        cells = columns[x * channels : (x + 3) * channels, :]
        parts = [lax.dot_general(weights[c], cells, TN, preferred_element_type=jnp.float32) for c in range(3)]
        out[x] = gather(parts).astype(out.dtype)


def fill_columns(cells_at, width_x, width_y, zeros, columns):
    channels, depth = zeros.shape
    for wide_x in range(width_x + 2):
        for row in range(-1, width_y + 1):
            cells = cells_at(wide_x, row) if 0 <= row < width_y else zeros
            for b in range(3):
                y = row + b - 1
                if 0 <= y < width_y:
                    first = (3 * wide_x + b) * channels
                    columns[first : first + channels, y * depth : (y + 1) * depth] = cells


def inner_kernel(slope, x_near, x_far, source, kernel, out, down, up, columns, moved, cells, weights):
    width_x, width_y, channels, depth = slope.shape
    cells_at = functools.partial(plane, slope, x_near, x_far, is_even("gx"))
    fill_columns(cells_at, width_x, width_y, jnp.zeros((channels, depth), slope.dtype), columns)
    for x in range(width_x):
        for y in range(width_y):
            for c in range(3):
                moved[x, c * channels : (c + 1) * channels, y * depth : (y + 1) * depth] = roll_lanes(
                    source[x, y], 1 - c
                )
    total = None
    for x in range(width_x):
        part = lax.dot_general(
            columns[3 * x * channels : 3 * (x + 3) * channels, :], moved[x], NT, preferred_element_type=jnp.float32
        )
        total = part if total is None else total + part
    out[...] = total
    edge_rows(cells_at, width_x, kernel, 0, 0, down, cells, weights)
    edge_rows(cells_at, width_x, kernel, width_y - 1, 2, up, cells, weights)


def weight_kernel(order, inner, slope, x_near, x_far, far, near, out, left, right, gram, ordered):
    width_x, width_y, channels, depth = slope.shape
    cells_at = functools.partial(plane, slope, x_near, x_far, is_even("gx"))
    even = is_even("gy")
    sides = {}
    for b, row in ((0, 0), (2, width_y - 1)):
        total = None
        for wide_x in range(width_x + 2):
            left[wide_x * channels : (wide_x + 1) * channels, :] = cells_at(wide_x, row)
        for x in range(width_x):
            cells = jnp.where(even, far[x], near[x]) if row == 0 else jnp.where(even, near[x], far[x])
            for c in range(3):
                right[c * channels : (c + 1) * channels, :] = roll_lanes(cells, 1 - c)
            part = lax.dot_general(
                left[x * channels : (x + 3) * channels, :], right[...], NT, preferred_element_type=jnp.float32
            )
            total = part if total is None else total + part
        sides[b] = total
    for k in range(3):
        for b in range(3):
            rows = slice((3 * k + b) * channels, (3 * k + b + 1) * channels)
            block = inner[rows, :]
            if b in sides:
                block += sides[b][k * channels : (k + 1) * channels, :]
            gram[0, rows, :] = block[:, : 2 * channels]
            gram[1, rows, :channels] = block[:, 2 * channels :]
    half = channels // 2
    first_half = lax.broadcasted_iota(jnp.int32, (half, 2 * channels), 1) < channels
    for a in range(3):
        for b in range(3):
            top = (3 * (2 - a) + b) * channels
            line = (9 * a + 3 * b) * half
            low = gram[0, pl.ds(top, half, stride=2), :]
            high = gram[0, pl.ds(top + 1, half, stride=2), :]
            ordered[line : line + half, :] = jnp.where(first_half, low, pltpu.roll(high, channels, axis=1))
            ordered[line + half : line + 2 * half, :] = jnp.where(first_half, pltpu.roll(low, channels, axis=1), high)
            low = gram[1, pl.ds(top, half, stride=2), :]
            high = gram[1, pl.ds(top + 1, half, stride=2), :]
            ordered[line + 2 * half : line + 3 * half, :] = jnp.where(
                first_half, low, pltpu.roll(high, channels, axis=1)
            )
    if len(out.shape) == 4:
        rows = out.shape[2]
        for core in range(2):
            for slot, part in enumerate(order[core]):
                out[core, slot] = ordered[part * rows : (part + 1) * rows, :].astype(out.dtype)
    else:
        out[...] = ordered[...].astype(out.dtype)


def source_kernel(slope, x_near, x_far, far, near, kernel, out, columns, weights, spread):
    width_x, width_y, channels, depth = slope.shape
    cells_at = functools.partial(plane, slope, x_near, x_far, is_even("gx"))
    even = is_even("gy")
    fill_columns(cells_at, width_x, width_y, jnp.zeros((channels, depth), slope.dtype), columns)
    for a in range(3):
        for b in range(3):
            for c in range(3):
                first = (3 * (2 - a) + b) * channels
                weights[c, first : first + channels, :] = kernel[9 * a + 3 * b + c]
    for x in range(width_x):
        cells = columns[3 * x * channels : 3 * (x + 3) * channels, :]
        for c in range(3):
            spread[c] = lax.dot_general(weights[c], cells, TN, preferred_element_type=jnp.float32)
        for y in range(width_y):
            lanes = slice(y * depth, (y + 1) * depth)
            total = gather([spread[c, :, lanes] for c in range(3)])
            if y == 0:
                total += jnp.where(even, far[x], near[x]).astype(jnp.float32)
            if y == width_y - 1:
                total += jnp.where(even, near[x], far[x]).astype(jnp.float32)
            out[x, y] = total.astype(out.dtype)


def on_device(source, preact, cotangent, kernel):
    channels, width_x, width_y, depth = source.shape
    devices = lax.axis_size("gx") * lax.axis_size("gy")
    cell_count = width_x * width_y * depth
    lines = 27 * channels * channels // 128
    pairs, count_y = lax.axis_size("gx") // 2, lax.axis_size("gy")
    share = (2, pairs * count_y, lines // devices, 128) if lines % devices == 0 else (lines, 128)
    places = [(i, (i + step) % count_y) for step in range(count_y) for i in range(pairs)][::-1]
    order = [[(2 * i + core) * count_y + j for i, j in places] for core in range(2)]

    slope = jnp.where(preact > 0, cotangent, jnp.zeros_like(cotangent)).transpose(1, 2, 0, 3)
    src = source.transpose(1, 2, 0, 3)
    slope, src = lax.optimization_barrier((slope, src))
    x_near, x_far = swapped(slope[:1], slope[width_x - 1 :], "gx")
    src_near, src_far = swapped(src[:, 0], src[:, -1], "gy")

    cost = pl.CostEstimate(
        flops=54 * channels * channels * cell_count, bytes_accessed=2 * 1024 * 1024, transcendentals=0
    )
    vmem = pl.BlockSpec(memory_space=pltpu.VMEM)
    edge = jax.ShapeDtypeStruct((width_x, channels, depth), jnp.bfloat16)
    columns = pltpu.VMEM((3 * (width_x + 2) * channels, width_y * depth), jnp.bfloat16)
    inner, down, up = pl.pallas_call(
        inner_kernel,
        out_shape=(jax.ShapeDtypeStruct((9 * channels, 3 * channels), jnp.float32), edge, edge),
        in_specs=[vmem] * 5,
        out_specs=(vmem, vmem, vmem),
        scratch_shapes=[
            columns,
            pltpu.VMEM((width_x, 3 * channels, width_y * depth), jnp.bfloat16),
            pltpu.VMEM(((width_x + 2) * channels, depth), jnp.bfloat16),
            pltpu.VMEM((3, 3 * channels, channels), jnp.bfloat16),
        ],
        compiler_params=PARAMS,
        cost_estimate=cost,
        name="weight_inner",
    )(slope, x_near, x_far, src, kernel)
    partial = pl.pallas_call(
        functools.partial(weight_kernel, order),
        out_shape=jax.ShapeDtypeStruct(share, jnp.bfloat16),
        in_specs=[vmem] * 6,
        out_specs=vmem,
        scratch_shapes=[
            pltpu.VMEM(((width_x + 2) * channels, depth), jnp.bfloat16),
            pltpu.VMEM((3 * channels, depth), jnp.bfloat16),
            pltpu.VMEM((2, 9 * channels, 2 * channels), jnp.float32),
            pltpu.VMEM((lines, 128), jnp.float32),
        ],
        compiler_params=PARAMS,
        cost_estimate=cost,
        name="weight_grad",
    )(inner, slope, x_near, x_far, src_far, src_near)
    near, far = swapped(down, up, "gy")
    if len(share) == 2:
        partial = partial.reshape(devices, -1)[jnp.array(order)]
    even = is_even("gx")
    swap = [(i, i ^ 1) for i in range(2 * pairs)]
    other = lax.ppermute(jnp.where(even, partial[1], partial[0]), "gx", swap)
    own = jnp.where(even, partial[0], partial[1])
    both = (own.astype(jnp.float32) + other.astype(jnp.float32)).astype(jnp.bfloat16)
    shares = lax.all_to_all(both, ("gx", "gy"), 0, 0, axis_index_groups=order, tiled=True)
    norm_scale = 1.0 / math.sqrt(cell_count * devices)
    grad_kernel = (jnp.sum(shares.astype(jnp.float32), axis=0) * norm_scale).reshape(-1)

    grad_source = pl.pallas_call(
        source_kernel,
        out_shape=jax.ShapeDtypeStruct(slope.shape, jnp.bfloat16),
        in_specs=[vmem] * 6,
        out_specs=vmem,
        scratch_shapes=[
            columns,
            pltpu.VMEM((3, 9 * channels, channels), jnp.bfloat16),
            pltpu.VMEM((3, channels, width_y * depth), jnp.float32),
        ],
        compiler_params=PARAMS,
        cost_estimate=pl.CostEstimate(
            flops=5400 * channels * channels * cell_count, bytes_accessed=2 * 1024 * 1024, transcendentals=0
        ),
        name="source_grad",
    )(slope, x_near, x_far, far, near, kernel)
    return (grad_source.transpose(2, 0, 1, 3), grad_kernel)


def solution(mesh):
    placed = (P(None, "gx", "gy", None), P(None, "gx", "gy", None), P(None, "gx", "gy", None), P())
    return jax.shard_map(
        on_device,
        mesh=mesh,
        in_specs=placed,
        out_specs=(P(None, "gx", "gy", None), P(("gx", "gy"))),
        check_vma=False,
    )
```
